32 devices in a mesh: dp: 4 (over y, x), ctx: 8 (over z, core).
Axes of the slice: x: 2, y: 2, z: 4, core: 2. Of those that a mesh axis runs over, the one named last changes fastest.
Arguments:
- tokens: bfloat16 [16384, 2048], P(('dp', 'ctx')), may hold values from -6 to 6
- cotangent: bfloat16 [16384, 2048], P(('dp', 'ctx')), may hold values from -6 to 6
- wqkv: bfloat16 [2048, 6144], P('dp'), may hold values from -0.125 to 0.125
- wo: bfloat16 [2048, 2048], P('dp'), may hold values from -1 to 1
- attn_gain: bfloat16 [2048], P('dp'), may hold values from 0.25 to 1.75
- query_gain: bfloat16 [2048], P('dp'), may hold values from 0.25 to 1.75
- key_gain: bfloat16 [2048], P('dp'), may hold values from 0.25 to 1.75
- moe_gain: bfloat16 [2048], P('dp'), may hold values from 0.25 to 1.75
- w_gate: bfloat16 [16, 2048, 1024], P('ctx', 'dp'), may hold values from -0.125 to 0.125
- w_up: bfloat16 [16, 2048, 1024], P('ctx', 'dp'), may hold values from -0.125 to 0.125
- w_down: bfloat16 [16, 1024, 2048], P('ctx', 'dp'), may hold values from -0.375 to 0.375
- expert_ids: int32 [16384, 8], P(('dp', 'ctx')), may hold values from 0 to 15, all different within a row
- gates: float32 [16384, 8], P(('dp', 'ctx')), may hold values from 0.25 to 0.6
- slot_order: int32 [16384, 8], P(('dp', 'ctx')), may hold values from 0 to 4095, as said below
- block_assign: int32 [4, 16], P('dp'), may hold values from 0 to 15, each once within a row
- segment_ids: int32 [4, 2048], P('dp'), may hold values from 0 to 7, never falling along the last dimension, each value on 1 to 512 neighbouring positions
Outputs:
- output: bfloat16 [16384, 2048], P(('dp', 'ctx'))
- input_grad: bfloat16 [16384, 2048], P(('dp', 'ctx'))
- grad_wqkv: float32 [2048, 6144], P('dp')
- grad_wo: float32 [2048, 2048], P('dp')
- grad_attn_gain: float32 [2048], P('dp')
- grad_query_gain: float32 [2048], P('dp')
- grad_key_gain: float32 [2048], P('dp')
- grad_moe_gain: float32 [2048], P('dp')
- grad_w_gate: float32 [16, 2048, 1024], P('ctx', 'dp')
- grad_w_up: float32 [16, 2048, 1024], P('ctx', 'dp')
- grad_w_down: float32 [16, 1024, 2048], P('ctx', 'dp')
The draws below stay inside these ranges and needn't reach their ends.
Inputs may be any that keep to these rules, and one draw needn't show every extreme that they name: `slot_order`: within each aligned block of 512 rows, the 4096 entries are each of 0 to 4095 once. `block_assign`: each row is a permutation. `segment_ids`: never falling along a row; each continuation has 1 to 512 tokens. `expert_ids`: each row names 8 different experts.
All inputs are finite; a program needn't handle non-finite values.
Results may differ from the reference program's by a relative error of at most 0.023.
Values may be sent and summed in bfloat16 or wider, within the bound.
No kernel may reach another device: no remote copies, remote signals or barrier semaphores. Data moves between devices by JAX's collectives and lax.ppermute only.
A program may use at most 512 MiB of HBM per device.

```python
import math
from functools import partial
import jax
import jax.numpy as jnp
import numpy as np
from jax import lax

D = 2048
HEADS = 16
HDIM = 128
FF = 1024
TOP = 8
PROMPT = 2048
CONT = 8
EXPERTS = 16
CONT_TOK = 2048
MOST = 512
TOK_GROUP = 4096
TOK_DEV = 512
BLK = 256
NBLK = 16
CAP = 288
TOKENS = 16384
N_DP = 4


def draw_slot_order(key, part):
    key = jax.random.fold_in(key, 11)
    count_blocks = TOKENS // TOK_DEV
    subkeys = jax.random.split(key, count_blocks)

    def ordering(subkey):
        return jax.random.permutation(subkey, TOK_DEV * TOP)
    ranked = jax.vmap(ordering)(subkeys)
    return ranked.reshape(TOKENS, TOP).astype(jnp.int32)


def block_scale(stream_key, dims, cuts, low, high):
    loudness, own = 1.0, jax.random.fold_in(stream_key, 6)
    for axis_at, blocks in cuts:
        draws = jnp.exp(jax.random.uniform(jax.random.fold_in(own, axis_at), (blocks,), jnp.float32, low / len(cuts), high / len(cuts)))
        loudness = loudness * jnp.repeat(draws, dims[axis_at] // blocks).reshape([-1 if axis == axis_at else 1 for axis in range(len(dims))])
    return loudness


def distinct(rng, rows, amount, top, lift):
    order = jax.random.permutation(jax.random.fold_in(rng, 1), amount)
    favour = order
    for power in range(3):
        favour = favour * favour // amount
    favour = favour * lift // amount
    tickets = jax.random.randint(jax.random.fold_in(rng, 2), (rows, amount), 0, 4096) + favour
    holders = jax.random.permutation(jax.random.fold_in(rng, 3), rows)[jnp.arange(amount) % rows]
    tickets = jnp.where(jnp.arange(rows)[:, None] == holders[None, :], 1 << 14, tickets)
    merit = tickets * amount + jnp.arange(amount)
    return lax.top_k(merit.astype(jnp.int32), top)[1].astype(jnp.int32)


def length_profile(count, total, reach, skew):
    portions = [(1 << 20) // math.isqrt(standing ** skew) + 1 for standing in range(2, count + 1)]
    surplus, holding = total - reach - (count - 1), [1] * (count - 1)
    while surplus > 0:
        candidates = [i for i in range(count - 1) if holding[i] < reach]
        pool, remaining = sum([portions[i] for i in candidates]), surplus
        for i in candidates:
            more = min(reach - holding[i], max(1, remaining * portions[i] // pool), surplus)
            holding[i] = holding[i] + more
            surplus = surplus - more
    return np.array([reach] + holding)


def ragged(stream_key, count, total, most, skew):
    if count == 2:
        one = jax.random.randint(stream_key, (), max(1, total - most), min(most, total - 1) + 1)
        return jnp.stack([one, total - one])
    lengths = jnp.asarray(length_profile(count, total, most, skew), jnp.int32)
    pairs = (count - 1) // 2
    source_of, sink = lengths[1:1 + 2 * pairs:2], lengths[2:2 + 2 * pairs:2]
    margin = jnp.minimum(source_of - 1, most - sink)
    passed = jax.random.randint(jax.random.fold_in(stream_key, 1), (pairs,), 0, 1 << 20) % (margin + 1)
    lengths = lengths.at[1:1 + 2 * pairs:2].set(source_of - passed).at[2:2 + 2 * pairs:2].set(sink + passed)
    return lengths[jax.random.permutation(jax.random.fold_in(stream_key, 2), count)]


def normal_values(key, shape, scale, most, cuts=(), kind=jnp.bfloat16):
    loudness = block_scale(key, shape, cuts, -0.22, 0.18) if cuts else 1.0
    values = jax.random.normal(key, shape, jnp.float32) * scale * loudness
    return jnp.minimum(jnp.maximum(values, -most), most).astype(kind)


def setup_inputs(seed: int = 0) -> dict:
    seeds = jax.random.split(jax.random.key(seed), 17)
    tokens = normal_values(seeds[0], (TOKENS, D), 1.0, 6.0, ((0, 32),))
    cotangent = normal_values(seeds[1], (TOKENS, D), 1.0, 6.0, ((0, 32),))
    wqkv = normal_values(seeds[2], (D, 3 * D), D ** -0.5, 0.125, ((0, 4),))
    wo = normal_values(seeds[3], (D, D), ((D + 63) // 64) ** -0.5, 1.0, ((0, 4),))
    attn_gain = jnp.clip(1.0 + 0.15 * jax.random.normal(seeds[4], (D,), jnp.float32), 0.25, 1.75).astype(jnp.bfloat16)
    query_gain = jnp.clip(1.0 + 0.15 * jax.random.normal(seeds[5], (D,), jnp.float32), 0.25, 1.75).astype(jnp.bfloat16)
    key_gain = jnp.clip(1.0 + 0.15 * jax.random.normal(seeds[6], (D,), jnp.float32), 0.25, 1.75).astype(jnp.bfloat16)
    moe_gain = jnp.clip(1.0 + 0.15 * jax.random.normal(seeds[7], (D,), jnp.float32), 0.25, 1.75).astype(jnp.bfloat16)
    w_gate = normal_values(seeds[8], (EXPERTS, D, FF), D ** -0.5, 0.125, ((0, 8), (1, 4)))
    w_up = normal_values(seeds[9], (EXPERTS, D, FF), D ** -0.5, 0.125, ((0, 8), (1, 4)))
    w_down = normal_values(seeds[10], (EXPERTS, FF, D), (FF // 4) ** -0.5, 0.375, ((0, 8), (1, 4)))
    expert_ids = distinct(seeds[11], TOKENS, EXPERTS, TOP, 4096)
    gates = jnp.clip(jnp.exp(math.log(0.6) - 0.8754688 * jax.random.uniform(seeds[12], (TOKENS, TOP), jnp.float32) ** block_scale(seeds[12], (TOKENS, TOP), ((0, 32),), -0.2, 0.2)), 0.25, 0.6)
    slot_order = draw_slot_order(jax.random.fold_in(seeds[16], 71), 0)
    block_assign = jax.vmap(lambda own: jax.random.permutation(own, NBLK))(jax.random.split(seeds[14], N_DP)).reshape((N_DP, NBLK)).astype(jnp.int32)
    segment_ids = jax.vmap(lambda own: jnp.searchsorted(jnp.cumsum(ragged(own, CONT, CONT_TOK, MOST, 1)), jnp.arange(CONT_TOK), side="right"))(jax.random.split(seeds[15], N_DP)).reshape((N_DP, CONT_TOK)).astype(jnp.int32)
    return dict(tokens=tokens, cotangent=cotangent, wqkv=wqkv, wo=wo, attn_gain=attn_gain, query_gain=query_gain, key_gain=key_gain, moe_gain=moe_gain, w_gate=w_gate, w_up=w_up, w_down=w_down, expert_ids=expert_ids, gates=gates, slot_order=slot_order, block_assign=block_assign, segment_ids=segment_ids)


epsilon = 1e-06
masked_value = -1e+30
highest = lax.Precision.HIGHEST

@jax.custom_vjp
def low(v):
    return lax.optimization_barrier(v.astype(jnp.bfloat16)).astype(jnp.float32)

@jax.custom_vjp
def low_back(v):
    return v

def low_keep(v):
    return (low(v), None)

def low_pass(kept, grad):
    return (grad,)

def back_keep(v):
    return (v, None)

def back_low(kept, grad):
    return (low(grad),)
low.defvjp(low_keep, low_pass)
low_back.defvjp(back_keep, back_low)

def rms_normed(values_in):
    return values_in * lax.rsqrt(lax.optimization_barrier(jnp.mean(values_in * values_in, axis=-1, keepdims=True)) + epsilon)

def layout(assign_row, segment_row):
    offsets = jnp.arange(BLK, dtype=jnp.int32)
    logical = (assign_row[:, None].astype(jnp.int32) * BLK + offsets[None, :]).reshape(TOK_GROUP)
    segment_full = jnp.concatenate([jnp.full((PROMPT,), -1, jnp.int32), segment_row.astype(jnp.int32)]).reshape(NBLK, BLK)
    stored = jnp.take(segment_full, assign_row.astype(jnp.int32), axis=0).reshape(TOK_GROUP)
    return (logical, stored)

def visible(query_pos, query_seg, key_pos, key_seg):
    causal = key_pos[None, :] <= query_pos[:, None]
    same_doc = (key_seg[None, :] == query_seg[:, None]) & causal
    prompt_key = (key_seg[None, :] < 0) & (query_seg[:, None] >= 0)
    return same_doc | prompt_key

def attend_group(queries, keys, values, positions, segments):
    query_block = min(512, TOK_GROUP)
    count_blocks = TOK_GROUP // query_block
    scale = HDIM ** (-0.5)

    def one_block(pieces):
        query_blk, pos_blk, seg_blk = pieces
        allowed = visible(pos_blk, seg_blk, positions, segments)
        raw_scores = jnp.einsum('thd,khd->htk', query_blk, keys, precision=highest) * scale
        scores = jnp.where(allowed[None], low_back(raw_scores), masked_value)
        largest = lax.optimization_barrier(jnp.max(scores, axis=-1, keepdims=True))
        exponent = jnp.exp(scores - largest)
        probs = exponent / lax.optimization_barrier(jnp.sum(exponent, axis=-1, keepdims=True))
        return jnp.einsum('htk,khd->thd', low(probs), values, precision=highest)
    outcome = lax.map(jax.checkpoint(one_block), (queries.reshape(count_blocks, query_block, HEADS, HDIM), positions.reshape(count_blocks, query_block), segments.reshape(count_blocks, query_block)))
    return outcome.reshape(TOK_GROUP, HEADS * HDIM)

def slot_positions(expert_rows, order_rows, count_experts, capacity):
    pair_count = expert_rows.shape[0] * expert_rows.shape[1]
    flat_expert = expert_rows.reshape(pair_count).astype(jnp.int32)
    flat_order = order_rows.reshape(pair_count).astype(jnp.int32)
    by_order = jnp.zeros((pair_count,), jnp.int32).at[flat_order].set(flat_expert)
    matched = (by_order[:, None] == jnp.arange(count_experts, dtype=jnp.int32)[None, :]).astype(jnp.int32)
    earlier = jnp.cumsum(matched, axis=0) - matched
    slot_sorted = lax.optimization_barrier(jnp.sum(earlier * matched, axis=1))
    slot_pair = jnp.take(slot_sorted, flat_order)
    position = jnp.where(slot_pair < capacity, flat_expert * capacity + slot_pair, -1)
    return position.reshape(expert_rows.shape).astype(jnp.int32)

def expert_block(weights, pieces):
    gate_weight, up_weight, down_weight = weights
    normed_blk, ids_blk, gates_blk, order_blk = pieces
    slots = EXPERTS * CAP
    position = slot_positions(ids_blk, order_blk, EXPERTS, CAP)
    target = jnp.where(position >= 0, position, slots).reshape(TOK_DEV * TOP).astype(jnp.int32)
    owners = jnp.repeat(jnp.arange(TOK_DEV, dtype=jnp.int32), TOP)
    table = jnp.full((slots + 1,), TOK_DEV, jnp.int32).at[target].set(owners)[:slots]
    padded = jnp.concatenate([normed_blk, jnp.zeros((1, D), normed_blk.dtype)], axis=0)
    sent = low_back(jnp.take(padded, table, axis=0)).reshape(EXPERTS, CAP, D)
    gate_pre = low_back(jnp.einsum('ecd,edf->ecf', sent, gate_weight, precision=highest))
    up_pre = low_back(jnp.einsum('ecd,edf->ecf', sent, up_weight, precision=highest))
    hidden = low(jax.nn.silu(gate_pre) * up_pre)
    returned = low(low_back(jnp.einsum('ecf,efd->ecd', hidden, down_weight, precision=highest))).reshape(slots, D)
    padded_out = jnp.concatenate([returned, jnp.zeros((1, D), returned.dtype)], axis=0)
    picked = jnp.take(padded_out, target, axis=0).reshape(TOK_DEV, TOP, D)
    return lax.optimization_barrier(jnp.sum(picked * gates_blk[..., None], axis=1))

def layer(inputs, wqkv, wo, attn_gain, query_gain, key_gain, moe_gain, w_gate, w_up, w_down, positions, segments, expert_ids, gates, slot_order):
    normed = low(rms_normed(inputs) * attn_gain)
    qkv = low_back(jnp.dot(normed, wqkv, precision=highest))
    queries = low(rms_normed(qkv[:, :D]) * query_gain)
    keys = low(rms_normed(qkv[:, D:2 * D]) * key_gain)
    values = low(qkv[:, 2 * D:])
    pieces = []
    for group_index in range(N_DP):
        first = group_index * TOK_GROUP
        last = first + TOK_GROUP
        pieces.append(attend_group(queries[first:last].reshape(TOK_GROUP, HEADS, HDIM), keys[first:last].reshape(TOK_GROUP, HEADS, HDIM), values[first:last].reshape(TOK_GROUP, HEADS, HDIM), positions[group_index], segments[group_index]))
    attended = low(low_back(jnp.concatenate(pieces, axis=0)))
    state = inputs + low_back(jnp.dot(attended, wo, precision=highest))
    normed_moe = low(rms_normed(state) * moe_gain)
    count_blocks = TOKENS // TOK_DEV
    mixed = lax.map(jax.checkpoint(partial(expert_block, (w_gate, w_up, w_down))), (normed_moe.reshape(count_blocks, TOK_DEV, D), expert_ids.reshape(count_blocks, TOK_DEV, TOP), gates.reshape(count_blocks, TOK_DEV, TOP), slot_order.reshape(count_blocks, TOK_DEV, TOP)))
    return state + mixed.reshape(TOKENS, D)

def reference(tokens, cotangent, wqkv, wo, attn_gain, query_gain, key_gain, moe_gain, w_gate, w_up, w_down, expert_ids, gates, slot_order, block_assign, segment_ids):
    layouts = [layout(block_assign[group_index], segment_ids[group_index]) for group_index in range(N_DP)]
    positions = jnp.stack([entry[0] for entry in layouts])
    segments = jnp.stack([entry[1] for entry in layouts])
    params = tuple((array.astype(jnp.float32) for array in (tokens, wqkv, wo, attn_gain, query_gain, key_gain, moe_gain, w_gate, w_up, w_down)))
    gates_f = gates.astype(jnp.float32)

    def forward(inputs, wqkv_f, wo_f, attn_f, query_f, key_f, moe_f, gate_f, up_f, down_f):
        return layer(inputs, wqkv_f, wo_f, attn_f, query_f, key_f, moe_f, gate_f, up_f, down_f, positions, segments, expert_ids, gates_f, slot_order)
    outputs, pullback = jax.vjp(forward, *params)
    grads = pullback(cotangent.astype(jnp.float32))
    return (outputs.astype(jnp.bfloat16), grads[0].astype(jnp.bfloat16), grads[1], grads[2], grads[3], grads[4], grads[5], grads[6], grads[7], grads[8], grads[9])
```

```python
import functools

import jax
import jax.numpy as jnp
from jax import lax
from jax.experimental import pallas as pl
from jax.experimental.pallas import tpu as pltpu
from jax.sharding import PartitionSpec as P

HEADS = 16
TOP = 8
BLK_DEV = 2
LOG2E = 1.4426950408889634

epsilon = 1e-06
masked_value = -1e30
f32 = jnp.float32
bf16 = jnp.bfloat16
NT = (((1,), (1,)), ((), ()))
TN = (((0,), (0,)), ((), ()))


def rms_scale(values_in):
    return lax.rsqrt(jnp.mean(values_in * values_in, axis=-1, keepdims=True) + epsilon)


def rms_back(grad_hat, normed, scale_rows):
    return scale_rows * (grad_hat - normed * jnp.mean(grad_hat * normed, axis=-1, keepdims=True))


def tile_mask(seg_col, seg_row, key_first, query_first):
    rows, columns = seg_col.shape[0], seg_row.shape[1]
    key_pos = key_first + lax.broadcasted_iota(jnp.int32, (rows, columns), 0)
    query_pos = query_first + lax.broadcasted_iota(jnp.int32, (rows, columns), 1)
    return (seg_col == seg_row) & (key_pos <= query_pos)


def forward_kernel(
    tile,
    prompt_tiles,
    block_len,
    scale,
    place,
    first_tile,
    raw_q,
    raw_k,
    raw_v,
    inv,
    gain_q,
    gain_k,
    seg_col,
    seg_row,
    out,
    lse,
    queries,
    keys,
    values,
    values_t,
    out_logical,
):
    group, width = raw_q.shape
    tiles = group // tile
    blocks = group // block_len

    def bring(block, carry):
        source = pl.ds(pl.multiple_of(place[block] * block_len, block_len), block_len)
        target = pl.ds(pl.multiple_of(block * block_len, block_len), block_len)
        scales = inv[source, :]
        queries[target, :] = (raw_q[source, :] * scales[:, 0:1] * gain_q[...]).astype(bf16)
        keys[target, :] = (raw_k[source, :] * scales[:, 1:2] * gain_k[...]).astype(bf16)
        values[target, :] = raw_v[source, :].astype(bf16)
        return carry

    lax.fori_loop(0, blocks, bring, 0)
    for index in range(tiles):
        values_t[:, index * tile : (index + 1) * tile] = values[
            index * tile : (index + 1) * tile, :
        ].T

    def query_tile(index, carry):
        first = pl.multiple_of(index * tile, tile)
        query = queries[pl.ds(first, tile), :]
        seg_query = seg_row[pl.ds(index, 1), :]

        def step(is_masked, at, state):
            largest, total, running = state
            key_first = pl.multiple_of(at * tile, tile)
            scores = lax.dot_general(
                keys[pl.ds(key_first, tile), :], query, NT, preferred_element_type=f32
            ) * (scale * LOG2E)
            if is_masked:
                allowed = tile_mask(seg_col[pl.ds(key_first, tile), :], seg_query, key_first, first)
                scores = jnp.where(allowed, scores, masked_value)
            new_largest = jnp.maximum(largest, jnp.max(scores, axis=0, keepdims=True))
            shrink = jnp.exp2(largest - new_largest)
            terms = jnp.exp2(scores - new_largest)
            total = total * shrink + jnp.sum(terms, axis=0, keepdims=True)
            running = running * shrink + jnp.dot(
                values_t[:, pl.ds(key_first, tile)], terms.astype(bf16), preferred_element_type=f32
            )
            return (new_largest, total, running)

        state = (
            jnp.full((1, tile), masked_value, f32),
            jnp.zeros((1, tile), f32),
            jnp.zeros((width, tile), f32),
        )
        state = lax.fori_loop(
            0, jnp.minimum(index, prompt_tiles), functools.partial(step, False), state
        )
        state = lax.fori_loop(first_tile[index], index + 1, functools.partial(step, True), state)
        largest, total, running = state
        lse[pl.ds(index, 1), :] = largest + jnp.log2(total)
        out_logical[pl.ds(first, tile), :] = (running / total).T
        return carry

    lax.fori_loop(0, tiles, query_tile, 0)

    def send(block, carry):
        target = pl.ds(pl.multiple_of(place[block] * block_len, block_len), block_len)
        source = pl.ds(pl.multiple_of(block * block_len, block_len), block_len)
        out[target, :] = out_logical[source, :].astype(bf16)
        return carry

    lax.fori_loop(0, blocks, send, 0)


def backward_kernel(
    tile,
    prompt_tiles,
    block_len,
    scale,
    place,
    first_tile,
    queries,
    keys,
    values,
    lse,
    out,
    grad_out,
    seg_col,
    seg_row,
    grad_q,
    grad_k,
    grad_v,
    keys_t,
    grad_here,
    delta,
    total_q,
    total_k,
    total_v,
):
    group, width = queries.shape
    tiles = group // tile
    blocks = group // block_len

    def bring(block, carry):
        source = pl.ds(pl.multiple_of(place[block] * block_len, block_len), block_len)
        target = pl.ds(pl.multiple_of(block * block_len, block_len), block_len)
        grad_here[target, :] = grad_out[source, :]
        total_q[target, :] = out[source, :].astype(f32) * grad_out[source, :].astype(f32)
        return carry

    lax.fori_loop(0, blocks, bring, 0)
    for index in range(tiles):
        rows = slice(index * tile, (index + 1) * tile)
        keys_t[:, rows] = keys[rows, :].T
        delta[index : index + 1, :] = jnp.sum(total_q[rows, :].T, axis=0, keepdims=True)
    total_k[...] = jnp.zeros_like(total_k)
    total_v[...] = jnp.zeros_like(total_v)

    def query_tile(index, carry):
        first = pl.multiple_of(index * tile, tile)
        query = queries[pl.ds(first, tile), :]
        grad_tile = grad_here[pl.ds(first, tile), :]
        seg_query = seg_row[pl.ds(index, 1), :]
        lse_tile = lse[pl.ds(index, 1), :]
        delta_tile = delta[pl.ds(index, 1), :]

        def step(is_masked, at, running):
            key_first = pl.multiple_of(at * tile, tile)
            here = pl.ds(key_first, tile)
            scores = lax.dot_general(keys[here, :], query, NT, preferred_element_type=f32) * (
                scale * LOG2E
            )
            probs = jnp.exp2(scores - lse_tile)
            if is_masked:
                allowed = tile_mask(seg_col[here, :], seg_query, key_first, first)
                probs = jnp.where(allowed, probs, 0.0)
            dprobs = lax.dot_general(values[here, :], grad_tile, NT, preferred_element_type=f32)
            dscores = (probs * (dprobs - delta_tile)).astype(bf16)
            total_v[here, :] += jnp.dot(probs.astype(bf16), grad_tile, preferred_element_type=f32)
            total_k[here, :] += jnp.dot(dscores, query, preferred_element_type=f32)
            return running + jnp.dot(keys_t[:, here], dscores, preferred_element_type=f32)

        running = jnp.zeros((width, tile), f32)
        running = lax.fori_loop(
            0, jnp.minimum(index, prompt_tiles), functools.partial(step, False), running
        )
        running = lax.fori_loop(
            first_tile[index], index + 1, functools.partial(step, True), running
        )
        total_q[pl.ds(first, tile), :] = running.T
        return carry

    lax.fori_loop(0, tiles, query_tile, 0)

    def send(block, carry):
        target = pl.ds(pl.multiple_of(place[block] * block_len, block_len), block_len)
        source = pl.ds(pl.multiple_of(block * block_len, block_len), block_len)
        grad_q[target, :] = total_q[source, :] * scale
        grad_k[target, :] = total_k[source, :] * scale
        grad_v[target, :] = total_v[source, :].astype(bf16)
        return carry

    lax.fori_loop(0, blocks, send, 0)


def attention_forward(
    raw, inv, gain_q, gain_k, seg_col, seg_row, place, first_tile, tile, block_len, scale
):
    group, width = raw.shape[0], raw.shape[1] // 3
    head_dim = 128
    heads = width // head_dim
    tiles = group // tile
    prompt_tiles = tiles // 2

    def part(which):
        return pl.BlockSpec((group, head_dim), lambda h, *_: (0, which * heads + h))

    def whole(shape):
        return pl.BlockSpec(shape, lambda h, *_: (0,) * len(shape))

    head = pl.BlockSpec((group, head_dim), lambda h, *_: (0, h))
    return pl.pallas_call(
        functools.partial(forward_kernel, tile, prompt_tiles, block_len, scale),
        grid_spec=pltpu.PrefetchScalarGridSpec(
            num_scalar_prefetch=2,
            grid=(heads,),
            in_specs=[
                part(0),
                part(1),
                part(2),
                whole((group, 2)),
                pl.BlockSpec((1, head_dim), lambda h, *_: (0, h)),
                pl.BlockSpec((1, head_dim), lambda h, *_: (0, h)),
                whole((group, 1)),
                whole((tiles, tile)),
            ],
            out_specs=[
                head,
                pl.BlockSpec((None, tiles, tile), lambda h, *_: (h, 0, 0)),
                head,
                head,
                head,
            ],
            scratch_shapes=[
                pltpu.VMEM((head_dim, group), bf16),
                pltpu.VMEM((group, head_dim), f32),
            ],
        ),
        out_shape=[
            jax.ShapeDtypeStruct((group, width), bf16),
            jax.ShapeDtypeStruct((heads, tiles, tile), f32),
            jax.ShapeDtypeStruct((group, width), bf16),
            jax.ShapeDtypeStruct((group, width), bf16),
            jax.ShapeDtypeStruct((group, width), bf16),
        ],
        compiler_params=pltpu.CompilerParams(vmem_limit_bytes=56 * 2**20),
        cost_estimate=pl.CostEstimate(
            flops=2 * heads * group * group * head_dim * 2,
            bytes_accessed=32 * group * width,
            transcendentals=0,
        ),
        name="attention_forward",
    )(place, first_tile, raw, raw, raw, inv, gain_q, gain_k, seg_col, seg_row)


def attention_backward(
    queries, keys, values, lse, out, grad_out, seg_col, seg_row, place, first_tile, tile, block_len, scale
):
    group, width = queries.shape
    head_dim = 128
    heads = width // head_dim
    tiles = group // tile
    prompt_tiles = tiles // 2

    def whole(shape):
        return pl.BlockSpec(shape, lambda h, *_: (0,) * len(shape))

    head = pl.BlockSpec((group, head_dim), lambda h, *_: (0, h))
    return pl.pallas_call(
        functools.partial(backward_kernel, tile, prompt_tiles, block_len, scale),
        grid_spec=pltpu.PrefetchScalarGridSpec(
            num_scalar_prefetch=2,
            grid=(heads,),
            in_specs=[
                head,
                head,
                head,
                pl.BlockSpec((None, tiles, tile), lambda h, *_: (h, 0, 0)),
                head,
                head,
                whole((group, 1)),
                whole((tiles, tile)),
            ],
            out_specs=[head, head, head],
            scratch_shapes=[
                pltpu.VMEM((head_dim, group), bf16),
                pltpu.VMEM((group, head_dim), bf16),
                pltpu.VMEM((tiles, tile), f32),
                pltpu.VMEM((group, head_dim), f32),
                pltpu.VMEM((group, head_dim), f32),
                pltpu.VMEM((group, head_dim), f32),
            ],
        ),
        out_shape=[
            jax.ShapeDtypeStruct((group, width), f32),
            jax.ShapeDtypeStruct((group, width), f32),
            jax.ShapeDtypeStruct((group, width), bf16),
        ],
        compiler_params=pltpu.CompilerParams(vmem_limit_bytes=56 * 2**20),
        cost_estimate=pl.CostEstimate(
            flops=5 * heads * group * group * head_dim,
            bytes_accessed=32 * group * width,
            transcendentals=0,
        ),
        name="attention_backward",
    )(place, first_tile, queries, keys, values, lse, out, grad_out, seg_col, seg_row)


def slot_table(expert_rows, order_rows, gate_rows, count_experts, capacity):
    chosen = expert_rows.T[None, :, :] == jnp.arange(count_experts, dtype=jnp.int32)[:, None, None]
    holds = jnp.any(chosen, axis=1)
    order = jnp.sum(jnp.where(chosen, order_rows.T[None], 0), axis=1)
    gate = jnp.sum(jnp.where(chosen, gate_rows.T[None], 0.0), axis=1)
    earlier = holds[:, None, :] & (order[:, None, :] < order[:, :, None])
    slot = jnp.sum(earlier.astype(jnp.int32), axis=2)
    return (jnp.where(holds & (slot < capacity), slot, -1), gate)


def on_device(
    tokens,
    cotangent,
    wqkv,
    wo,
    attn_gain,
    query_gain,
    key_gain,
    moe_gain,
    w_gate,
    w_up,
    w_down,
    expert_ids,
    gates,
    slot_order,
    block_assign,
    segment_ids,
):
    count_rows, width = tokens.shape
    head_dim = width // HEADS
    scale = head_dim ** (-0.5)
    peers = lax.axis_size("ctx")
    groups = lax.axis_size("dp")
    me = lax.axis_index("ctx")
    my_dp = lax.axis_index("dp")
    group_rows = count_rows * peers
    rep = max(1, peers // HEADS)
    own_heads = max(1, HEADS // peers)
    own_width = own_heads * head_dim
    first_head = (me // rep) * own_heads
    block_len = count_rows // BLK_DEV
    tile = 512

    gain_all = lax.all_gather(
        jnp.stack([attn_gain, query_gain, key_gain, moe_gain]), "dp", axis=1, tiled=True
    ).astype(f32)
    gain_attn, gain_moe = gain_all[0:1], gain_all[3:4]
    gain_own = lax.dynamic_slice_in_dim(gain_all, first_head * head_dim, own_width, 1)
    gain_q, gain_k = gain_own[1:2], gain_own[2:3]

    assign = block_assign[0]
    count_blocks = assign.shape[0]
    place = jnp.argmax(
        assign[None, :] == jnp.arange(count_blocks, dtype=jnp.int32)[:, None], axis=1
    ).astype(jnp.int32)
    cont = segment_ids[0]
    prompt_len = group_rows - cont.shape[0]
    seg_logical = jnp.concatenate([jnp.full((prompt_len,), -1, jnp.int32), cont])
    tiles = group_rows // tile
    tile_seg = seg_logical.reshape(tiles, tile)[:, 0]
    first_tile = jnp.where(
        tile_seg < 0,
        jnp.arange(tiles, dtype=jnp.int32),
        jnp.sum((seg_logical[None, :] < tile_seg[:, None]).astype(jnp.int32), axis=1) // tile,
    ).astype(jnp.int32)
    seg_col = seg_logical[:, None]
    seg_row = seg_logical.reshape(tiles, tile)

    inputs = tokens.astype(f32)
    inv_in = rms_scale(inputs)
    hat_in = inputs * inv_in
    normed = (hat_in * gain_attn).astype(bf16)
    normed_all = lax.all_gather(normed, "ctx", axis=0, tiled=True)
    w_own = lax.dynamic_slice_in_dim(
        wqkv.reshape(wqkv.shape[0], 3, HEADS, head_dim), first_head, own_heads, 2
    ).reshape(wqkv.shape[0], 3 * own_width)
    w_own = lax.all_gather(w_own, "dp", axis=0, tiled=True)
    raw = jnp.dot(normed_all, w_own, preferred_element_type=f32)
    square = raw[:, : 2 * own_width].reshape(group_rows, 2, own_width)
    square = lax.psum(jnp.sum(square * square, axis=2).T, "ctx") * (1.0 / rep)
    inv_qk = lax.rsqrt(square / width + epsilon).T
    attended, lse, queries, keys, values = attention_forward(
        raw, inv_qk, gain_q, gain_k, seg_col, seg_row, place, first_tile, tile, block_len, scale
    )
    attn_low = lax.all_to_all(
        attended.reshape(peers, count_rows, own_width), "ctx", split_axis=0, concat_axis=0, tiled=True
    )[::rep]
    attn_low = attn_low.transpose(1, 0, 2).reshape(count_rows, width)
    full_wo = lax.all_gather(wo, "dp", axis=0, tiled=True)
    state = inputs + jnp.dot(attn_low, full_wo, preferred_element_type=f32)
    inv_state = rms_scale(state)
    hat_state = state * inv_state
    normed_moe = (hat_state * gain_moe).astype(bf16)

    local_experts = w_gate.shape[0]
    count_experts = local_experts * peers
    capacity = 9 * count_rows * TOP // (8 * count_experts)
    slot, gate = slot_table(expert_ids, slot_order, gates, count_experts, capacity)
    slot = lax.all_to_all(
        slot.reshape(peers, local_experts, count_rows), "ctx", split_axis=0, concat_axis=0, tiled=True
    )
    gate = lax.all_to_all(
        gate.reshape(peers, local_experts, count_rows), "ctx", split_axis=0, concat_axis=0, tiled=True
    )
    picks = slot[:, :, None, :] == jnp.arange(capacity, dtype=jnp.int32)[:, None]
    slot_gate = jnp.sum(jnp.where(picks, gate[:, :, None, :], 0.0), axis=3)[..., None]
    picks = picks.astype(bf16)

    full_gate = lax.all_gather(w_gate, "dp", axis=1, tiled=True)
    full_up = lax.all_gather(w_up, "dp", axis=1, tiled=True)
    full_down = lax.all_gather(w_down, "dp", axis=1, tiled=True)

    cot_all = lax.all_gather(cotangent, "ctx", axis=0, tiled=True).reshape(peers, count_rows, width)
    grad_rows = (
        jnp.einsum("sncr,srd->sncd", picks, cot_all, preferred_element_type=f32) * slot_gate
    ).astype(bf16)
    grad_hidden = jnp.einsum("sncd,nfd->sncf", grad_rows, full_down, preferred_element_type=f32)

    moe_all = lax.all_gather(normed_moe, "ctx", axis=0, tiled=True).reshape(
        peers, count_rows, width
    )
    expert_in = jnp.einsum("sncr,srd->sncd", picks, moe_all, preferred_element_type=f32).astype(
        bf16
    )
    gate_pre = jnp.einsum("sncd,ndf->sncf", expert_in, full_gate, preferred_element_type=f32)
    up_pre = jnp.einsum("sncd,ndf->sncf", expert_in, full_up, preferred_element_type=f32)
    sigmoid = jax.nn.sigmoid(gate_pre)
    silu = gate_pre * sigmoid
    hidden = (silu * up_pre).astype(bf16)
    grad_gate_pre = (
        grad_hidden * up_pre * sigmoid * (1.0 + gate_pre * (1.0 - sigmoid))
    ).astype(bf16)
    grad_up_pre = (grad_hidden * silu).astype(bf16)
    grad_in = (
        jnp.einsum("sncf,ndf->sncd", grad_gate_pre, full_gate, preferred_element_type=f32)
        + jnp.einsum("sncf,ndf->sncd", grad_up_pre, full_up, preferred_element_type=f32)
    ).astype(bf16)
    part_moe = jnp.einsum("sncr,sncd->srd", picks, grad_in, preferred_element_type=f32).astype(bf16)
    grad_normed_moe = lax.psum_scatter(
        part_moe.reshape(group_rows, width), "ctx", scatter_dimension=0, tiled=True
    ).astype(f32)

    out_rows = (
        jnp.einsum("sncf,nfd->sncd", hidden, full_down, preferred_element_type=f32) * slot_gate
    ).astype(bf16)
    part_mixed = jnp.einsum("sncr,sncd->srd", picks, out_rows, preferred_element_type=f32).astype(
        bf16
    )
    mixed = lax.psum_scatter(
        part_mixed.reshape(group_rows, width), "ctx", scatter_dimension=0, tiled=True
    ).astype(f32)
    output = (state + mixed).astype(bf16)

    grad_down = jnp.einsum("sncf,sncd->nfd", hidden, grad_rows, preferred_element_type=f32)
    grad_gate = jnp.einsum("sncd,sncf->ndf", expert_in, grad_gate_pre, preferred_element_type=f32)
    grad_up = jnp.einsum("sncd,sncf->ndf", expert_in, grad_up_pre, preferred_element_type=f32)

    def expert_sum(term):
        return lax.psum_scatter(term.astype(bf16), "dp", scatter_dimension=1, tiled=True).astype(f32)

    moe_gain_term = jnp.sum(grad_normed_moe * hat_state, axis=0)
    grad_state = cotangent.astype(f32) + rms_back(grad_normed_moe * gain_moe, hat_state, inv_state)
    grad_branch = grad_state.astype(bf16)
    grad_attn = lax.dot_general(grad_branch, full_wo, NT, preferred_element_type=f32).astype(bf16)
    grad_attn = grad_attn.reshape(count_rows, peers // rep, own_width).transpose(1, 0, 2)
    grad_attn = jnp.repeat(grad_attn, rep, axis=0)
    grad_attended = lax.all_to_all(
        grad_attn, "ctx", split_axis=0, concat_axis=0, tiled=True
    ).reshape(group_rows, own_width)
    grad_q, grad_k, grad_v = attention_backward(
        queries,
        keys,
        values,
        lse,
        attended,
        grad_attended,
        seg_col,
        seg_row,
        place,
        first_tile,
        tile,
        block_len,
        scale,
    )
    hat_q = raw[:, :own_width] * inv_qk[:, 0:1]
    hat_k = raw[:, own_width : 2 * own_width] * inv_qk[:, 1:2]
    query_gain_term = jnp.sum(grad_q * hat_q, axis=0)
    key_gain_term = jnp.sum(grad_k * hat_k, axis=0)
    means = jnp.stack(
        [
            jnp.sum(grad_q * gain_q * hat_q, axis=1),
            jnp.sum(grad_k * gain_k * hat_k, axis=1),
        ]
    )
    means = (lax.psum(means, "ctx") * (1.0 / (rep * width))).T
    grad_raw_q = inv_qk[:, 0:1] * (grad_q * gain_q - hat_q * means[:, 0:1])
    grad_raw_k = inv_qk[:, 1:2] * (grad_k * gain_k - hat_k * means[:, 1:2])
    grad_qkv = jnp.concatenate([grad_raw_q.astype(bf16), grad_raw_k.astype(bf16), grad_v], axis=1)
    part_normed = lax.dot_general(grad_qkv, w_own, NT, preferred_element_type=f32) * (1.0 / rep)
    grad_normed = lax.psum_scatter(
        part_normed.astype(bf16), "ctx", scatter_dimension=0, tiled=True
    ).astype(f32)
    attn_gain_term = jnp.sum(grad_normed * hat_in, axis=0)
    input_grad = (grad_state + rms_back(grad_normed * gain_attn, hat_in, inv_in)).astype(bf16)

    part_qkv = lax.dot_general(normed_all, grad_qkv, TN, preferred_element_type=f32).astype(bf16)
    part_qkv = lax.psum_scatter(part_qkv, "dp", scatter_dimension=0, tiled=True)
    qkv_total = lax.all_gather(part_qkv, "ctx", axis=0, tiled=False)[::rep]
    rows_dp = part_qkv.shape[0]
    qkv_total = (
        qkv_total.reshape(peers // rep, rows_dp, 3, own_width)
        .transpose(1, 2, 0, 3)
        .reshape(rows_dp, 3 * width)
        .astype(f32)
    )
    part_out = lax.dot_general(attn_low, grad_branch, TN, preferred_element_type=f32).astype(bf16)
    out_total = lax.psum(
        lax.psum_scatter(part_out, "dp", scatter_dimension=0, tiled=True), "ctx"
    ).astype(f32)

    own_terms = jnp.stack([query_gain_term, key_gain_term]) * (1.0 / rep)
    spread = lax.dynamic_update_slice_in_dim(
        jnp.zeros((2, width), f32), own_terms, first_head * head_dim, 1
    )
    gain_terms = jnp.concatenate([attn_gain_term[None], spread, moe_gain_term[None]], axis=0)
    gain_terms = lax.psum(gain_terms, ("dp", "ctx"))
    gain_terms = lax.dynamic_slice_in_dim(
        gain_terms, my_dp * (width // groups), width // groups, 1
    )
    return (
        output,
        input_grad,
        qkv_total,
        out_total,
        gain_terms[0],
        gain_terms[1],
        gain_terms[2],
        gain_terms[3],
        expert_sum(grad_gate),
        expert_sum(grad_up),
        expert_sum(grad_down),
    )


def solution(mesh):
    rows = P(("dp", "ctx"), None)
    expert = P("ctx", "dp", None)
    by_dp = P("dp", None)
    return jax.shard_map(
        on_device,
        mesh=mesh,
        in_specs=(
            rows,
            rows,
            by_dp,
            by_dp,
            P("dp"),
            P("dp"),
            P("dp"),
            P("dp"),
            expert,
            expert,
            expert,
            rows,
            rows,
            rows,
            by_dp,
            by_dp,
        ),
        out_specs=(
            rows,
            rows,
            by_dp,
            by_dp,
            P("dp"),
            P("dp"),
            P("dp"),
            P("dp"),
            expert,
            expert,
            expert,
        ),
        check_vma=False,
    )
```

```python
import functools

import jax
import jax.numpy as jnp
from jax import lax
from jax.experimental import pallas as pl
from jax.experimental.pallas import tpu as pltpu
from jax.sharding import PartitionSpec as P

HEADS = 16
TOP = 8
BLK_DEV = 2
LOG2E = 1.4426950408889634

epsilon = 1e-06
masked_value = -1e30
f32 = jnp.float32
bf16 = jnp.bfloat16
NT = (((1,), (1,)), ((), ()))
TN = (((0,), (0,)), ((), ()))


def rms_scale(values_in):
    return lax.rsqrt(jnp.mean(values_in * values_in, axis=-1, keepdims=True) + epsilon)


def rms_back(grad_hat, normed, scale_rows):
    return scale_rows * (grad_hat - normed * jnp.mean(grad_hat * normed, axis=-1, keepdims=True))


def tile_mask(seg_col, seg_row, key_first, query_first):
    rows, columns = seg_col.shape[0], seg_row.shape[1]
    key_pos = key_first + lax.broadcasted_iota(jnp.int32, (rows, columns), 0)
    query_pos = query_first + lax.broadcasted_iota(jnp.int32, (rows, columns), 1)
    return (seg_col == seg_row) & (key_pos <= query_pos)


def forward_kernel(
    tile,
    prompt_tiles,
    block_len,
    scale,
    place,
    first_tile,
    raw_q,
    raw_k,
    raw_v,
    inv,
    gain_q,
    gain_k,
    seg_col,
    seg_row,
    out,
    lse,
    queries,
    keys,
    values,
    values_t,
    out_logical,
):
    group, width = raw_q.shape
    tiles = group // tile
    blocks = group // block_len

    def bring(block, carry):
        source = pl.ds(pl.multiple_of(place[block] * block_len, block_len), block_len)
        target = pl.ds(pl.multiple_of(block * block_len, block_len), block_len)
        scales = inv[source, :]
        queries[target, :] = (raw_q[source, :] * scales[:, 0:1] * gain_q[...]).astype(bf16)
        keys[target, :] = (raw_k[source, :] * scales[:, 1:2] * gain_k[...]).astype(bf16)
        values[target, :] = raw_v[source, :].astype(bf16)
        return carry

    lax.fori_loop(0, blocks, bring, 0)
    for index in range(tiles):
        values_t[:, index * tile : (index + 1) * tile] = values[
            index * tile : (index + 1) * tile, :
        ].T

    def query_tile(index, carry):
        first = pl.multiple_of(index * tile, tile)
        query = queries[pl.ds(first, tile), :]
        seg_query = seg_row[pl.ds(index, 1), :]

        def step(is_masked, at, state):
            largest, total, running = state
            key_first = pl.multiple_of(at * tile, tile)
            scores = lax.dot_general(
                keys[pl.ds(key_first, tile), :], query, NT, preferred_element_type=f32
            ) * (scale * LOG2E)
            if is_masked:
                allowed = tile_mask(seg_col[pl.ds(key_first, tile), :], seg_query, key_first, first)
                scores = jnp.where(allowed, scores, masked_value)
            new_largest = jnp.maximum(largest, jnp.max(scores, axis=0, keepdims=True))
            shrink = jnp.exp2(largest - new_largest)
            terms = jnp.exp2(scores - new_largest)
            total = total * shrink + jnp.sum(terms, axis=0, keepdims=True)
            running = running * shrink + jnp.dot(
                values_t[:, pl.ds(key_first, tile)], terms.astype(bf16), preferred_element_type=f32
            )
            return (new_largest, total, running)

        state = (
            jnp.full((1, tile), masked_value, f32),
            jnp.zeros((1, tile), f32),
            jnp.zeros((width, tile), f32),
        )
        state = lax.fori_loop(
            0, jnp.minimum(index, prompt_tiles), functools.partial(step, False), state
        )
        state = lax.fori_loop(first_tile[index], index + 1, functools.partial(step, True), state)
        largest, total, running = state
        lse[pl.ds(index, 1), :] = largest + jnp.log2(total)
        out_logical[pl.ds(first, tile), :] = (running / total).T
        return carry

    lax.fori_loop(0, tiles, query_tile, 0)

    def send(block, carry):
        target = pl.ds(pl.multiple_of(place[block] * block_len, block_len), block_len)
        source = pl.ds(pl.multiple_of(block * block_len, block_len), block_len)
        out[target, :] = out_logical[source, :].astype(bf16)
        return carry

    lax.fori_loop(0, blocks, send, 0)


def backward_kernel(
    tile,
    prompt_tiles,
    block_len,
    scale,
    place,
    first_tile,
    queries,
    keys,
    values,
    lse,
    out,
    grad_out,
    seg_col,
    seg_row,
    grad_q,
    grad_k,
    grad_v,
    keys_t,
    grad_here,
    delta,
    total_q,
    total_k,
    total_v,
):
    group, width = queries.shape
    tiles = group // tile
    blocks = group // block_len

    def bring(block, carry):
        source = pl.ds(pl.multiple_of(place[block] * block_len, block_len), block_len)
        target = pl.ds(pl.multiple_of(block * block_len, block_len), block_len)
        grad_here[target, :] = grad_out[source, :]
        total_q[target, :] = out[source, :].astype(f32) * grad_out[source, :].astype(f32)
        return carry

    lax.fori_loop(0, blocks, bring, 0)
    for index in range(tiles):
        rows = slice(index * tile, (index + 1) * tile)
        keys_t[:, rows] = keys[rows, :].T
        delta[index : index + 1, :] = jnp.sum(total_q[rows, :].T, axis=0, keepdims=True)
    total_k[...] = jnp.zeros_like(total_k)
    total_v[...] = jnp.zeros_like(total_v)

    def query_tile(index, carry):
        first = pl.multiple_of(index * tile, tile)
        query = queries[pl.ds(first, tile), :]
        grad_tile = grad_here[pl.ds(first, tile), :]
        seg_query = seg_row[pl.ds(index, 1), :]
        lse_tile = lse[pl.ds(index, 1), :]
        delta_tile = delta[pl.ds(index, 1), :]

        def step(is_masked, at, running):
            key_first = pl.multiple_of(at * tile, tile)
            here = pl.ds(key_first, tile)
            scores = lax.dot_general(keys[here, :], query, NT, preferred_element_type=f32) * (
                scale * LOG2E
            )
            probs = jnp.exp2(scores - lse_tile)
            if is_masked:
                allowed = tile_mask(seg_col[here, :], seg_query, key_first, first)
                probs = jnp.where(allowed, probs, 0.0)
            dprobs = lax.dot_general(values[here, :], grad_tile, NT, preferred_element_type=f32)
            dscores = (probs * (dprobs - delta_tile)).astype(bf16)
            total_v[here, :] += jnp.dot(probs.astype(bf16), grad_tile, preferred_element_type=f32)
            total_k[here, :] += jnp.dot(dscores, query, preferred_element_type=f32)
            return running + jnp.dot(keys_t[:, here], dscores, preferred_element_type=f32)

        running = jnp.zeros((width, tile), f32)
        running = lax.fori_loop(
            0, jnp.minimum(index, prompt_tiles), functools.partial(step, False), running
        )
        running = lax.fori_loop(
            first_tile[index], index + 1, functools.partial(step, True), running
        )
        total_q[pl.ds(first, tile), :] = running.T
        return carry

    lax.fori_loop(0, tiles, query_tile, 0)

    def send(block, carry):
        target = pl.ds(pl.multiple_of(place[block] * block_len, block_len), block_len)
        source = pl.ds(pl.multiple_of(block * block_len, block_len), block_len)
        grad_q[target, :] = total_q[source, :] * scale
        grad_k[target, :] = total_k[source, :] * scale
        grad_v[target, :] = total_v[source, :].astype(bf16)
        return carry

    lax.fori_loop(0, blocks, send, 0)


def attention_forward(
    raw, inv, gain_q, gain_k, seg_col, seg_row, place, first_tile, tile, prompt_tiles, block_len, scale
):
    group, width = raw.shape[0], raw.shape[1] // 3
    head_dim = 128
    heads = width // head_dim
    tiles = group // tile

    def part(which):
        return pl.BlockSpec((group, head_dim), lambda h, *_: (0, which * heads + h))

    def whole(shape):
        return pl.BlockSpec(shape, lambda h, *_: (0,) * len(shape))

    head = pl.BlockSpec((group, head_dim), lambda h, *_: (0, h))
    return pl.pallas_call(
        functools.partial(forward_kernel, tile, prompt_tiles, block_len, scale),
        grid_spec=pltpu.PrefetchScalarGridSpec(
            num_scalar_prefetch=2,
            grid=(heads,),
            in_specs=[
                part(0),
                part(1),
                part(2),
                whole((group, 2)),
                pl.BlockSpec((1, head_dim), lambda h, *_: (0, h)),
                pl.BlockSpec((1, head_dim), lambda h, *_: (0, h)),
                whole((group, 1)),
                whole((tiles, tile)),
            ],
            out_specs=[
                head,
                pl.BlockSpec((None, tiles, tile), lambda h, *_: (h, 0, 0)),
                head,
                head,
                head,
            ],
            scratch_shapes=[
                pltpu.VMEM((head_dim, group), bf16),
                pltpu.VMEM((group, head_dim), f32),
            ],
        ),
        out_shape=[
            jax.ShapeDtypeStruct((group, width), bf16),
            jax.ShapeDtypeStruct((heads, tiles, tile), f32),
            jax.ShapeDtypeStruct((group, width), bf16),
            jax.ShapeDtypeStruct((group, width), bf16),
            jax.ShapeDtypeStruct((group, width), bf16),
        ],
        compiler_params=pltpu.CompilerParams(vmem_limit_bytes=56 * 2**20),
        cost_estimate=pl.CostEstimate(
            flops=2 * heads * group * group * head_dim * 2,
            bytes_accessed=32 * group * width,
            transcendentals=0,
        ),
        name="attention_forward",
    )(place, first_tile, raw, raw, raw, inv, gain_q, gain_k, seg_col, seg_row)


def attention_backward(
    queries, keys, values, lse, out, grad_out, seg_col, seg_row, place, first_tile, tile, prompt_tiles, block_len, scale
):
    group, width = queries.shape
    head_dim = 128
    heads = width // head_dim
    tiles = group // tile

    def whole(shape):
        return pl.BlockSpec(shape, lambda h, *_: (0,) * len(shape))

    head = pl.BlockSpec((group, head_dim), lambda h, *_: (0, h))
    return pl.pallas_call(
        functools.partial(backward_kernel, tile, prompt_tiles, block_len, scale),
        grid_spec=pltpu.PrefetchScalarGridSpec(
            num_scalar_prefetch=2,
            grid=(heads,),
            in_specs=[
                head,
                head,
                head,
                pl.BlockSpec((None, tiles, tile), lambda h, *_: (h, 0, 0)),
                head,
                head,
                whole((group, 1)),
                whole((tiles, tile)),
            ],
            out_specs=[head, head, head],
            scratch_shapes=[
                pltpu.VMEM((head_dim, group), bf16),
                pltpu.VMEM((group, head_dim), bf16),
                pltpu.VMEM((tiles, tile), f32),
                pltpu.VMEM((group, head_dim), f32),
                pltpu.VMEM((group, head_dim), f32),
                pltpu.VMEM((group, head_dim), f32),
            ],
        ),
        out_shape=[
            jax.ShapeDtypeStruct((group, width), f32),
            jax.ShapeDtypeStruct((group, width), f32),
            jax.ShapeDtypeStruct((group, width), bf16),
        ],
        compiler_params=pltpu.CompilerParams(vmem_limit_bytes=56 * 2**20),
        cost_estimate=pl.CostEstimate(
            flops=5 * heads * group * group * head_dim,
            bytes_accessed=32 * group * width,
            transcendentals=0,
        ),
        name="attention_backward",
    )(place, first_tile, queries, keys, values, lse, out, grad_out, seg_col, seg_row)


def slot_table(expert_rows, order_rows, gate_rows, count_experts, capacity):
    chosen = expert_rows.T[None, :, :] == jnp.arange(count_experts, dtype=jnp.int32)[:, None, None]
    holds = jnp.any(chosen, axis=1)
    order = jnp.sum(jnp.where(chosen, order_rows.T[None], 0), axis=1)
    gate = jnp.sum(jnp.where(chosen, gate_rows.T[None], 0.0), axis=1)
    earlier = holds[:, None, :] & (order[:, None, :] < order[:, :, None])
    slot = jnp.sum(earlier.astype(jnp.int32), axis=2)
    return (jnp.where(holds & (slot < capacity), slot, -1), gate)


def tied(array, *after):
    return lax.optimization_barrier((array, *after))[0]


def barrier(*arrays):
    return lax.optimization_barrier(arrays)


class Line:
    def __init__(self):
        peers = lax.axis_size("ctx")
        self.chips = peers // 2
        self.chip = lax.axis_index("ctx") // 2
        self.up = [(i, i + 2) for i in range(peers - 2)]
        self.down = [(i + 2, i) for i in range(peers - 2)]
        self.pair = [(i, i ^ 1) for i in range(peers)]
        steps = range(1, self.chips)
        every = [d for s in steps for d in (s, -s)]
        self.orders = [
            sorted((d for d in every if 0 <= z + d < self.chips), key=lambda d: (abs(d), -d))
            for z in range(self.chips)
        ]

    def step(self, from_below, from_above):
        return (
            lax.ppermute(from_below, "ctx", self.up),
            lax.ppermute(from_above, "ctx", self.down),
        )

    def other(self, rows):
        return lax.ppermute(rows, "ctx", self.pair)

    def take(self, turn, arrived):
        offsets = [self.orders[z][turn - 1] for z in range(self.chips)]
        offset = jnp.array(offsets, jnp.int32)[self.chip]
        kinds = sorted(set(offsets))
        chosen = arrived[kinds[0]]
        for kind in kinds[1:]:
            chosen = jnp.where(offset == kind, arrived[kind], chosen)
        return chosen, self.chip + offset


def swap_partners(groups, shift):
    return [(i, i ^ shift) for i in range(groups)]


def swap_dp(part, shift):
    return lax.ppermute(part, "dp", swap_partners(lax.axis_size("dp"), shift))


def first_dp(part):
    return [swap_dp(part, 1), swap_dp(part, 2)]


def second_dp(pieces, axis):
    half = pieces[0].shape[axis] // 2
    return [
        swap_dp(lax.slice_in_dim(pieces[0], 0, half, axis=axis), 2),
        swap_dp(lax.slice_in_dim(pieces[1], half, 2 * half, axis=axis), 1),
    ]


def join_dp(part, pieces, axis):
    mine = lax.axis_index("dp")
    size = part.shape[axis]
    half = size // 2

    def both(shift):
        return [(mine ^ shift) * size, (mine ^ shift) * size + half]

    parts = [
        (part, both(0)),
        (pieces[0], both(1)),
        (pieces[1], both(2)),
        (pieces[2], both(3)[:1]),
        (pieces[3], both(3)[1:]),
    ]
    return join(parts, axis, size * lax.axis_size("dp"), half)


def pick_dp(term, shift, axis):
    size = term.shape[axis] // lax.axis_size("dp")
    return lax.dynamic_slice_in_dim(term, (lax.axis_index("dp") ^ shift) * size, size, axis)


def scatter_one(term, shift, axis):
    return swap_dp(pick_dp(term, shift, axis), shift)


def total_dp(term, pieces, axis):
    groups = lax.axis_size("dp")
    size = term.shape[axis] // groups
    total = lax.dynamic_slice_in_dim(term, lax.axis_index("dp") * size, size, axis).astype(f32)
    for piece in pieces:
        total = total + piece.astype(f32)
    return total


def sum_small(array, axes="ctx"):
    return jnp.sum(lax.all_gather(array, axes, axis=0, tiled=False), axis=0)


def project_kernel(places, own, other, weight, gain, *rest):
    normed, raw, square = rest[-3:]

    def work(rows_ref):
        rows = rows_ref[...].astype(f32)
        hat = rows * lax.rsqrt(jnp.mean(rows * rows, axis=1, keepdims=True) + epsilon)
        low = (hat * gain[...]).astype(bf16)
        normed[...] = low
        product = jnp.dot(low, weight[...], preferred_element_type=f32)
        raw[...] = product
        third = product.shape[1] // 3
        for which in range(2):
            part = product[:, which * third : (which + 1) * third]
            square[which : which + 1, :] = jnp.sum((part * part).T, axis=0, keepdims=True)

    pl.when(pl.program_id(0) == 0)(lambda: work(own))
    pl.when(pl.program_id(0) == 1)(lambda: work(other))


def project(unit_index, own, other, weight, gain, peers, kept=()):
    rows, width = own.shape
    columns = weight.shape[1]

    def fixed(shape):
        return pl.BlockSpec(shape, lambda s, *_: (0,) * len(shape))

    return pl.pallas_call(
        project_kernel,
        grid_spec=pltpu.PrefetchScalarGridSpec(
            num_scalar_prefetch=1,
            grid=(2,),
            in_specs=[
                fixed((rows, width)),
                fixed((rows, width)),
                fixed((width, columns)),
                fixed((1, width)),
            ]
            + [pl.BlockSpec(memory_space=pl.ANY)] * len(kept),
            out_specs=[
                pl.BlockSpec((rows, width), lambda s, at: (at[s], 0)),
                pl.BlockSpec((rows, columns), lambda s, at: (at[s], 0)),
                pl.BlockSpec((None, 2, rows), lambda s, at: (at[s], 0, 0)),
            ],
        ),
        out_shape=[
            jax.ShapeDtypeStruct((peers * rows, width), bf16),
            jax.ShapeDtypeStruct((peers * rows, columns), f32),
            jax.ShapeDtypeStruct((peers, 2, rows), f32),
        ],
        input_output_aliases={5 + i: i for i in range(len(kept))},
        compiler_params=pltpu.CompilerParams(vmem_limit_bytes=56 * 2**20),
        name="project",
    )(unit_index, own, other, weight, gain, *kept)


def join_kernel(axis, blocks, block, at, *refs):
    out = refs[-1]
    turn = 0
    for ref, count in zip(refs[:-1], blocks):
        for index in range(count):
            here = (slice(None),) * axis + (slice(index * block, (index + 1) * block),)

            @pl.when(pl.program_id(0) == turn)
            def copy(ref=ref, here=here):
                out[...] = ref[here]

            turn += 1


def join(parts, axis, length, block):
    shape = list(parts[0][0].shape)
    shape[axis] = block
    blocks = [len(starts) for _, starts in parts]
    at = jnp.stack([start // block for _, starts in parts for start in starts]).astype(jnp.int32)
    rank = len(shape)

    def target(turn, at):
        return tuple(at[turn] if index == axis else 0 for index in range(rank))

    def fixed(part):
        return pl.BlockSpec(
            part.shape, lambda turn, at: (0,) * rank, pipeline_mode=pl.Buffered(1)
        )

    return pl.pallas_call(
        functools.partial(join_kernel, axis, blocks, block),
        grid_spec=pltpu.PrefetchScalarGridSpec(
            num_scalar_prefetch=1,
            grid=(sum(blocks),),
            in_specs=[fixed(part) for part, _ in parts],
            out_specs=pl.BlockSpec(tuple(shape), target),
        ),
        out_shape=jax.ShapeDtypeStruct(
            tuple(length if index == axis else size for index, size in enumerate(shape)),
            parts[0][0].dtype,
        ),
        compiler_params=pltpu.CompilerParams(vmem_limit_bytes=40 * 2**20),
        name="join",
    )(at, *[part for part, _ in parts])


def lay_kernel(at, own, other, *rest):
    out = rest[-1]

    def work(source):
        out[...] = source[...].astype(f32)

    pl.when(pl.program_id(0) == 0)(lambda: work(own))
    pl.when(pl.program_id(0) == 1)(lambda: work(other))


def lay(at, own, other, out_shape, pieces, index, kept=()):
    rows, columns = own.shape
    block = (rows, columns // pieces)
    return pl.pallas_call(
        lay_kernel,
        grid_spec=pltpu.PrefetchScalarGridSpec(
            num_scalar_prefetch=1,
            grid=(2, pieces),
            in_specs=[pl.BlockSpec(block, lambda s, t, at: (0, t))] * 2
            + [pl.BlockSpec(memory_space=pl.ANY)] * len(kept),
            out_specs=pl.BlockSpec(block, lambda s, t, at: index(at[s], t)),
        ),
        out_shape=jax.ShapeDtypeStruct(out_shape, f32),
        input_output_aliases={3: 0} if kept else {},
        name="lay",
    )(at, own, other, *kept)


def expert_kernel(
    unit, own, other, cots, slots, gates, columns, w_gate, w_up, w_down, *rest
):
    expert_in, grad_rows, hidden, grad_gate, grad_up, part, total, ready = rest[-8:]
    expert, piece = pl.program_id(0), pl.program_id(1)
    last_expert = expert == pl.num_programs(0) - 1
    last_piece = piece == pl.num_programs(1) - 1
    room, width = expert_in.shape[1:]
    rows = own.shape[0]
    core = unit[1]

    @pl.when(piece == 0)
    def bring():
        at = lax.broadcasted_iota(jnp.int32, (room, rows), 0)
        for s in range(2):
            found = at == slots[s, pl.ds(expert, 1), :]
            picks = jnp.where(found, 1.0, 0.0).astype(bf16)
            slot_gate = jnp.sum(
                jnp.where(found, gates[s, pl.ds(expert, 1), :], 0.0), axis=1, keepdims=True
            )
            grad_rows[s] = (
                jnp.dot(picks, cots[s], preferred_element_type=f32) * slot_gate
            ).astype(bf16)

            @pl.when(core == s)
            def from_own():
                expert_in[s] = jnp.dot(picks, own[...], preferred_element_type=f32).astype(bf16)

            @pl.when(core != s)
            def from_other():
                expert_in[s] = jnp.dot(picks, other[...], preferred_element_type=f32).astype(bf16)

    rows_in = expert_in[...].reshape(2 * room, width)
    gate_pre = jnp.dot(rows_in, w_gate[...], preferred_element_type=f32)
    up_pre = jnp.dot(rows_in, w_up[...], preferred_element_type=f32)
    grad_hidden = lax.dot_general(
        grad_rows[...].reshape(2 * room, width), w_down[...], NT, preferred_element_type=f32
    )
    sigmoid = 1.0 / (1.0 + jnp.exp(-gate_pre))
    silu = gate_pre * sigmoid
    hidden[...] = (silu * up_pre).astype(bf16).reshape(hidden.shape)
    gate_here = (grad_hidden * up_pre * sigmoid * (1.0 + gate_pre * (1.0 - sigmoid))).astype(bf16)
    up_here = (grad_hidden * silu).astype(bf16)
    grad_gate[...] = gate_here.reshape(grad_gate.shape)
    grad_up[...] = up_here.reshape(grad_up.shape)

    def back():
        return lax.dot_general(gate_here, w_gate[...], NT, preferred_element_type=f32) + lax.dot_general(
            up_here, w_up[...], NT, preferred_element_type=f32
        )

    @pl.when(piece == 0)
    def first():
        total[...] = back()

    @pl.when(piece != 0)
    def later():
        total[...] += back()

    @pl.when(last_piece)
    def keep():
        for s in range(2):
            ready[s, pl.ds(pl.multiple_of(expert * room, 16), room), :] = total[
                s * room : (s + 1) * room, :
            ].astype(bf16)

    @pl.when(last_piece & last_expert)
    def send():
        for s in range(2):
            at = lax.broadcasted_iota(jnp.int32, (rows, ready.shape[1]), 1)
            here = columns[s]
            found = at == here[:, 0:1]
            for e in range(1, here.shape[1]):
                found = found | (at == here[:, e : e + 1])
            part[s] = jnp.dot(
                jnp.where(found, 1.0, 0.0).astype(bf16), ready[s], preferred_element_type=f32
            ).astype(bf16)


def expert_unit(unit, own, other, cot_all, slots, gates, columns, w_gate, w_up, w_down, room, kept=(), piece=256):
    rows, width = own.shape
    experts, _, inner = w_gate.shape
    peers = cot_all.shape[0]
    wide_shape = (peers, experts, room, width)
    thin_shape = (peers, experts, room, inner)
    anywhere = pl.BlockSpec(memory_space=pl.ANY)
    once = pl.Buffered(1)

    def fixed(shape):
        return pl.BlockSpec(shape, lambda e, f, u: (0,) * len(shape), pipeline_mode=once)

    def chip(shape):
        return pl.BlockSpec((2, *shape), lambda e, f, u: (u[0], 0, 0), pipeline_mode=once)

    wide = pl.BlockSpec((2, None, room, width), lambda e, f, u: (u[0], e, 0, 0))
    thin = pl.BlockSpec((2, None, room, piece), lambda e, f, u: (u[0], e, 0, f))
    return pl.pallas_call(
        expert_kernel,
        grid_spec=pltpu.PrefetchScalarGridSpec(
            num_scalar_prefetch=1,
            grid=(experts, inner // piece),
            in_specs=[
                fixed((rows, width)), fixed((rows, width)), chip((rows, width)),
                chip((experts, rows)), chip((experts, rows)), chip((rows, experts)),
                pl.BlockSpec((None, width, piece), lambda e, f, u: (e, 0, f)),
                pl.BlockSpec((None, width, piece), lambda e, f, u: (e, 0, f)),
                pl.BlockSpec((None, piece, width), lambda e, f, u: (e, f, 0)),
            ] + [anywhere] * len(kept),
            out_specs=[wide, wide, thin, thin, thin,
                pl.BlockSpec((2, rows, width), lambda e, f, u: (u[0], 0, 0))],
            scratch_shapes=[
                pltpu.VMEM((2 * room, width), f32),
                pltpu.VMEM((2, experts * room, width), bf16),
            ],
        ),
        out_shape=[
            jax.ShapeDtypeStruct(shape, bf16)
            for shape in [wide_shape] * 2 + [thin_shape] * 3 + [cot_all.shape]
        ],
        input_output_aliases={10 + i: i for i in range(len(kept))},
        compiler_params=pltpu.CompilerParams(vmem_limit_bytes=60 * 2**20),
        name="expert_unit",
    )(unit, own, other, cot_all, slots, gates, columns, w_gate, w_up, w_down, *kept)


def out_kernel(hidden, w_down, slots, gates, columns, part, ready):
    expert = pl.program_id(1)
    room = hidden.shape[1]
    rows = slots.shape[2]
    at = lax.broadcasted_iota(jnp.int32, (room, rows), 0)
    product = jnp.dot(
        hidden[...].reshape(2 * room, hidden.shape[2]), w_down[...], preferred_element_type=f32
    )
    for s in range(2):
        found = at == slots[s, pl.ds(expert, 1), :]
        slot_gate = jnp.sum(jnp.where(found, gates[s, pl.ds(expert, 1), :], 0.0), axis=1, keepdims=True)
        ready[s, pl.ds(pl.multiple_of(expert * room, 16), room), :] = (
            product[s * room : (s + 1) * room] * slot_gate
        ).astype(bf16)

    @pl.when(expert == pl.num_programs(1) - 1)
    def send():
        for s in range(2):
            at = lax.broadcasted_iota(jnp.int32, (rows, ready.shape[1]), 1)
            here = columns[s]
            found = at == here[:, 0:1]
            for e in range(1, here.shape[1]):
                found = found | (at == here[:, e : e + 1])
            part[s] = jnp.dot(
                jnp.where(found, 1.0, 0.0).astype(bf16), ready[s], preferred_element_type=f32
            ).astype(bf16)


def expert_out(hidden, w_down, slots, gates, columns):
    peers, experts, room, inner = hidden.shape
    width = w_down.shape[2]
    rows = slots.shape[2]
    return pl.pallas_call(
        out_kernel,
        grid=(peers // 2, experts),
        in_specs=[
            pl.BlockSpec((2, None, room, inner), lambda c, e: (c, e, 0, 0)),
            pl.BlockSpec((None, inner, width), lambda c, e: (e, 0, 0)),
            pl.BlockSpec((2, experts, rows), lambda c, e: (c, 0, 0)),
            pl.BlockSpec((2, experts, rows), lambda c, e: (c, 0, 0)),
            pl.BlockSpec((2, rows, experts), lambda c, e: (c, 0, 0)),
        ],
        out_specs=pl.BlockSpec((2, rows, width), lambda c, e: (c, 0, 0)),
        out_shape=jax.ShapeDtypeStruct((peers, rows, width), bf16),
        scratch_shapes=[pltpu.VMEM((2, experts * room, width), bf16)],
        compiler_params=pltpu.CompilerParams(vmem_limit_bytes=60 * 2**20),
        name="expert_out",
    )(hidden, w_down, slots, gates, columns)


def on_device(
    tokens,
    cotangent,
    wqkv,
    wo,
    attn_gain,
    query_gain,
    key_gain,
    moe_gain,
    w_gate,
    w_up,
    w_down,
    expert_ids,
    gates,
    slot_order,
    block_assign,
    segment_ids,
):
    count_rows, width = tokens.shape
    head_dim = width // HEADS
    scale = head_dim ** (-0.5)
    peers = lax.axis_size("ctx")
    groups = lax.axis_size("dp")
    me = lax.axis_index("ctx")
    core = me % 2
    my_dp = lax.axis_index("dp")
    group_rows = count_rows * peers
    rep = max(1, peers // HEADS)
    own_heads = max(1, HEADS // peers)
    own_width = own_heads * head_dim
    first_head = (me // rep) * own_heads
    block_len = count_rows // BLK_DEV
    tile = 512
    line = Line()
    turns = range(1, line.chips)

    full_gate = lax.all_gather(w_gate, "dp", axis=1, tiled=True)

    assign = block_assign[0]
    count_blocks = assign.shape[0]
    place = jnp.argmax(
        assign[None, :] == jnp.arange(count_blocks, dtype=jnp.int32)[:, None], axis=1
    ).astype(jnp.int32)
    cont = segment_ids[0]
    prompt_len = group_rows - cont.shape[0]
    prompt_tiles = prompt_len // tile
    seg_logical = jnp.concatenate([jnp.full((prompt_len,), -1, jnp.int32), cont])
    tiles = group_rows // tile
    tile_seg = seg_logical.reshape(tiles, tile)[:, 0]
    first_tile = jnp.where(
        tile_seg < 0,
        jnp.arange(tiles, dtype=jnp.int32),
        jnp.sum((seg_logical[None, :] < tile_seg[:, None]).astype(jnp.int32), axis=1) // tile,
    ).astype(jnp.int32)
    seg_col = seg_logical[:, None]
    seg_row = seg_logical.reshape(tiles, tile)

    local_experts = w_gate.shape[0]
    count_experts = local_experts * peers
    capacity = 9 * count_rows * TOP // (8 * count_experts)
    room = (capacity + 15) // 16 * 16
    slot, gate = slot_table(expert_ids, slot_order, gates, count_experts, capacity)
    table = jnp.stack(
        [
            slot.reshape(peers, local_experts, count_rows).astype(f32),
            gate.reshape(peers, local_experts, count_rows),
        ],
        axis=1,
    )

    inputs = tokens.astype(f32)
    below, above = line.step(tokens, tokens)
    other = line.other(tokens)
    w_part = lax.dynamic_slice_in_dim(
        wqkv.reshape(wqkv.shape[0], 3, HEADS, head_dim), first_head, own_heads, 2
    ).reshape(wqkv.shape[0], 3 * own_width)
    w_pieces = first_dp(w_part)
    w_pieces = w_pieces + second_dp(w_pieces, 0)
    gain_part = jnp.stack([attn_gain, query_gain, key_gain, moe_gain])
    gain_all = jnp.zeros((4, width), bf16)
    for shift in range(groups):
        piece = swap_dp(gain_part, shift) if shift else gain_part
        gain_all = lax.dynamic_update_slice_in_dim(
            gain_all, piece, (my_dp ^ shift) * gain_part.shape[1], 1
        )
    gain_all = gain_all.astype(f32)
    below, above, other, gain_all, table, wo, *w_pieces = barrier(
        below, above, other, gain_all, table, wo, *w_pieces
    )
    w_own = join_dp(w_part, w_pieces, 0)
    gain_attn, gain_moe = gain_all[0:1], gain_all[3:4]
    gain_own = lax.dynamic_slice_in_dim(gain_all, first_head * head_dim, own_width, 1)
    gain_q, gain_k = gain_own[1:2], gain_own[2:3]

    half_rows = wo.shape[0] // 2
    arrived = {-1: below, 1: above}
    own, chip = tokens, line.chip
    kept = ()
    for turn in turns:
        if turn + 1 < line.chips:
            below, above = line.step(below, above)
            arrived[-turn - 1], arrived[turn + 1] = below, above
        next_own, next_chip = line.take(turn, arrived)
        next_other = line.other(next_own)
        at = jnp.stack([2 * chip + core, 2 * chip + 1 - core]).astype(jnp.int32)
        kept = project(at, own, other, w_own, gain_attn, peers, kept)
        travel = []
        if turn == 1:
            wo_half = lax.dynamic_slice_in_dim(wo, core * half_rows, half_rows, 0)
            wo_pieces = first_dp(wo_half)
            travel = wo_pieces + second_dp(wo_pieces, 0)
        if turn == 2:
            wo_pieces = [wo_half, *travelled[:2], jnp.concatenate(travelled[2:], axis=0)]
            wo_mine = jnp.concatenate(wo_pieces, axis=0)
            down_pieces = first_dp(w_down)
            travel = [line.other(wo_mine), wo_mine, full_gate] + down_pieces
            table = lax.all_to_all(table, "ctx", split_axis=0, concat_axis=0, tiled=True)
            travel.append(table)
        own, other, chip = next_own, next_other, next_chip
        square = kept[2]
        below, above, own, other, square, w_down, *travelled = barrier(
            below, above, own, other, square, w_down, *travel
        )
        if turn == 2:
            wo_theirs, wo_mine, full_gate, down_one, down_two, table = travelled
        kept = (kept[0], kept[1], square)
        if turn + 1 < line.chips:
            arrived[-turn - 1], arrived[turn + 1] = below, above
    cotangent_now, other = barrier(cotangent, other)
    cot_all = lax.all_gather(cotangent_now, "ctx", axis=0, tiled=True).reshape(
        peers, count_rows, width
    )
    down_pieces = [down_one, down_two] + second_dp([down_one, down_two], 1)
    at = jnp.stack([2 * chip + core, 2 * chip + 1 - core]).astype(jnp.int32)
    normed_all, raw, square = project(at, own, other, w_own, gain_attn, peers, kept)
    square = sum_small(square.transpose(1, 0, 2).reshape(2, group_rows)) * (1.0 / rep)
    inv_qk = lax.rsqrt(square / width + epsilon).T
    slot = table[:, 0].astype(jnp.int32)
    gate_rows = table[:, 1]
    offsets = (jnp.arange(local_experts, dtype=jnp.int32) * room)[None, :, None]
    columns = jnp.where(slot >= 0, slot + offsets, -1).transpose(0, 2, 1)

    inv_qk, w_up, columns, *down_pieces = barrier(inv_qk, w_up, columns, *down_pieces)
    up_pieces = first_dp(w_up)
    attended, lse, queries, keys, values = attention_forward(
        raw,
        inv_qk,
        gain_q,
        gain_k,
        seg_col,
        seg_row,
        place,
        first_tile,
        tile,
        prompt_tiles,
        block_len,
        scale,
    )
    attended, *up_pieces = barrier(attended, *up_pieces)
    up_pieces = up_pieces + second_dp(up_pieces, 1)
    attn_low = lax.all_to_all(
        attended.reshape(peers, count_rows, own_width), "ctx", split_axis=0, concat_axis=0, tiled=True
    )[::rep]
    full_down = join_dp(w_down, down_pieces, 1)
    starts = [(my_dp ^ shift) * wo.shape[0] for shift in range(groups)]
    full_wo = join(
        [
            (wo_mine, [start + core * half_rows for start in starts]),
            (wo_theirs, [start + (1 - core) * half_rows for start in starts]),
        ],
        0,
        width,
        half_rows,
    )
    attn_low, full_wo, full_down, *up_pieces = barrier(attn_low, full_wo, full_down, *up_pieces)
    attn_low = attn_low.transpose(1, 0, 2).reshape(count_rows, width)
    state = inputs + jnp.dot(attn_low, full_wo, preferred_element_type=f32)
    inv_state = rms_scale(state)
    hat_state = state * inv_state
    normed_moe = (hat_state * gain_moe).astype(bf16)
    full_up = join_dp(w_up, up_pieces, 1)

    normed_moe, full_up, cot_all = barrier(normed_moe, full_up, cot_all)
    below, above = normed_moe, normed_moe
    own, chip = normed_moe, line.chip
    arrived = {}
    kept = ()
    for turn in range(line.chips):
        if turn + 1 < line.chips:
            below, above = line.step(below, above)
            arrived[-turn - 1], arrived[turn + 1] = below, above
        if turn > 0:
            own, chip = line.take(turn, arrived)
        other = line.other(own)
        kept = expert_unit(
            jnp.stack([chip, core]).astype(jnp.int32),
            own,
            other,
            cot_all,
            slot,
            gate_rows,
            columns,
            full_gate,
            full_up,
            full_down,
            room,
            kept,
        )
        if turn + 1 < line.chips:
            below, above, *kept = barrier(below, above, *kept)
            arrived[-turn - 1], arrived[turn + 1] = below, above
    expert_in, grad_rows, hidden, grad_gate_pre, grad_up_pre, part_moe = kept
    grad_normed_moe = lax.psum_scatter(
        part_moe.reshape(group_rows, width), "ctx", scatter_dimension=0, tiled=True
    )

    part_mixed = expert_out(hidden, full_down, slot, gate_rows, columns)
    grad_down = jnp.einsum("sncf,sncd->nfd", hidden, grad_rows, preferred_element_type=f32)
    grad_down = grad_down.astype(bf16)
    part_mixed, grad_down, expert_in = barrier(part_mixed, grad_down, expert_in)
    down_pieces = [scatter_one(grad_down, shift, 1) for shift in (1, 2, 3)]
    grad_gate = jnp.einsum("sncd,sncf->ndf", expert_in, grad_gate_pre, preferred_element_type=f32)
    grad_up = jnp.einsum("sncd,sncf->ndf", expert_in, grad_up_pre, preferred_element_type=f32)
    grad_gate, grad_up = grad_gate.astype(bf16), grad_up.astype(bf16)
    grad_normed_moe, part_mixed, grad_gate, grad_up, *down_pieces = barrier(
        grad_normed_moe, part_mixed, grad_gate, grad_up, *down_pieces
    )
    mixed = lax.psum_scatter(
        part_mixed.reshape(group_rows, width), "ctx", scatter_dimension=0, tiled=True
    )

    gate_pieces = [scatter_one(grad_gate, shift, 1) for shift in (1, 2)]
    grad_normed_moe = grad_normed_moe.astype(f32)
    moe_gain_term = jnp.sum(grad_normed_moe * hat_state, axis=0)
    grad_state = cotangent.astype(f32) + rms_back(grad_normed_moe * gain_moe, hat_state, inv_state)
    grad_branch = grad_state.astype(bf16)
    grad_attn = lax.dot_general(grad_branch, full_wo, NT, preferred_element_type=f32).astype(bf16)
    grad_attn = grad_attn.reshape(count_rows, peers // rep, own_width).transpose(1, 0, 2)
    grad_attn = jnp.repeat(grad_attn, rep, axis=0)
    grad_attended = lax.all_to_all(
        grad_attn, "ctx", split_axis=0, concat_axis=0, tiled=True
    ).reshape(group_rows, own_width)
    part_out = lax.dot_general(attn_low, grad_branch, TN, preferred_element_type=f32).astype(bf16)
    part_out = part_out.reshape(groups, 2, half_rows, width)
    out_theirs = line.other(lax.dynamic_index_in_dim(part_out, 1 - core, 1, keepdims=False))
    part_out = lax.dynamic_index_in_dim(part_out, core, 1, keepdims=False).astype(f32)
    part_out = (part_out + out_theirs.astype(f32)).astype(bf16)
    down_sum = total_dp(grad_down, down_pieces, 1)
    grad_attended, part_out, down_sum, *gate_pieces = barrier(
        grad_attended, part_out, down_sum, *gate_pieces
    )
    gate_pieces.append(scatter_one(grad_gate, 3, 1))
    out_pieces = [scatter_one(part_out, shift, 0) for shift in (1, 2)]
    grad_q, grad_k, grad_v = attention_backward(
        queries,
        keys,
        values,
        lse,
        attended,
        grad_attended,
        seg_col,
        seg_row,
        place,
        first_tile,
        tile,
        prompt_tiles,
        block_len,
        scale,
    )
    grad_q, gate_last, *out_pieces = barrier(grad_q, gate_pieces[2], *out_pieces)
    gate_pieces[2] = gate_last
    out_pieces.append(scatter_one(part_out, 3, 0))
    hat_q = raw[:, :own_width] * inv_qk[:, 0:1]
    hat_k = raw[:, own_width : 2 * own_width] * inv_qk[:, 1:2]
    query_gain_term = jnp.sum(grad_q * hat_q, axis=0)
    key_gain_term = jnp.sum(grad_k * hat_k, axis=0)
    means = jnp.stack(
        [
            jnp.sum(grad_q * gain_q * hat_q, axis=1),
            jnp.sum(grad_k * gain_k * hat_k, axis=1),
        ]
    )
    means = (sum_small(means) * (1.0 / (rep * width))).T
    grad_raw_q = inv_qk[:, 0:1] * (grad_q * gain_q - hat_q * means[:, 0:1])
    grad_raw_k = inv_qk[:, 1:2] * (grad_k * gain_k - hat_k * means[:, 1:2])
    grad_qkv = jnp.concatenate([grad_raw_q.astype(bf16), grad_raw_k.astype(bf16), grad_v], axis=1)
    part_normed = lax.dot_general(grad_qkv, w_own, NT, preferred_element_type=f32) * (1.0 / rep)
    part_normed = part_normed.astype(bf16)
    part_normed, grad_qkv, mixed, *out_pieces = barrier(part_normed, grad_qkv, mixed, *out_pieces)
    grad_normed = lax.psum_scatter(part_normed, "ctx", scatter_dimension=0, tiled=True)

    out_sum = total_dp(part_out, out_pieces, 0).astype(bf16).reshape(half_rows, width)
    out_share = half_rows // (peers // 2)
    out_sum = lax.all_to_all(
        out_sum.reshape(peers // 2, out_share, width),
        "ctx",
        split_axis=0,
        concat_axis=0,
        tiled=True,
        axis_index_groups=[[2 * z + c for z in range(peers // 2)] for c in range(2)],
    )
    part_qkv = lax.dot_general(normed_all, grad_qkv, TN, preferred_element_type=f32).astype(bf16)
    qkv_pieces = [scatter_one(part_qkv, shift, 0) for shift in (1, 2, 3)]
    gate_sum = total_dp(grad_gate, gate_pieces, 1)
    own_terms = jnp.stack([query_gain_term, key_gain_term]) * (1.0 / rep)
    spread = lax.dynamic_update_slice_in_dim(
        jnp.zeros((2, width), f32), own_terms, first_head * head_dim, 1
    )
    gain_terms = jnp.concatenate([spread, moe_gain_term[None]], axis=0)
    grad_up, gate_sum, gain_terms, out_sum, *qkv_pieces = barrier(
        grad_up, gate_sum, gain_terms, out_sum, *qkv_pieces
    )
    up_pieces = [scatter_one(grad_up, shift, 1) for shift in (1, 2, 3)]
    qkv_sum = total_dp(part_qkv, qkv_pieces, 0).astype(bf16)
    out_sum = jnp.sum(out_sum.astype(f32), axis=0).astype(bf16)
    rows_dp = qkv_sum.shape[0]
    weights = jnp.concatenate([qkv_sum.reshape(out_share, -1), out_sum], axis=1)
    qkv_columns = weights.shape[1] - width
    below, above = weights, weights
    own, chip = weights, line.chip
    arrived = {}
    qkv_kept, out_kept = (), ()
    for turn in range(line.chips):
        if turn + 1 < line.chips:
            below, above = line.step(below, above)
            arrived[-turn - 1], arrived[turn + 1] = below, above
        if turn > 0:
            own, chip = line.take(turn, arrived)
        other = line.other(own)
        at = jnp.stack([2 * chip + core, 2 * chip + 1 - core]).astype(jnp.int32)
        qkv_kept = [
            lay(
                at // rep,
                own[:, :qkv_columns].reshape(rows_dp, 3 * own_width),
                other[:, :qkv_columns].reshape(rows_dp, 3 * own_width),
                (rows_dp, 3 * width),
                3,
                lambda p, t: (0, t * (peers // rep) + p),
                qkv_kept,
            )
        ]
        at = jnp.stack([core * line.chips + chip, (1 - core) * line.chips + chip]).astype(jnp.int32)
        out_kept = [
            lay(
                at,
                own[:, qkv_columns:],
                other[:, qkv_columns:],
                (rows_dp, width),
                1,
                lambda p, t: (p, 0),
                out_kept,
            )
        ]
    qkv_total, out_total = qkv_kept[0], out_kept[0]
    up_sum = total_dp(grad_up, up_pieces, 1)
    output = (state + mixed.astype(f32)).astype(bf16)
    out_total, qkv_total, up_sum, output, grad_normed = barrier(
        out_total, qkv_total, up_sum, output, grad_normed
    )

    grad_normed = grad_normed.astype(f32)
    inv_in = rms_scale(inputs)
    hat_in = inputs * inv_in
    attn_gain_term = jnp.sum(grad_normed * hat_in, axis=0)
    input_grad = (grad_state + rms_back(grad_normed * gain_attn, hat_in, inv_in)).astype(bf16)
    gain_terms = sum_small(jnp.concatenate([attn_gain_term[None], gain_terms], axis=0))
    gain_terms = total_dp(gain_terms, [scatter_one(gain_terms, shift, 1) for shift in (1, 2, 3)], 1)
    return (
        output,
        input_grad,
        qkv_total,
        out_total,
        gain_terms[0],
        gain_terms[1],
        gain_terms[2],
        gain_terms[3],
        gate_sum,
        up_sum,
        down_sum,
    )


def solution(mesh):
    rows = P(("dp", "ctx"), None)
    expert = P("ctx", "dp", None)
    by_dp = P("dp", None)
    return jax.shard_map(
        on_device,
        mesh=mesh,
        in_specs=(
            rows,
            rows,
            by_dp,
            by_dp,
            P("dp"),
            P("dp"),
            P("dp"),
            P("dp"),
            expert,
            expert,
            expert,
            rows,
            rows,
            rows,
            by_dp,
            by_dp,
        ),
        out_specs=(
            rows,
            rows,
            by_dp,
            by_dp,
            P("dp"),
            P("dp"),
            P("dp"),
            P("dp"),
            expert,
            expert,
            expert,
        ),
        check_vma=False,
    )
```

```python
import functools

import jax
import jax.numpy as jnp
from jax import lax
from jax.experimental import pallas as pl
from jax.experimental.pallas import tpu as pltpu
from jax.sharding import PartitionSpec as P

HEADS = 16
TOP = 8
BLK_DEV = 2
LOG2E = 1.4426950408889634

epsilon = 1e-06
masked_value = -1e30
f32 = jnp.float32
bf16 = jnp.bfloat16
NT = (((1,), (1,)), ((), ()))
TN = (((0,), (0,)), ((), ()))


def rms_scale(values_in):
    return lax.rsqrt(jnp.mean(values_in * values_in, axis=-1, keepdims=True) + epsilon)


def rms_back(grad_hat, normed, scale_rows):
    return scale_rows * (grad_hat - normed * jnp.mean(grad_hat * normed, axis=-1, keepdims=True))


def tile_mask(seg_col, seg_row, key_first, query_first):
    rows, columns = seg_col.shape[0], seg_row.shape[1]
    key_pos = key_first + lax.broadcasted_iota(jnp.int32, (rows, columns), 0)
    query_pos = query_first + lax.broadcasted_iota(jnp.int32, (rows, columns), 1)
    return (seg_col == seg_row) & (key_pos <= query_pos)


def forward_kernel(
    tile,
    prompt_tiles,
    block_len,
    scale,
    place,
    first_tile,
    raw_q,
    raw_k,
    raw_v,
    inv,
    gain_q,
    gain_k,
    seg_col,
    seg_row,
    out,
    lse,
    queries,
    keys,
    values,
    values_t,
    out_logical,
):
    group, width = raw_q.shape
    tiles = group // tile
    blocks = group // block_len

    def bring(block, carry):
        source = pl.ds(pl.multiple_of(place[block] * block_len, block_len), block_len)
        target = pl.ds(pl.multiple_of(block * block_len, block_len), block_len)
        scales = inv[source, :]
        queries[target, :] = (raw_q[source, :] * scales[:, 0:1] * gain_q[...]).astype(bf16)
        keys[target, :] = (raw_k[source, :] * scales[:, 1:2] * gain_k[...]).astype(bf16)
        values[target, :] = raw_v[source, :].astype(bf16)
        return carry

    lax.fori_loop(0, blocks, bring, 0)
    for index in range(tiles):
        values_t[:, index * tile : (index + 1) * tile] = values[
            index * tile : (index + 1) * tile, :
        ].T

    def query_tile(index, carry):
        first = pl.multiple_of(index * tile, tile)
        query = queries[pl.ds(first, tile), :]
        seg_query = seg_row[pl.ds(index, 1), :]

        def step(is_masked, at, state):
            largest, total, running = state
            key_first = pl.multiple_of(at * tile, tile)
            scores = lax.dot_general(
                keys[pl.ds(key_first, tile), :], query, NT, preferred_element_type=f32
            ) * (scale * LOG2E)
            if is_masked:
                allowed = tile_mask(seg_col[pl.ds(key_first, tile), :], seg_query, key_first, first)
                scores = jnp.where(allowed, scores, masked_value)
            new_largest = jnp.maximum(largest, jnp.max(scores, axis=0, keepdims=True))
            shrink = jnp.exp2(largest - new_largest)
            terms = jnp.exp2(scores - new_largest)
            total = total * shrink + jnp.sum(terms, axis=0, keepdims=True)
            running = running * shrink + jnp.dot(
                values_t[:, pl.ds(key_first, tile)], terms.astype(bf16), preferred_element_type=f32
            )
            return (new_largest, total, running)

        state = (
            jnp.full((1, tile), masked_value, f32),
            jnp.zeros((1, tile), f32),
            jnp.zeros((width, tile), f32),
        )
        state = lax.fori_loop(
            0, jnp.minimum(index, prompt_tiles), functools.partial(step, False), state
        )
        state = lax.fori_loop(first_tile[index], index + 1, functools.partial(step, True), state)
        largest, total, running = state
        lse[pl.ds(index, 1), :] = largest + jnp.log2(total)
        out_logical[pl.ds(first, tile), :] = (running / total).T
        return carry

    lax.fori_loop(0, tiles, query_tile, 0)

    def send(block, carry):
        target = pl.ds(pl.multiple_of(place[block] * block_len, block_len), block_len)
        source = pl.ds(pl.multiple_of(block * block_len, block_len), block_len)
        out[target, :] = out_logical[source, :].astype(bf16)
        return carry

    lax.fori_loop(0, blocks, send, 0)


def backward_kernel(
    tile,
    prompt_tiles,
    block_len,
    scale,
    place,
    first_tile,
    queries,
    keys,
    values,
    lse,
    out,
    grad_out,
    seg_col,
    seg_row,
    grad_q,
    grad_k,
    grad_v,
    keys_t,
    grad_here,
    delta,
    total_q,
    total_k,
    total_v,
):
    group, width = queries.shape
    tiles = group // tile
    blocks = group // block_len

    def bring(block, carry):
        source = pl.ds(pl.multiple_of(place[block] * block_len, block_len), block_len)
        target = pl.ds(pl.multiple_of(block * block_len, block_len), block_len)
        grad_here[target, :] = grad_out[source, :]
        total_q[target, :] = out[source, :].astype(f32) * grad_out[source, :].astype(f32)
        return carry

    lax.fori_loop(0, blocks, bring, 0)
    for index in range(tiles):
        rows = slice(index * tile, (index + 1) * tile)
        keys_t[:, rows] = keys[rows, :].T
        delta[index : index + 1, :] = jnp.sum(total_q[rows, :].T, axis=0, keepdims=True)
    total_k[...] = jnp.zeros_like(total_k)
    total_v[...] = jnp.zeros_like(total_v)

    def query_tile(index, carry):
        first = pl.multiple_of(index * tile, tile)
        query = queries[pl.ds(first, tile), :]
        grad_tile = grad_here[pl.ds(first, tile), :]
        seg_query = seg_row[pl.ds(index, 1), :]
        lse_tile = lse[pl.ds(index, 1), :]
        delta_tile = delta[pl.ds(index, 1), :]

        def step(is_masked, at, running):
            key_first = pl.multiple_of(at * tile, tile)
            here = pl.ds(key_first, tile)
            scores = lax.dot_general(keys[here, :], query, NT, preferred_element_type=f32) * (
                scale * LOG2E
            )
            probs = jnp.exp2(scores - lse_tile)
            if is_masked:
                allowed = tile_mask(seg_col[here, :], seg_query, key_first, first)
                probs = jnp.where(allowed, probs, 0.0)
            dprobs = lax.dot_general(values[here, :], grad_tile, NT, preferred_element_type=f32)
            dscores = (probs * (dprobs - delta_tile)).astype(bf16)
            total_v[here, :] += jnp.dot(probs.astype(bf16), grad_tile, preferred_element_type=f32)
            total_k[here, :] += jnp.dot(dscores, query, preferred_element_type=f32)
            return running + jnp.dot(keys_t[:, here], dscores, preferred_element_type=f32)

        running = jnp.zeros((width, tile), f32)
        running = lax.fori_loop(
            0, jnp.minimum(index, prompt_tiles), functools.partial(step, False), running
        )
        running = lax.fori_loop(
            first_tile[index], index + 1, functools.partial(step, True), running
        )
        total_q[pl.ds(first, tile), :] = running.T
        return carry

    lax.fori_loop(0, tiles, query_tile, 0)

    def send(block, carry):
        target = pl.ds(pl.multiple_of(place[block] * block_len, block_len), block_len)
        source = pl.ds(pl.multiple_of(block * block_len, block_len), block_len)
        grad_q[target, :] = total_q[source, :] * scale
        grad_k[target, :] = total_k[source, :] * scale
        grad_v[target, :] = total_v[source, :].astype(bf16)
        return carry

    lax.fori_loop(0, blocks, send, 0)


def attention_forward(
    raw, inv, gain_q, gain_k, seg_col, seg_row, place, first_tile, tile, prompt_tiles, block_len, scale
):
    group, width = raw.shape[0], raw.shape[1] // 3
    head_dim = 128
    heads = width // head_dim
    tiles = group // tile

    def part(which):
        return pl.BlockSpec((group, head_dim), lambda h, *_: (0, which * heads + h))

    def whole(shape):
        return pl.BlockSpec(shape, lambda h, *_: (0,) * len(shape))

    head = pl.BlockSpec((group, head_dim), lambda h, *_: (0, h))
    return pl.pallas_call(
        functools.partial(forward_kernel, tile, prompt_tiles, block_len, scale),
        grid_spec=pltpu.PrefetchScalarGridSpec(
            num_scalar_prefetch=2,
            grid=(heads,),
            in_specs=[
                part(0),
                part(1),
                part(2),
                whole((group, 2)),
                pl.BlockSpec((1, head_dim), lambda h, *_: (0, h)),
                pl.BlockSpec((1, head_dim), lambda h, *_: (0, h)),
                whole((group, 1)),
                whole((tiles, tile)),
            ],
            out_specs=[
                head,
                pl.BlockSpec((None, tiles, tile), lambda h, *_: (h, 0, 0)),
                head,
                head,
                head,
            ],
            scratch_shapes=[
                pltpu.VMEM((head_dim, group), bf16),
                pltpu.VMEM((group, head_dim), f32),
            ],
        ),
        out_shape=[
            jax.ShapeDtypeStruct((group, width), bf16),
            jax.ShapeDtypeStruct((heads, tiles, tile), f32),
            jax.ShapeDtypeStruct((group, width), bf16),
            jax.ShapeDtypeStruct((group, width), bf16),
            jax.ShapeDtypeStruct((group, width), bf16),
        ],
        compiler_params=pltpu.CompilerParams(vmem_limit_bytes=56 * 2**20),
        cost_estimate=pl.CostEstimate(
            flops=2 * heads * group * group * head_dim * 2,
            bytes_accessed=32 * group * width,
            transcendentals=0,
        ),
        name="attention_forward",
    )(place, first_tile, raw, raw, raw, inv, gain_q, gain_k, seg_col, seg_row)


def attention_backward(
    queries, keys, values, lse, out, grad_out, seg_col, seg_row, place, first_tile, tile, prompt_tiles, block_len, scale
):
    group, width = queries.shape
    head_dim = 128
    heads = width // head_dim
    tiles = group // tile

    def whole(shape):
        return pl.BlockSpec(shape, lambda h, *_: (0,) * len(shape))

    head = pl.BlockSpec((group, head_dim), lambda h, *_: (0, h))
    return pl.pallas_call(
        functools.partial(backward_kernel, tile, prompt_tiles, block_len, scale),
        grid_spec=pltpu.PrefetchScalarGridSpec(
            num_scalar_prefetch=2,
            grid=(heads,),
            in_specs=[
                head,
                head,
                head,
                pl.BlockSpec((None, tiles, tile), lambda h, *_: (h, 0, 0)),
                head,
                head,
                whole((group, 1)),
                whole((tiles, tile)),
            ],
            out_specs=[head, head, head],
            scratch_shapes=[
                pltpu.VMEM((head_dim, group), bf16),
                pltpu.VMEM((group, head_dim), bf16),
                pltpu.VMEM((tiles, tile), f32),
                pltpu.VMEM((group, head_dim), f32),
                pltpu.VMEM((group, head_dim), f32),
                pltpu.VMEM((group, head_dim), f32),
            ],
        ),
        out_shape=[
            jax.ShapeDtypeStruct((group, width), f32),
            jax.ShapeDtypeStruct((group, width), f32),
            jax.ShapeDtypeStruct((group, width), bf16),
        ],
        compiler_params=pltpu.CompilerParams(vmem_limit_bytes=56 * 2**20),
        cost_estimate=pl.CostEstimate(
            flops=5 * heads * group * group * head_dim,
            bytes_accessed=32 * group * width,
            transcendentals=0,
        ),
        name="attention_backward",
    )(place, first_tile, queries, keys, values, lse, out, grad_out, seg_col, seg_row)


def slot_table(expert_rows, order_rows, gate_rows, count_experts, capacity):
    chosen = expert_rows.T[None, :, :] == jnp.arange(count_experts, dtype=jnp.int32)[:, None, None]
    holds = jnp.any(chosen, axis=1)
    order = jnp.sum(jnp.where(chosen, order_rows.T[None], 0), axis=1)
    gate = jnp.sum(jnp.where(chosen, gate_rows.T[None], 0.0), axis=1)
    earlier = holds[:, None, :] & (order[:, None, :] < order[:, :, None])
    slot = jnp.sum(earlier.astype(jnp.int32), axis=2)
    return (jnp.where(holds & (slot < capacity), slot, -1), gate)


def tied(array, *after):
    return lax.optimization_barrier((array, *after))[0]


def barrier(*arrays):
    return lax.optimization_barrier(arrays)


class Line:
    def __init__(self):
        peers = lax.axis_size("ctx")
        self.chips = peers // 2
        self.chip = lax.axis_index("ctx") // 2
        self.peers = peers
        self.pair = [(i, i ^ 1) for i in range(peers)]
        steps = range(1, self.chips)
        every = [d for s in steps for d in (s, -s)]
        self.orders = [
            sorted((d for d in every if 0 <= z + d < self.chips), key=lambda d: (abs(d), -d))
            for z in range(self.chips)
        ]

    def step(self, turn, from_below, from_above):
        up = [(i, i + 2) for i in range(2 * (turn - 1), self.peers - 2)]
        down = [(i + 2, i) for i in range(self.peers - 2 * turn)]
        return (
            lax.ppermute(from_below, "ctx", up),
            lax.ppermute(from_above, "ctx", down),
        )

    def other(self, rows):
        return lax.ppermute(rows, "ctx", self.pair)

    def take(self, turn, arrived):
        offsets = [self.orders[z][turn - 1] for z in range(self.chips)]
        offset = jnp.array(offsets, jnp.int32)[self.chip]
        kinds = sorted(set(offsets))
        chosen = arrived[kinds[0]]
        for kind in kinds[1:]:
            chosen = jnp.where(offset == kind, arrived[kind], chosen)
        return chosen, self.chip + offset


def swap_partners(groups, shift):
    return [(i, i ^ shift) for i in range(groups)]


def swap_dp(part, shift):
    return lax.ppermute(part, "dp", swap_partners(lax.axis_size("dp"), shift))


def first_dp(part):
    return [swap_dp(part, 1), swap_dp(part, 2)]


def send_dp(part):
    return [swap_dp(part, shift) for shift in (1, 2, 3)]


def second_dp(pieces, axis):
    half = pieces[0].shape[axis] // 2
    return [
        swap_dp(lax.slice_in_dim(pieces[0], 0, half, axis=axis), 2),
        swap_dp(lax.slice_in_dim(pieces[1], half, 2 * half, axis=axis), 1),
    ]


def join_dp(part, pieces, axis):
    mine = lax.axis_index("dp")
    size = part.shape[axis]
    half = size // 2

    def both(shift):
        return [(mine ^ shift) * size, (mine ^ shift) * size + half]

    parts = [(part, both(0)), (pieces[0], both(1)), (pieces[1], both(2))]
    if len(pieces) == 3:
        parts.append((pieces[2], both(3)))
    else:
        parts += [(pieces[2], both(3)[:1]), (pieces[3], both(3)[1:])]
    return join(parts, axis, size * lax.axis_size("dp"), half)


def pick_dp(term, shift, axis):
    size = term.shape[axis] // lax.axis_size("dp")
    return lax.dynamic_slice_in_dim(term, (lax.axis_index("dp") ^ shift) * size, size, axis)


def scatter_one(term, shift, axis):
    return swap_dp(pick_dp(term, shift, axis), shift)


def total_dp(term, pieces, axis):
    groups = lax.axis_size("dp")
    size = term.shape[axis] // groups
    total = lax.dynamic_slice_in_dim(term, lax.axis_index("dp") * size, size, axis).astype(f32)
    for piece in pieces:
        total = total + piece.astype(f32)
    return total


def sum_small(array):
    peers = lax.axis_size("ctx")

    def swap(rows, shift):
        return lax.ppermute(rows, "ctx", [(i, i ^ shift) for i in range(peers)])

    array = array + swap(array, 1)
    return sum((swap(array, 2 * shift) for shift in range(1, peers // 2)), start=array)


def project_kernel(places, own, other, weight, gain, *rest):
    normed, raw, square = rest[-3:]

    def work(rows_ref):
        rows = rows_ref[...].astype(f32)
        hat = rows * lax.rsqrt(jnp.mean(rows * rows, axis=1, keepdims=True) + epsilon)
        low = (hat * gain[...]).astype(bf16)
        normed[...] = low
        product = jnp.dot(low, weight[...], preferred_element_type=f32)
        raw[...] = product
        third = product.shape[1] // 3
        for which in range(2):
            part = product[:, which * third : (which + 1) * third]
            square[which : which + 1, :] = jnp.sum((part * part).T, axis=0, keepdims=True)

    pl.when(pl.program_id(0) == 0)(lambda: work(own))
    pl.when(pl.program_id(0) == 1)(lambda: work(other))


def project(unit_index, own, other, weight, gain, peers, kept=()):
    rows, width = own.shape
    columns = weight.shape[1]

    def fixed(shape):
        return pl.BlockSpec(shape, lambda s, *_: (0,) * len(shape))

    return pl.pallas_call(
        project_kernel,
        grid_spec=pltpu.PrefetchScalarGridSpec(
            num_scalar_prefetch=1,
            grid=(2,),
            in_specs=[
                fixed((rows, width)),
                fixed((rows, width)),
                fixed((width, columns)),
                fixed((1, width)),
            ]
            + [pl.BlockSpec(memory_space=pl.ANY)] * len(kept),
            out_specs=[
                pl.BlockSpec((rows, width), lambda s, at: (at[s], 0)),
                pl.BlockSpec((rows, columns), lambda s, at: (at[s], 0)),
                pl.BlockSpec((None, 2, rows), lambda s, at: (at[s], 0, 0)),
            ],
        ),
        out_shape=[
            jax.ShapeDtypeStruct((peers * rows, width), bf16),
            jax.ShapeDtypeStruct((peers * rows, columns), f32),
            jax.ShapeDtypeStruct((peers, 2, rows), f32),
        ],
        input_output_aliases={5 + i: i for i in range(len(kept))},
        compiler_params=pltpu.CompilerParams(vmem_limit_bytes=56 * 2**20),
        name="project",
    )(unit_index, own, other, weight, gain, *kept)


def join_kernel(axis, blocks, block, at, *refs):
    out = refs[-1]
    turn = 0
    for ref, count in zip(refs[:-1], blocks):
        for index in range(count):
            here = (slice(None),) * axis + (slice(index * block, (index + 1) * block),)

            @pl.when(pl.program_id(0) == turn)
            def copy(ref=ref, here=here):
                out[...] = ref[here]

            turn += 1


def join(parts, axis, length, block):
    shape = list(parts[0][0].shape)
    shape[axis] = block
    blocks = [len(starts) for _, starts in parts]
    at = jnp.stack([start // block for _, starts in parts for start in starts]).astype(jnp.int32)
    rank = len(shape)

    def target(turn, at):
        return tuple(at[turn] if index == axis else 0 for index in range(rank))

    def fixed(part):
        return pl.BlockSpec(
            part.shape, lambda turn, at: (0,) * rank, pipeline_mode=pl.Buffered(1)
        )

    return pl.pallas_call(
        functools.partial(join_kernel, axis, blocks, block),
        grid_spec=pltpu.PrefetchScalarGridSpec(
            num_scalar_prefetch=1,
            grid=(sum(blocks),),
            in_specs=[fixed(part) for part, _ in parts],
            out_specs=pl.BlockSpec(tuple(shape), target),
        ),
        out_shape=jax.ShapeDtypeStruct(
            tuple(length if index == axis else size for index, size in enumerate(shape)),
            parts[0][0].dtype,
        ),
        compiler_params=pltpu.CompilerParams(vmem_limit_bytes=40 * 2**20),
        name="join",
    )(at, *[part for part, _ in parts])


def lay_kernel(at, own, other, *rest):
    out = rest[-1]

    def work(source):
        out[...] = source[...].astype(f32)

    pl.when(pl.program_id(0) == 0)(lambda: work(own))
    pl.when(pl.program_id(0) == 1)(lambda: work(other))


def lay(at, own, other, out_shape, pieces, index, kept=()):
    rows, columns = own.shape
    block = (rows, columns // pieces)
    return pl.pallas_call(
        lay_kernel,
        grid_spec=pltpu.PrefetchScalarGridSpec(
            num_scalar_prefetch=1,
            grid=(2, pieces),
            in_specs=[pl.BlockSpec(block, lambda s, t, at: (0, t))] * 2
            + [pl.BlockSpec(memory_space=pl.ANY)] * len(kept),
            out_specs=pl.BlockSpec(block, lambda s, t, at: index(at[s], t)),
        ),
        out_shape=jax.ShapeDtypeStruct(out_shape, f32),
        input_output_aliases={3: 0} if kept else {},
        name="lay",
    )(at, own, other, *kept)


def expert_kernel(
    unit, own, other, cots, slots, gates, columns, w_gate, w_up, w_down, *rest
):
    expert_in, grad_rows, hidden, grad_gate, grad_up, part, total, ready = rest[-8:]
    expert, piece = pl.program_id(0), pl.program_id(1)
    last_expert = expert == pl.num_programs(0) - 1
    last_piece = piece == pl.num_programs(1) - 1
    room, width = expert_in.shape[1:]
    rows = own.shape[0]
    core = unit[1]

    @pl.when(piece == 0)
    def bring():
        at = lax.broadcasted_iota(jnp.int32, (room, rows), 0)
        for s in range(2):
            found = at == slots[s, pl.ds(expert, 1), :]
            picks = jnp.where(found, 1.0, 0.0).astype(bf16)
            slot_gate = jnp.sum(
                jnp.where(found, gates[s, pl.ds(expert, 1), :], 0.0), axis=1, keepdims=True
            )
            grad_rows[s] = (
                jnp.dot(picks, cots[s], preferred_element_type=f32) * slot_gate
            ).astype(bf16)

            @pl.when(core == s)
            def from_own():
                expert_in[s] = jnp.dot(picks, own[...], preferred_element_type=f32).astype(bf16)

            @pl.when(core != s)
            def from_other():
                expert_in[s] = jnp.dot(picks, other[...], preferred_element_type=f32).astype(bf16)

    rows_in = expert_in[...].reshape(2 * room, width)
    gate_pre = jnp.dot(rows_in, w_gate[...], preferred_element_type=f32)
    up_pre = jnp.dot(rows_in, w_up[...], preferred_element_type=f32)
    grad_hidden = lax.dot_general(
        grad_rows[...].reshape(2 * room, width), w_down[...], NT, preferred_element_type=f32
    )
    sigmoid = 1.0 / (1.0 + jnp.exp(-gate_pre))
    silu = gate_pre * sigmoid
    hidden[...] = (silu * up_pre).astype(bf16).reshape(hidden.shape)
    gate_here = (grad_hidden * up_pre * sigmoid * (1.0 + gate_pre * (1.0 - sigmoid))).astype(bf16)
    up_here = (grad_hidden * silu).astype(bf16)
    grad_gate[...] = gate_here.reshape(grad_gate.shape)
    grad_up[...] = up_here.reshape(grad_up.shape)

    def back():
        return lax.dot_general(gate_here, w_gate[...], NT, preferred_element_type=f32) + lax.dot_general(
            up_here, w_up[...], NT, preferred_element_type=f32
        )

    @pl.when(piece == 0)
    def first():
        total[...] = back()

    @pl.when(piece != 0)
    def later():
        total[...] += back()

    @pl.when(last_piece)
    def keep():
        for s in range(2):
            ready[s, pl.ds(pl.multiple_of(expert * room, 16), room), :] = total[
                s * room : (s + 1) * room, :
            ].astype(bf16)

    @pl.when(last_piece & last_expert)
    def send():
        for s in range(2):
            at = lax.broadcasted_iota(jnp.int32, (rows, ready.shape[1]), 1)
            here = columns[s]
            found = at == here[:, 0:1]
            for e in range(1, here.shape[1]):
                found = found | (at == here[:, e : e + 1])
            part[s] = jnp.dot(
                jnp.where(found, 1.0, 0.0).astype(bf16), ready[s], preferred_element_type=f32
            ).astype(bf16)


def expert_unit(unit, own, other, cot_all, slots, gates, columns, w_gate, w_up, w_down, room, kept=(), piece=256):
    rows, width = own.shape
    experts, _, inner = w_gate.shape
    peers = cot_all.shape[0]
    wide_shape = (peers, experts, room, width)
    thin_shape = (peers, experts, room, inner)
    anywhere = pl.BlockSpec(memory_space=pl.ANY)
    once = pl.Buffered(1)

    def fixed(shape):
        return pl.BlockSpec(shape, lambda e, f, u: (0,) * len(shape), pipeline_mode=once)

    def chip(shape):
        return pl.BlockSpec((2, *shape), lambda e, f, u: (u[0], 0, 0), pipeline_mode=once)

    wide = pl.BlockSpec((2, None, room, width), lambda e, f, u: (u[0], e, 0, 0))
    thin = pl.BlockSpec((2, None, room, piece), lambda e, f, u: (u[0], e, 0, f))
    return pl.pallas_call(
        expert_kernel,
        grid_spec=pltpu.PrefetchScalarGridSpec(
            num_scalar_prefetch=1,
            grid=(experts, inner // piece),
            in_specs=[
                fixed((rows, width)), fixed((rows, width)), chip((rows, width)),
                chip((experts, rows)), chip((experts, rows)), chip((rows, experts)),
                pl.BlockSpec((None, width, piece), lambda e, f, u: (e, 0, f)),
                pl.BlockSpec((None, width, piece), lambda e, f, u: (e, 0, f)),
                pl.BlockSpec((None, piece, width), lambda e, f, u: (e, f, 0)),
            ] + [anywhere] * len(kept),
            out_specs=[wide, wide, thin, thin, thin,
                pl.BlockSpec((2, rows, width), lambda e, f, u: (u[0], 0, 0))],
            scratch_shapes=[
                pltpu.VMEM((2 * room, width), f32),
                pltpu.VMEM((2, experts * room, width), bf16),
            ],
        ),
        out_shape=[
            jax.ShapeDtypeStruct(shape, bf16)
            for shape in [wide_shape] * 2 + [thin_shape] * 3 + [cot_all.shape]
        ],
        input_output_aliases={10 + i: i for i in range(len(kept))},
        compiler_params=pltpu.CompilerParams(vmem_limit_bytes=60 * 2**20),
        name="expert_unit",
    )(unit, own, other, cot_all, slots, gates, columns, w_gate, w_up, w_down, *kept)


def out_kernel(hidden, w_down, slots, gates, columns, part, ready):
    expert = pl.program_id(1)
    room = hidden.shape[1]
    rows = slots.shape[2]
    at = lax.broadcasted_iota(jnp.int32, (room, rows), 0)
    product = jnp.dot(
        hidden[...].reshape(2 * room, hidden.shape[2]), w_down[...], preferred_element_type=f32
    )
    for s in range(2):
        found = at == slots[s, pl.ds(expert, 1), :]
        slot_gate = jnp.sum(jnp.where(found, gates[s, pl.ds(expert, 1), :], 0.0), axis=1, keepdims=True)
        ready[s, pl.ds(pl.multiple_of(expert * room, 16), room), :] = (
            product[s * room : (s + 1) * room] * slot_gate
        ).astype(bf16)

    @pl.when(expert == pl.num_programs(1) - 1)
    def send():
        for s in range(2):
            at = lax.broadcasted_iota(jnp.int32, (rows, ready.shape[1]), 1)
            here = columns[s]
            found = at == here[:, 0:1]
            for e in range(1, here.shape[1]):
                found = found | (at == here[:, e : e + 1])
            part[s] = jnp.dot(
                jnp.where(found, 1.0, 0.0).astype(bf16), ready[s], preferred_element_type=f32
            ).astype(bf16)


def expert_out(hidden, w_down, slots, gates, columns):
    peers, experts, room, inner = hidden.shape
    width = w_down.shape[2]
    rows = slots.shape[2]
    return pl.pallas_call(
        out_kernel,
        grid=(peers // 2, experts),
        in_specs=[
            pl.BlockSpec((2, None, room, inner), lambda c, e: (c, e, 0, 0)),
            pl.BlockSpec((None, inner, width), lambda c, e: (e, 0, 0)),
            pl.BlockSpec((2, experts, rows), lambda c, e: (c, 0, 0)),
            pl.BlockSpec((2, experts, rows), lambda c, e: (c, 0, 0)),
            pl.BlockSpec((2, rows, experts), lambda c, e: (c, 0, 0)),
        ],
        out_specs=pl.BlockSpec((2, rows, width), lambda c, e: (c, 0, 0)),
        out_shape=jax.ShapeDtypeStruct((peers, rows, width), bf16),
        scratch_shapes=[pltpu.VMEM((2, experts * room, width), bf16)],
        compiler_params=pltpu.CompilerParams(vmem_limit_bytes=60 * 2**20),
        name="expert_out",
    )(hidden, w_down, slots, gates, columns)


def on_device(
    tokens,
    cotangent,
    wqkv,
    wo,
    attn_gain,
    query_gain,
    key_gain,
    moe_gain,
    w_gate,
    w_up,
    w_down,
    expert_ids,
    gates,
    slot_order,
    block_assign,
    segment_ids,
):
    count_rows, width = tokens.shape
    head_dim = width // HEADS
    scale = head_dim ** (-0.5)
    peers = lax.axis_size("ctx")
    groups = lax.axis_size("dp")
    me = lax.axis_index("ctx")
    core = me % 2
    my_dp = lax.axis_index("dp")
    group_rows = count_rows * peers
    rep = max(1, peers // HEADS)
    own_heads = max(1, HEADS // peers)
    own_width = own_heads * head_dim
    first_head = (me // rep) * own_heads
    block_len = count_rows // BLK_DEV
    tile = 512
    line = Line()
    turns = range(1, line.chips)

    assign = block_assign[0]
    count_blocks = assign.shape[0]
    place = jnp.argmax(
        assign[None, :] == jnp.arange(count_blocks, dtype=jnp.int32)[:, None], axis=1
    ).astype(jnp.int32)
    cont = segment_ids[0]
    prompt_len = group_rows - cont.shape[0]
    prompt_tiles = prompt_len // tile
    seg_logical = jnp.concatenate([jnp.full((prompt_len,), -1, jnp.int32), cont])
    tiles = group_rows // tile
    tile_seg = seg_logical.reshape(tiles, tile)[:, 0]
    first_tile = jnp.where(
        tile_seg < 0,
        jnp.arange(tiles, dtype=jnp.int32),
        jnp.sum((seg_logical[None, :] < tile_seg[:, None]).astype(jnp.int32), axis=1) // tile,
    ).astype(jnp.int32)
    seg_col = seg_logical[:, None]
    seg_row = seg_logical.reshape(tiles, tile)

    local_experts = w_gate.shape[0]
    count_experts = local_experts * peers
    capacity = 9 * count_rows * TOP // (8 * count_experts)
    room = (capacity + 15) // 16 * 16
    slot, gate = slot_table(expert_ids, slot_order, gates, count_experts, capacity)
    table = jnp.stack(
        [
            slot.reshape(peers, local_experts, count_rows).astype(f32),
            gate.reshape(peers, local_experts, count_rows),
        ],
        axis=1,
    )

    inputs = tokens.astype(f32)
    below, above = line.step(1, tokens, tokens)
    other = line.other(tokens)
    w_part = jnp.concatenate(
        [
            lax.dynamic_slice_in_dim(wqkv, which * width + first_head * head_dim, own_width, 1)
            for which in range(3)
        ],
        axis=1,
    )
    w_pieces = send_dp(w_part)
    gain_part = jnp.stack([attn_gain, query_gain, key_gain, moe_gain])
    gain_all = jnp.zeros((4, width), bf16)
    for shift in range(groups):
        piece = swap_dp(gain_part, shift) if shift else gain_part
        gain_all = lax.dynamic_update_slice_in_dim(
            gain_all, piece, (my_dp ^ shift) * gain_part.shape[1], 1
        )
    gain_all = gain_all.astype(f32)
    below, above, other, gain_all, table, wo, w_gate, *w_pieces = barrier(
        below, above, other, gain_all, table, wo, w_gate, *w_pieces
    )
    full_gate = lax.all_gather(w_gate, "dp", axis=1, tiled=True)
    w_own = join_dp(w_part, w_pieces, 0)
    gain_attn, gain_moe = gain_all[0:1], gain_all[3:4]
    gain_own = lax.dynamic_slice_in_dim(gain_all, first_head * head_dim, own_width, 1)
    gain_q, gain_k = gain_own[1:2], gain_own[2:3]

    half_rows = wo.shape[0] // 2
    arrived = {-1: below, 1: above}
    own, chip = tokens, line.chip
    kept, travelled = (), ()
    for turn in turns:
        if turn + 1 < line.chips:
            below, above = line.step(turn + 1, below, above)
            arrived[-turn - 1], arrived[turn + 1] = below, above
        next_own, next_chip = line.take(turn, arrived)
        next_other = line.other(next_own)
        at = jnp.stack([2 * chip + core, 2 * chip + 1 - core]).astype(jnp.int32)
        kept = project(at, own, other, w_own, gain_attn, peers, kept)
        travel = list(travelled)
        if turn == 1:
            wo_half = lax.dynamic_slice_in_dim(wo, core * half_rows, half_rows, 0)
            travel = first_dp(wo_half)
        if turn == 2:
            travel.append(swap_dp(wo_half, 3))
        own, other, chip = next_own, next_other, next_chip
        square = kept[2]
        below, above, own, other, square, w_down, *travelled = barrier(
            below, above, own, other, square, w_down, *travel
        )
        kept = (kept[0], kept[1], square)
        if turn + 1 < line.chips:
            arrived[-turn - 1], arrived[turn + 1] = below, above
    cotangent_now, other = barrier(cotangent, other)
    cot_all = lax.all_gather(cotangent_now, "ctx", axis=0, tiled=True).reshape(
        peers, count_rows, width
    )
    down_pieces = first_dp(w_down)
    wo_mine = jnp.concatenate([wo_half, *travelled[:3]], axis=0)
    wo_theirs = line.other(wo_mine)
    table = lax.all_to_all(table, "ctx", split_axis=0, concat_axis=0, tiled=True)
    at = jnp.stack([2 * chip + core, 2 * chip + 1 - core]).astype(jnp.int32)
    normed_all, raw, square = project(at, own, other, w_own, gain_attn, peers, kept)
    square = sum_small(square.transpose(1, 0, 2).reshape(2, group_rows)) * (1.0 / rep)
    inv_qk = lax.rsqrt(square / width + epsilon).T
    slot = table[:, 0].astype(jnp.int32)
    gate_rows = table[:, 1]
    offsets = (jnp.arange(local_experts, dtype=jnp.int32) * room)[None, :, None]
    columns = jnp.where(slot >= 0, slot + offsets, -1).transpose(0, 2, 1)

    inv_qk, w_up, slot, gate_rows, columns, full_gate, wo_mine, wo_theirs, *down_pieces = barrier(
        inv_qk, w_up, slot, gate_rows, columns, full_gate, wo_mine, wo_theirs, *down_pieces
    )
    down_pieces = down_pieces + second_dp(down_pieces, 1)
    up_pieces = first_dp(w_up)
    attended, lse, queries, keys, values = attention_forward(
        raw,
        inv_qk,
        gain_q,
        gain_k,
        seg_col,
        seg_row,
        place,
        first_tile,
        tile,
        prompt_tiles,
        block_len,
        scale,
    )
    attended, *pieces = barrier(attended, *up_pieces, *down_pieces)
    up_pieces, down_pieces = pieces[:2], pieces[2:]
    up_pieces = up_pieces + second_dp(up_pieces, 1)
    attn_low = lax.all_to_all(
        attended.reshape(peers, count_rows, own_width), "ctx", split_axis=0, concat_axis=0, tiled=True
    )[::rep]
    full_down = join_dp(w_down, down_pieces, 1)
    starts = [(my_dp ^ shift) * wo.shape[0] for shift in range(groups)]
    full_wo = join(
        [
            (wo_mine, [start + core * half_rows for start in starts]),
            (wo_theirs, [start + (1 - core) * half_rows for start in starts]),
        ],
        0,
        width,
        half_rows,
    )
    full_up = join_dp(w_up, up_pieces, 1)
    attn_low, full_wo, full_down, full_up = barrier(attn_low, full_wo, full_down, full_up)
    attn_low = attn_low.transpose(1, 0, 2).reshape(count_rows, width)
    state = inputs + jnp.dot(attn_low, full_wo, preferred_element_type=f32)
    inv_state = rms_scale(state)
    hat_state = state * inv_state
    normed_moe = (hat_state * gain_moe).astype(bf16)

    normed_moe, cot_all = barrier(normed_moe, cot_all)
    below, above = normed_moe, normed_moe
    own, chip = normed_moe, line.chip
    arrived = {}
    kept = ()
    for turn in range(line.chips):
        if turn + 1 < line.chips:
            below, above = line.step(turn + 1, below, above)
            arrived[-turn - 1], arrived[turn + 1] = below, above
        if turn > 0:
            own, chip = line.take(turn, arrived)
        other = line.other(own)
        kept = expert_unit(
            jnp.stack([chip, core]).astype(jnp.int32),
            own,
            other,
            cot_all,
            slot,
            gate_rows,
            columns,
            full_gate,
            full_up,
            full_down,
            room,
            kept,
        )
        if turn + 1 < line.chips:
            below, above, *kept = barrier(below, above, *kept)
            arrived[-turn - 1], arrived[turn + 1] = below, above
    expert_in, grad_rows, hidden, grad_gate_pre, grad_up_pre, part_moe = kept
    grad_normed_moe = lax.psum_scatter(
        part_moe.reshape(group_rows, width), "ctx", scatter_dimension=0, tiled=True
    )

    part_mixed = expert_out(hidden, full_down, slot, gate_rows, columns)
    grad_down = jnp.einsum("sncf,sncd->nfd", hidden, grad_rows, preferred_element_type=f32)
    grad_down = grad_down.astype(bf16)
    part_mixed, grad_down, expert_in = barrier(part_mixed, grad_down, expert_in)
    down_pieces = [scatter_one(grad_down, shift, 1) for shift in (1, 2, 3)]
    grad_gate = jnp.einsum("sncd,sncf->ndf", expert_in, grad_gate_pre, preferred_element_type=f32)
    grad_up = jnp.einsum("sncd,sncf->ndf", expert_in, grad_up_pre, preferred_element_type=f32)
    grad_gate, grad_up = grad_gate.astype(bf16), grad_up.astype(bf16)
    grad_normed_moe, part_mixed, grad_gate, grad_up, *down_pieces = barrier(
        grad_normed_moe, part_mixed, grad_gate, grad_up, *down_pieces
    )
    mixed = lax.psum_scatter(
        part_mixed.reshape(group_rows, width), "ctx", scatter_dimension=0, tiled=True
    )

    gate_pieces = [scatter_one(grad_gate, shift, 1) for shift in (1, 2)]
    grad_normed_moe = grad_normed_moe.astype(f32)
    moe_gain_term = jnp.sum(grad_normed_moe * hat_state, axis=0)
    grad_state = cotangent.astype(f32) + rms_back(grad_normed_moe * gain_moe, hat_state, inv_state)
    grad_branch = grad_state.astype(bf16)
    grad_attn = lax.dot_general(grad_branch, full_wo, NT, preferred_element_type=f32).astype(bf16)
    grad_attn = grad_attn.reshape(count_rows, peers // rep, own_width).transpose(1, 0, 2)
    grad_attn = jnp.repeat(grad_attn, rep, axis=0)
    grad_attended = lax.all_to_all(
        grad_attn, "ctx", split_axis=0, concat_axis=0, tiled=True
    ).reshape(group_rows, own_width)
    part_out = lax.dot_general(
        attn_low, tied(grad_branch, grad_attn), TN, preferred_element_type=f32
    ).astype(bf16)
    part_out = part_out.reshape(groups, 2, half_rows, width)
    out_theirs = line.other(lax.dynamic_index_in_dim(part_out, 1 - core, 1, keepdims=False))
    part_out = lax.dynamic_index_in_dim(part_out, core, 1, keepdims=False).astype(f32)
    part_out = (part_out + out_theirs.astype(f32)).astype(bf16)
    down_sum = total_dp(grad_down, down_pieces, 1)
    grad_attended, part_out, down_sum, *gate_pieces = barrier(
        grad_attended, part_out, down_sum, *gate_pieces
    )
    gate_pieces.append(scatter_one(grad_gate, 3, 1))
    out_pieces = [scatter_one(part_out, shift, 0) for shift in (1, 2)]
    grad_q, grad_k, grad_v = attention_backward(
        queries,
        keys,
        values,
        lse,
        attended,
        grad_attended,
        seg_col,
        seg_row,
        place,
        first_tile,
        tile,
        prompt_tiles,
        block_len,
        scale,
    )
    grad_q, gate_last, grad_up, *out_pieces = barrier(grad_q, gate_pieces[2], grad_up, *out_pieces)
    gate_pieces[2] = gate_last
    out_pieces.append(scatter_one(part_out, 3, 0))
    hat_q = raw[:, :own_width] * inv_qk[:, 0:1]
    hat_k = raw[:, own_width : 2 * own_width] * inv_qk[:, 1:2]
    query_gain_term = jnp.sum(grad_q * hat_q, axis=0)
    key_gain_term = jnp.sum(grad_k * hat_k, axis=0)
    means = jnp.stack(
        [
            jnp.sum(grad_q * gain_q * hat_q, axis=1),
            jnp.sum(grad_k * gain_k * hat_k, axis=1),
        ]
    )
    means = (sum_small(means) * (1.0 / (rep * width))).T
    grad_raw_q = inv_qk[:, 0:1] * (grad_q * gain_q - hat_q * means[:, 0:1])
    grad_raw_k = inv_qk[:, 1:2] * (grad_k * gain_k - hat_k * means[:, 1:2])
    grad_qkv = jnp.concatenate([grad_raw_q.astype(bf16), grad_raw_k.astype(bf16), grad_v], axis=1)
    part_normed = lax.dot_general(grad_qkv, w_own, NT, preferred_element_type=f32) * (1.0 / rep)
    part_normed = part_normed.astype(bf16)
    part_normed, grad_qkv, mixed, grad_up, *out_pieces = barrier(
        part_normed, grad_qkv, mixed, grad_up, *out_pieces
    )
    grad_normed = lax.psum_scatter(part_normed, "ctx", scatter_dimension=0, tiled=True)

    out_sum = total_dp(part_out, out_pieces, 0).astype(bf16).reshape(half_rows, width)
    out_share = half_rows // (peers // 2)
    out_sum = lax.all_to_all(
        out_sum.reshape(peers // 2, out_share, width),
        "ctx",
        split_axis=0,
        concat_axis=0,
        tiled=True,
        axis_index_groups=[[2 * z + c for z in range(peers // 2)] for c in range(2)],
    )
    part_qkv = lax.dot_general(normed_all, grad_qkv, TN, preferred_element_type=f32).astype(bf16)
    qkv_pieces = [scatter_one(part_qkv, shift, 0) for shift in (1, 2, 3)]
    gate_sum = total_dp(grad_gate, gate_pieces, 1)
    own_terms = jnp.stack([query_gain_term, key_gain_term]) * (1.0 / rep)
    spread = lax.dynamic_update_slice_in_dim(
        jnp.zeros((2, width), f32), own_terms, first_head * head_dim, 1
    )
    attn_gain_term = (
        jnp.sum(part_normed.astype(f32) * normed_all.astype(f32), axis=0) / gain_attn[0]
    )
    gain_terms = jnp.concatenate([attn_gain_term[None], spread, moe_gain_term[None]], axis=0)
    gate_sum, out_sum, gain_terms, grad_up, *qkv_pieces = barrier(
        gate_sum, out_sum, gain_terms, grad_up, *qkv_pieces
    )
    up_pieces = [scatter_one(grad_up, shift, 1) for shift in (1, 2)]
    gain_terms = sum_small(gain_terms)
    gain_terms = total_dp(gain_terms, [scatter_one(gain_terms, shift, 1) for shift in (1, 2, 3)], 1)
    qkv_sum = total_dp(part_qkv, qkv_pieces, 0).astype(bf16)
    out_sum = jnp.sum(out_sum.astype(f32), axis=0).astype(bf16)
    rows_dp = qkv_sum.shape[0]
    own, chip = [qkv_sum, out_sum], line.chip
    below, above = own, own
    arrived = {}
    qkv_kept, out_kept = (), ()
    for turn in range(line.chips):
        if turn > 0:
            own, chips = zip(*[line.take(turn, {d: a[i] for d, a in arrived.items()}) for i in (0, 1)])
            chip = chips[0]
        if turn + 1 < line.chips:
            steps = [line.step(turn + 1, b, a) for b, a in zip(below, above)]
            below, above = [s[0] for s in steps], [s[1] for s in steps]
        other = [line.other(part) for part in own]
        at = jnp.stack([2 * chip + core, 2 * chip + 1 - core]).astype(jnp.int32) // rep
        qkv_kept = [
            lay(
                at,
                own[0],
                other[0],
                (rows_dp, 3 * width),
                3,
                lambda p, t: (0, t * (peers // rep) + p),
                qkv_kept,
            )
        ]
        at = jnp.stack([core * line.chips + chip, (1 - core) * line.chips + chip]).astype(jnp.int32)
        out_kept = [
            lay(at, own[1], other[1], (rows_dp, width), 1, lambda p, t: (p, 0), out_kept)
        ]
        if turn + 1 < line.chips:
            *both, qkv_kept[0], out_kept[0], grad_up = barrier(
                *below, *above, qkv_kept[0], out_kept[0], grad_up, *up_pieces
            )[: len(below) + len(above) + 3]
            below, above = both[:2], both[2:]
            if turn == 0:
                up_pieces.append(scatter_one(grad_up, 3, 1))
            arrived[-turn - 1], arrived[turn + 1] = below, above
    qkv_total, out_total = qkv_kept[0], out_kept[0]
    up_sum = total_dp(grad_up, up_pieces, 1)
    output = (state + mixed.astype(f32)).astype(bf16)
    out_total, qkv_total, up_sum, output, gain_terms, grad_normed = barrier(
        out_total, qkv_total, up_sum, output, gain_terms, grad_normed
    )

    grad_normed = grad_normed.astype(f32)
    inv_in = rms_scale(inputs)
    hat_in = inputs * inv_in
    input_grad = (grad_state + rms_back(grad_normed * gain_attn, hat_in, inv_in)).astype(bf16)
    return (
        output,
        input_grad,
        qkv_total,
        out_total,
        gain_terms[0],
        gain_terms[1],
        gain_terms[2],
        gain_terms[3],
        gate_sum,
        up_sum,
        down_sum,
    )


def solution(mesh):
    rows = P(("dp", "ctx"), None)
    expert = P("ctx", "dp", None)
    by_dp = P("dp", None)
    return jax.shard_map(
        on_device,
        mesh=mesh,
        in_specs=(
            rows,
            rows,
            by_dp,
            by_dp,
            P("dp"),
            P("dp"),
            P("dp"),
            P("dp"),
            expert,
            expert,
            expert,
            rows,
            rows,
            rows,
            by_dp,
            by_dp,
        ),
        out_specs=(
            rows,
            rows,
            by_dp,
            by_dp,
            P("dp"),
            P("dp"),
            P("dp"),
            P("dp"),
            expert,
            expert,
            expert,
        ),
        check_vma=False,
    )
```

```python
import functools

import jax
import jax.numpy as jnp
from jax import lax
from jax.experimental import pallas as pl
from jax.experimental.pallas import tpu as pltpu
from jax.sharding import PartitionSpec as P

HEADS = 16
TOP = 8
BLK_DEV = 2
LOG2E = 1.4426950408889634
HEAD_DIM = 128

epsilon = 1e-06
masked_value = -1e30
f32 = jnp.float32
bf16 = jnp.bfloat16
NT = (((1,), (1,)), ((), ()))
TN = (((0,), (0,)), ((), ()))


def rms_scale(values_in):
    return lax.rsqrt(jnp.mean(values_in * values_in, axis=-1, keepdims=True) + epsilon)


def rms_back(grad_hat, normed, scale_rows):
    return scale_rows * (grad_hat - normed * jnp.mean(grad_hat * normed, axis=-1, keepdims=True))


def tile_mask(seg_col, seg_row, key_first, query_first):
    rows, columns = seg_col.shape[0], seg_row.shape[1]
    key_pos = key_first + lax.broadcasted_iota(jnp.int32, (rows, columns), 0)
    query_pos = query_first + lax.broadcasted_iota(jnp.int32, (rows, columns), 1)
    return (seg_col == seg_row) & (key_pos <= query_pos)


def forward_kernel(
    tile,
    prompt_tiles,
    block_len,
    scale,
    place,
    first_tile,
    raw_q,
    raw_k,
    raw_v,
    inv,
    gain_q,
    gain_k,
    seg_col,
    seg_row,
    out,
    lse,
    queries,
    keys,
    values,
    values_t,
    out_logical,
):
    group, width = raw_q.shape
    tiles = group // tile
    blocks = group // block_len
    columns = [slice(first, first + HEAD_DIM) for first in range(0, width, HEAD_DIM)]

    def bring(block, carry):
        source = pl.ds(pl.multiple_of(place[block] * block_len, block_len), block_len)
        target = pl.ds(pl.multiple_of(block * block_len, block_len), block_len)
        scales = inv[source, :]
        queries[target, :] = (raw_q[source, :] * scales[:, 0:1] * gain_q[...]).astype(bf16)
        keys[target, :] = (raw_k[source, :] * scales[:, 1:2] * gain_k[...]).astype(bf16)
        values[target, :] = raw_v[source, :].astype(bf16)
        return carry

    lax.fori_loop(0, blocks, bring, 0)
    for index in range(tiles):
        values_t[:, index * tile : (index + 1) * tile] = values[
            index * tile : (index + 1) * tile, :
        ].T

    def query_tile(index, carry):
        first = pl.multiple_of(index * tile, tile)
        here = pl.ds(first, tile)
        seg_query = seg_row[pl.ds(index, 1), :]

        def step(is_masked, at, states):
            key_first = pl.multiple_of(at * tile, tile)
            there = pl.ds(key_first, tile)
            if is_masked:
                allowed = tile_mask(seg_col[there, :], seg_query, key_first, first)
            every = [
                lax.dot_general(
                    keys[there, head], queries[here, head], NT, preferred_element_type=f32
                )
                for head in columns
            ]
            after = []
            for scores, head, (largest, total, running) in zip(every, columns, states):
                scores = scores * (scale * LOG2E)
                if is_masked:
                    scores = jnp.where(allowed, scores, masked_value)
                new_largest = jnp.maximum(largest, jnp.max(scores, axis=0, keepdims=True))
                shrink = jnp.exp2(largest - new_largest)
                terms = jnp.exp2(scores - new_largest)
                total = total * shrink + jnp.sum(terms, axis=0, keepdims=True)
                running = running * shrink + jnp.dot(
                    values_t[head, there], terms.astype(bf16), preferred_element_type=f32
                )
                after.append((new_largest, total, running))
            return after

        states = [
            (
                jnp.full((1, tile), masked_value, f32),
                jnp.zeros((1, tile), f32),
                jnp.zeros((HEAD_DIM, tile), f32),
            )
            for _ in columns
        ]
        states = lax.fori_loop(
            0, jnp.minimum(index, prompt_tiles), functools.partial(step, False), states
        )
        states = lax.fori_loop(first_tile[index], index + 1, functools.partial(step, True), states)
        for which, (head, (largest, total, running)) in enumerate(zip(columns, states)):
            lse[which, pl.ds(index, 1), :] = largest + jnp.log2(total)
            out_logical[here, head] = (running / total).T.astype(bf16)
        return carry

    lax.fori_loop(0, tiles, query_tile, 0)

    def send(block, carry):
        target = pl.ds(pl.multiple_of(place[block] * block_len, block_len), block_len)
        source = pl.ds(pl.multiple_of(block * block_len, block_len), block_len)
        out[target, :] = out_logical[source, :]
        return carry

    lax.fori_loop(0, blocks, send, 0)


def backward_kernel(
    tile,
    prompt_tiles,
    block_len,
    scale,
    place,
    first_tile,
    queries,
    keys,
    values,
    lse,
    out,
    grad_out,
    seg_col,
    seg_row,
    grad_q,
    grad_k,
    grad_v,
    keys_t,
    grad_here,
    delta,
    total_q,
    total_k,
    total_v,
):
    group, width = queries.shape
    tiles = group // tile
    blocks = group // block_len
    columns = [slice(first, first + HEAD_DIM) for first in range(0, width, HEAD_DIM)]

    def bring(block, carry):
        source = pl.ds(pl.multiple_of(place[block] * block_len, block_len), block_len)
        target = pl.ds(pl.multiple_of(block * block_len, block_len), block_len)
        grad_here[target, :] = grad_out[source, :]
        total_q[target, :] = out[source, :].astype(f32) * grad_out[source, :].astype(f32)
        return carry

    lax.fori_loop(0, blocks, bring, 0)
    for index in range(tiles):
        rows = slice(index * tile, (index + 1) * tile)
        keys_t[:, rows] = keys[rows, :].T
        for which, head in enumerate(columns):
            delta[which, index : index + 1, :] = jnp.sum(
                total_q[rows, head].T, axis=0, keepdims=True
            )
    total_k[...] = jnp.zeros_like(total_k)
    total_v[...] = jnp.zeros_like(total_v)

    def query_tile(index, carry):
        first = pl.multiple_of(index * tile, tile)
        here = pl.ds(first, tile)
        seg_query = seg_row[pl.ds(index, 1), :]

        def step(is_masked, at, states):
            key_first = pl.multiple_of(at * tile, tile)
            there = pl.ds(key_first, tile)
            if is_masked:
                allowed = tile_mask(seg_col[there, :], seg_query, key_first, first)
            every = [
                (
                    lax.dot_general(
                        keys[there, head], queries[here, head], NT, preferred_element_type=f32
                    ),
                    lax.dot_general(
                        values[there, head], grad_here[here, head], NT, preferred_element_type=f32
                    ),
                )
                for head in columns
            ]
            after = []
            for which, (head, running) in enumerate(zip(columns, states)):
                scores, dprobs = every[which]
                probs = jnp.exp2(scores * (scale * LOG2E) - lse[which, pl.ds(index, 1), :])
                if is_masked:
                    probs = jnp.where(allowed, probs, 0.0)
                dscores = (probs * (dprobs - delta[which, pl.ds(index, 1), :])).astype(bf16)
                total_v[there, head] += jnp.dot(
                    probs.astype(bf16), grad_here[here, head], preferred_element_type=f32
                )
                total_k[there, head] += jnp.dot(
                    dscores, queries[here, head], preferred_element_type=f32
                )
                after.append(
                    running + jnp.dot(keys_t[head, there], dscores, preferred_element_type=f32)
                )
            return after

        states = [jnp.zeros((HEAD_DIM, tile), f32) for _ in columns]
        states = lax.fori_loop(
            0, jnp.minimum(index, prompt_tiles), functools.partial(step, False), states
        )
        states = lax.fori_loop(first_tile[index], index + 1, functools.partial(step, True), states)
        for head, running in zip(columns, states):
            total_q[here, head] = running.T
        return carry

    lax.fori_loop(0, tiles, query_tile, 0)

    def send(block, carry):
        target = pl.ds(pl.multiple_of(place[block] * block_len, block_len), block_len)
        source = pl.ds(pl.multiple_of(block * block_len, block_len), block_len)
        grad_q[target, :] = total_q[source, :] * scale
        grad_k[target, :] = total_k[source, :] * scale
        grad_v[target, :] = total_v[source, :].astype(bf16)
        return carry

    lax.fori_loop(0, blocks, send, 0)


def attention_forward(
    raw, inv, gain_q, gain_k, seg_col, seg_row, place, first_tile, tile, prompt_tiles, block_len, scale
):
    group, width = raw.shape[0], raw.shape[1] // 3
    heads = width // HEAD_DIM
    tiles = group // tile

    def part(which):
        return pl.BlockSpec((group, width), lambda i, *_: (0, which), pipeline_mode=pl.Buffered(1))

    def whole(shape):
        return pl.BlockSpec(
            shape, lambda i, *_: (0,) * len(shape), pipeline_mode=pl.Buffered(1)
        )

    head = whole((group, width))
    return pl.pallas_call(
        functools.partial(forward_kernel, tile, prompt_tiles, block_len, scale),
        grid_spec=pltpu.PrefetchScalarGridSpec(
            num_scalar_prefetch=2,
            grid=(1,),
            in_specs=[
                part(0),
                part(1),
                part(2),
                whole((group, 2)),
                whole((1, width)),
                whole((1, width)),
                whole((group, 1)),
                whole((tiles, tile)),
            ],
            out_specs=[head, whole((heads, tiles, tile)), head, head, head],
            scratch_shapes=[
                pltpu.VMEM((width, group), bf16),
                pltpu.VMEM((group, width), bf16),
            ],
        ),
        out_shape=[
            jax.ShapeDtypeStruct((group, width), bf16),
            jax.ShapeDtypeStruct((heads, tiles, tile), f32),
            jax.ShapeDtypeStruct((group, width), bf16),
            jax.ShapeDtypeStruct((group, width), bf16),
            jax.ShapeDtypeStruct((group, width), bf16),
        ],
        compiler_params=pltpu.CompilerParams(vmem_limit_bytes=60 * 2**20),
        cost_estimate=pl.CostEstimate(
            flops=4 * group * group * width, bytes_accessed=24 * group * width, transcendentals=0
        ),
        name="attention_forward",
    )(place, first_tile, raw, raw, raw, inv, gain_q, gain_k, seg_col, seg_row)


def attention_backward(
    queries, keys, values, lse, out, grad_out, seg_col, seg_row, place, first_tile, tile, prompt_tiles, block_len, scale
):
    group, width = queries.shape
    heads = width // HEAD_DIM
    tiles = group // tile

    def whole(shape):
        return pl.BlockSpec(
            shape, lambda i, *_: (0,) * len(shape), pipeline_mode=pl.Buffered(1)
        )

    head = whole((group, width))
    return pl.pallas_call(
        functools.partial(backward_kernel, tile, prompt_tiles, block_len, scale),
        grid_spec=pltpu.PrefetchScalarGridSpec(
            num_scalar_prefetch=2,
            grid=(1,),
            in_specs=[
                head,
                head,
                head,
                whole((heads, tiles, tile)),
                head,
                head,
                whole((group, 1)),
                whole((tiles, tile)),
            ],
            out_specs=[head, head, head],
            scratch_shapes=[
                pltpu.VMEM((width, group), bf16),
                pltpu.VMEM((group, width), bf16),
                pltpu.VMEM((heads, tiles, tile), f32),
                pltpu.VMEM((group, width), f32),
                pltpu.VMEM((group, width), f32),
                pltpu.VMEM((group, width), f32),
            ],
        ),
        out_shape=[
            jax.ShapeDtypeStruct((group, width), f32),
            jax.ShapeDtypeStruct((group, width), f32),
            jax.ShapeDtypeStruct((group, width), bf16),
        ],
        compiler_params=pltpu.CompilerParams(vmem_limit_bytes=60 * 2**20),
        cost_estimate=pl.CostEstimate(
            flops=5 * group * group * width, bytes_accessed=24 * group * width, transcendentals=0
        ),
        name="attention_backward",
    )(place, first_tile, queries, keys, values, lse, out, grad_out, seg_col, seg_row)


def slot_table(expert_rows, order_rows, gate_rows, count_experts, capacity):
    chosen = expert_rows.T[None, :, :] == jnp.arange(count_experts, dtype=jnp.int32)[:, None, None]
    holds = jnp.any(chosen, axis=1)
    order = jnp.sum(jnp.where(chosen, order_rows.T[None], 0), axis=1)
    gate = jnp.sum(jnp.where(chosen, gate_rows.T[None], 0.0), axis=1)
    earlier = holds[:, None, :] & (order[:, None, :] < order[:, :, None])
    slot = jnp.sum(earlier.astype(jnp.int32), axis=2)
    return (jnp.where(holds & (slot < capacity), slot, -1), gate)


def barrier(*arrays):
    return lax.optimization_barrier(arrays)


class Line:
    def __init__(self):
        peers = lax.axis_size("ctx")
        self.chips = peers // 2
        self.chip = lax.axis_index("ctx") // 2
        self.peers = peers
        self.pair = [(i, i ^ 1) for i in range(peers)]
        steps = range(1, self.chips)
        every = [d for s in steps for d in (s, -s)]
        self.orders = [
            sorted((d for d in every if 0 <= z + d < self.chips), key=lambda d: (abs(d), -d))
            for z in range(self.chips)
        ]

    def step(self, turn, from_below, from_above):
        up = [(i, i + 2) for i in range(2 * (turn - 1), self.peers - 2)]
        down = [(i + 2, i) for i in range(self.peers - 2 * turn)]
        return (
            lax.ppermute(from_below, "ctx", up),
            lax.ppermute(from_above, "ctx", down),
        )

    def other(self, rows):
        return lax.ppermute(rows, "ctx", self.pair)

    def take(self, turn, arrived):
        offsets = [self.orders[z][turn - 1] for z in range(self.chips)]
        offset = jnp.array(offsets, jnp.int32)[self.chip]
        kinds = sorted(set(offsets))
        chosen = arrived[kinds[0]]
        for kind in kinds[1:]:
            chosen = jnp.where(offset == kind, arrived[kind], chosen)
        return chosen, self.chip + offset


def swap_partners(groups, shift):
    return [(i, i ^ shift) for i in range(groups)]


def swap_dp(part, shift):
    return lax.ppermute(part, "dp", swap_partners(lax.axis_size("dp"), shift))


def first_dp(part):
    return [swap_dp(part, 1), swap_dp(part, 2)]


def send_dp(part):
    return [swap_dp(part, shift) for shift in (1, 2, 3)]


def second_dp(pieces, axis):
    half = pieces[0].shape[axis] // 2
    return [
        swap_dp(lax.slice_in_dim(pieces[0], 0, half, axis=axis), 2),
        swap_dp(lax.slice_in_dim(pieces[1], half, 2 * half, axis=axis), 1),
    ]


def join_dp(part, pieces, axis):
    mine = lax.axis_index("dp")
    size = part.shape[axis]
    half = size // 2

    def both(shift):
        return [(mine ^ shift) * size, (mine ^ shift) * size + half]

    parts = [(part, both(0)), (pieces[0], both(1)), (pieces[1], both(2))]
    if len(pieces) == 3:
        parts.append((pieces[2], both(3)))
    else:
        parts += [(pieces[2], both(3)[:1]), (pieces[3], both(3)[1:])]
    return join(parts, axis, size * lax.axis_size("dp"), half)


def pick_dp(term, shift, axis):
    size = term.shape[axis] // lax.axis_size("dp")
    return lax.dynamic_slice_in_dim(term, (lax.axis_index("dp") ^ shift) * size, size, axis)


def scatter_one(term, shift, axis):
    return swap_dp(pick_dp(term, shift, axis), shift)


def total_dp(term, pieces, axis):
    groups = lax.axis_size("dp")
    size = term.shape[axis] // groups
    total = lax.dynamic_slice_in_dim(term, lax.axis_index("dp") * size, size, axis).astype(f32)
    for piece in pieces:
        total = total + piece.astype(f32)
    return total


def sum_small(array):
    peers = lax.axis_size("ctx")

    def swap(rows, shift):
        return lax.ppermute(rows, "ctx", [(i, i ^ shift) for i in range(peers)])

    array = array + swap(array, 1)
    return sum((swap(array, 2 * shift) for shift in range(1, peers // 2)), start=array)


def project_kernel(places, own, other, weight, gain, *rest):
    normed, raw, square = rest[-3:]

    def work(rows_ref):
        rows = rows_ref[...].astype(f32)
        hat = rows * lax.rsqrt(jnp.mean(rows * rows, axis=1, keepdims=True) + epsilon)
        low = (hat * gain[...]).astype(bf16)
        normed[...] = low
        product = jnp.dot(low, weight[...], preferred_element_type=f32)
        raw[...] = product
        third = product.shape[1] // 3
        for which in range(2):
            part = product[:, which * third : (which + 1) * third]
            square[which : which + 1, :] = jnp.sum((part * part).T, axis=0, keepdims=True)

    pl.when(pl.program_id(0) == 0)(lambda: work(own))
    pl.when(pl.program_id(0) == 1)(lambda: work(other))


def project(unit_index, own, other, weight, gain, peers, kept=()):
    rows, width = own.shape
    columns = weight.shape[1]

    def fixed(shape):
        return pl.BlockSpec(shape, lambda s, *_: (0,) * len(shape))

    return pl.pallas_call(
        project_kernel,
        grid_spec=pltpu.PrefetchScalarGridSpec(
            num_scalar_prefetch=1,
            grid=(2,),
            in_specs=[
                fixed((rows, width)),
                fixed((rows, width)),
                fixed((width, columns)),
                fixed((1, width)),
            ]
            + [pl.BlockSpec(memory_space=pl.ANY)] * len(kept),
            out_specs=[
                pl.BlockSpec((rows, width), lambda s, at: (at[s], 0)),
                pl.BlockSpec((rows, columns), lambda s, at: (at[s], 0)),
                pl.BlockSpec((None, 2, rows), lambda s, at: (at[s], 0, 0)),
            ],
        ),
        out_shape=[
            jax.ShapeDtypeStruct((peers * rows, width), bf16),
            jax.ShapeDtypeStruct((peers * rows, columns), f32),
            jax.ShapeDtypeStruct((peers, 2, rows), f32),
        ],
        input_output_aliases={5 + i: i for i in range(len(kept))},
        compiler_params=pltpu.CompilerParams(vmem_limit_bytes=56 * 2**20),
        name="project",
    )(unit_index, own, other, weight, gain, *kept)


def join_kernel(axis, blocks, block, at, *refs):
    out = refs[-1]
    turn = 0
    for ref, count in zip(refs[:-1], blocks):
        for index in range(count):
            here = (slice(None),) * axis + (slice(index * block, (index + 1) * block),)

            @pl.when(pl.program_id(0) == turn)
            def copy(ref=ref, here=here):
                out[...] = ref[here]

            turn += 1


def join(parts, axis, length, block):
    shape = list(parts[0][0].shape)
    shape[axis] = block
    blocks = [len(starts) for _, starts in parts]
    at = jnp.stack([start // block for _, starts in parts for start in starts]).astype(jnp.int32)
    rank = len(shape)

    def target(turn, at):
        return tuple(at[turn] if index == axis else 0 for index in range(rank))

    def fixed(part):
        return pl.BlockSpec(
            part.shape, lambda turn, at: (0,) * rank, pipeline_mode=pl.Buffered(1)
        )

    return pl.pallas_call(
        functools.partial(join_kernel, axis, blocks, block),
        grid_spec=pltpu.PrefetchScalarGridSpec(
            num_scalar_prefetch=1,
            grid=(sum(blocks),),
            in_specs=[fixed(part) for part, _ in parts],
            out_specs=pl.BlockSpec(tuple(shape), target),
        ),
        out_shape=jax.ShapeDtypeStruct(
            tuple(length if index == axis else size for index, size in enumerate(shape)),
            parts[0][0].dtype,
        ),
        compiler_params=pltpu.CompilerParams(vmem_limit_bytes=40 * 2**20),
        name="join",
    )(at, *[part for part, _ in parts])


def lay_kernel(at, own, other, *rest):
    out = rest[-1]

    def work(source):
        out[...] = source[...].astype(f32)

    pl.when(pl.program_id(0) == 0)(lambda: work(own))
    pl.when(pl.program_id(0) == 1)(lambda: work(other))


def lay(at, own, other, out_shape, block_columns, first, pieces, index, kept=()):
    block = (out_shape[0], block_columns)
    return pl.pallas_call(
        lay_kernel,
        grid_spec=pltpu.PrefetchScalarGridSpec(
            num_scalar_prefetch=1,
            grid=(2, pieces),
            in_specs=[pl.BlockSpec(block, lambda s, t, at: (0, first + t))] * 2
            + [pl.BlockSpec(memory_space=pl.ANY)] * len(kept),
            out_specs=pl.BlockSpec(block, lambda s, t, at: (0, index(at[s], t))),
        ),
        out_shape=jax.ShapeDtypeStruct(out_shape, f32),
        input_output_aliases={3: 0} if kept else {},
        name="lay",
    )(at, own, other, *kept)


def expert_kernel(
    unit, own, other, cots, slots, gates, columns, w_gate, w_up, w_down, *rest
):
    expert_in, grad_rows, hidden, grad_gate, grad_up, part, total, ready = rest[-8:]
    expert, piece = pl.program_id(0), pl.program_id(1)
    last_expert = expert == pl.num_programs(0) - 1
    last_piece = piece == pl.num_programs(1) - 1
    room, width = expert_in.shape[1:]
    rows = own.shape[0]
    core = unit[1]

    @pl.when(piece == 0)
    def bring():
        at = lax.broadcasted_iota(jnp.int32, (room, rows), 0)
        for s in range(2):
            found = at == slots[s, pl.ds(expert, 1), :]
            picks = jnp.where(found, 1.0, 0.0).astype(bf16)
            slot_gate = jnp.sum(
                jnp.where(found, gates[s, pl.ds(expert, 1), :], 0.0), axis=1, keepdims=True
            )
            grad_rows[s] = (
                jnp.dot(picks, cots[s], preferred_element_type=f32) * slot_gate
            ).astype(bf16)

            @pl.when(core == s)
            def from_own():
                expert_in[s] = jnp.dot(picks, own[...], preferred_element_type=f32).astype(bf16)

            @pl.when(core != s)
            def from_other():
                expert_in[s] = jnp.dot(picks, other[...], preferred_element_type=f32).astype(bf16)

    rows_in = expert_in[...].reshape(2 * room, width)
    gate_pre = jnp.dot(rows_in, w_gate[...], preferred_element_type=f32)
    up_pre = jnp.dot(rows_in, w_up[...], preferred_element_type=f32)
    grad_hidden = lax.dot_general(
        grad_rows[...].reshape(2 * room, width), w_down[...], NT, preferred_element_type=f32
    )
    sigmoid = 1.0 / (1.0 + jnp.exp(-gate_pre))
    silu = gate_pre * sigmoid
    hidden[...] = (silu * up_pre).astype(bf16).reshape(hidden.shape)
    gate_here = (grad_hidden * up_pre * sigmoid * (1.0 + gate_pre * (1.0 - sigmoid))).astype(bf16)
    up_here = (grad_hidden * silu).astype(bf16)
    grad_gate[...] = gate_here.reshape(grad_gate.shape)
    grad_up[...] = up_here.reshape(grad_up.shape)

    def back():
        return lax.dot_general(gate_here, w_gate[...], NT, preferred_element_type=f32) + lax.dot_general(
            up_here, w_up[...], NT, preferred_element_type=f32
        )

    @pl.when(piece == 0)
    def first():
        total[...] = back()

    @pl.when(piece != 0)
    def later():
        total[...] += back()

    @pl.when(last_piece)
    def keep():
        for s in range(2):
            ready[s, pl.ds(pl.multiple_of(expert * room, 16), room), :] = total[
                s * room : (s + 1) * room, :
            ].astype(bf16)

    @pl.when(last_piece & last_expert)
    def send():
        for s in range(2):
            at = lax.broadcasted_iota(jnp.int32, (rows, ready.shape[1]), 1)
            here = columns[s]
            found = at == here[:, 0:1]
            for e in range(1, here.shape[1]):
                found = found | (at == here[:, e : e + 1])
            part[s] = jnp.dot(
                jnp.where(found, 1.0, 0.0).astype(bf16), ready[s], preferred_element_type=f32
            ).astype(bf16)


def expert_unit(unit, own, other, cot_all, slots, gates, columns, w_gate, w_up, w_down, room, kept=(), piece=256):
    rows, width = own.shape
    experts, _, inner = w_gate.shape
    peers = cot_all.shape[0]
    wide_shape = (peers, experts, room, width)
    thin_shape = (peers, experts, room, inner)
    anywhere = pl.BlockSpec(memory_space=pl.ANY)
    once = pl.Buffered(1)

    def fixed(shape):
        return pl.BlockSpec(shape, lambda e, f, u: (0,) * len(shape), pipeline_mode=once)

    def chip(shape):
        return pl.BlockSpec((2, *shape), lambda e, f, u: (u[0], 0, 0), pipeline_mode=once)

    wide = pl.BlockSpec((2, None, room, width), lambda e, f, u: (u[0], e, 0, 0))
    thin = pl.BlockSpec((2, None, room, piece), lambda e, f, u: (u[0], e, 0, f))
    return pl.pallas_call(
        expert_kernel,
        grid_spec=pltpu.PrefetchScalarGridSpec(
            num_scalar_prefetch=1,
            grid=(experts, inner // piece),
            in_specs=[
                fixed((rows, width)), fixed((rows, width)), chip((rows, width)),
                chip((experts, rows)), chip((experts, rows)), chip((rows, experts)),
                pl.BlockSpec((None, width, piece), lambda e, f, u: (e, 0, f)),
                pl.BlockSpec((None, width, piece), lambda e, f, u: (e, 0, f)),
                pl.BlockSpec((None, piece, width), lambda e, f, u: (e, f, 0)),
            ] + [anywhere] * len(kept),
            out_specs=[wide, wide, thin, thin, thin,
                pl.BlockSpec((2, rows, width), lambda e, f, u: (u[0], 0, 0))],
            scratch_shapes=[
                pltpu.VMEM((2 * room, width), f32),
                pltpu.VMEM((2, experts * room, width), bf16),
            ],
        ),
        out_shape=[
            jax.ShapeDtypeStruct(shape, bf16)
            for shape in [wide_shape] * 2 + [thin_shape] * 3 + [cot_all.shape]
        ],
        input_output_aliases={10 + i: i for i in range(len(kept))},
        compiler_params=pltpu.CompilerParams(vmem_limit_bytes=60 * 2**20),
        name="expert_unit",
    )(unit, own, other, cot_all, slots, gates, columns, w_gate, w_up, w_down, *kept)


def out_kernel(hidden, w_down, slots, gates, columns, part, ready):
    expert = pl.program_id(1)
    room = hidden.shape[1]
    rows = slots.shape[2]
    at = lax.broadcasted_iota(jnp.int32, (room, rows), 0)
    product = jnp.dot(
        hidden[...].reshape(2 * room, hidden.shape[2]), w_down[...], preferred_element_type=f32
    )
    for s in range(2):
        found = at == slots[s, pl.ds(expert, 1), :]
        slot_gate = jnp.sum(jnp.where(found, gates[s, pl.ds(expert, 1), :], 0.0), axis=1, keepdims=True)
        ready[s, pl.ds(pl.multiple_of(expert * room, 16), room), :] = (
            product[s * room : (s + 1) * room] * slot_gate
        ).astype(bf16)

    @pl.when(expert == pl.num_programs(1) - 1)
    def send():
        for s in range(2):
            at = lax.broadcasted_iota(jnp.int32, (rows, ready.shape[1]), 1)
            here = columns[s]
            found = at == here[:, 0:1]
            for e in range(1, here.shape[1]):
                found = found | (at == here[:, e : e + 1])
            part[s] = jnp.dot(
                jnp.where(found, 1.0, 0.0).astype(bf16), ready[s], preferred_element_type=f32
            ).astype(bf16)


def expert_out(hidden, w_down, slots, gates, columns):
    peers, experts, room, inner = hidden.shape
    width = w_down.shape[2]
    rows = slots.shape[2]
    return pl.pallas_call(
        out_kernel,
        grid=(peers // 2, experts),
        in_specs=[
            pl.BlockSpec((2, None, room, inner), lambda c, e: (c, e, 0, 0)),
            pl.BlockSpec((None, inner, width), lambda c, e: (e, 0, 0)),
            pl.BlockSpec((2, experts, rows), lambda c, e: (c, 0, 0)),
            pl.BlockSpec((2, experts, rows), lambda c, e: (c, 0, 0)),
            pl.BlockSpec((2, rows, experts), lambda c, e: (c, 0, 0)),
        ],
        out_specs=pl.BlockSpec((2, rows, width), lambda c, e: (c, 0, 0)),
        out_shape=jax.ShapeDtypeStruct((peers, rows, width), bf16),
        scratch_shapes=[pltpu.VMEM((2, experts * room, width), bf16)],
        compiler_params=pltpu.CompilerParams(vmem_limit_bytes=60 * 2**20),
        name="expert_out",
    )(hidden, w_down, slots, gates, columns)


def on_device(
    tokens,
    cotangent,
    wqkv,
    wo,
    attn_gain,
    query_gain,
    key_gain,
    moe_gain,
    w_gate,
    w_up,
    w_down,
    expert_ids,
    gates,
    slot_order,
    block_assign,
    segment_ids,
):
    count_rows, width = tokens.shape
    head_dim = width // HEADS
    scale = head_dim ** (-0.5)
    peers = lax.axis_size("ctx")
    groups = lax.axis_size("dp")
    me = lax.axis_index("ctx")
    core = me % 2
    my_dp = lax.axis_index("dp")
    group_rows = count_rows * peers
    rep = max(1, peers // HEADS)
    own_heads = max(1, HEADS // peers)
    own_width = own_heads * head_dim
    first_head = (me // rep) * own_heads
    block_len = count_rows // BLK_DEV
    tile = 512
    line = Line()
    turns = range(1, line.chips)

    assign = block_assign[0]
    count_blocks = assign.shape[0]
    place = jnp.argmax(
        assign[None, :] == jnp.arange(count_blocks, dtype=jnp.int32)[:, None], axis=1
    ).astype(jnp.int32)
    cont = segment_ids[0]
    prompt_len = group_rows - cont.shape[0]
    prompt_tiles = prompt_len // tile
    seg_logical = jnp.concatenate([jnp.full((prompt_len,), -1, jnp.int32), cont])
    tiles = group_rows // tile
    tile_seg = seg_logical.reshape(tiles, tile)[:, 0]
    first_tile = jnp.where(
        tile_seg < 0,
        jnp.arange(tiles, dtype=jnp.int32),
        jnp.sum((seg_logical[None, :] < tile_seg[:, None]).astype(jnp.int32), axis=1) // tile,
    ).astype(jnp.int32)
    seg_col = seg_logical[:, None]
    seg_row = seg_logical.reshape(tiles, tile)

    local_experts = w_gate.shape[0]
    count_experts = local_experts * peers
    capacity = 9 * count_rows * TOP // (8 * count_experts)
    room = (capacity + 15) // 16 * 16
    slot, gate = slot_table(expert_ids, slot_order, gates, count_experts, capacity)
    table = jnp.stack(
        [
            slot.reshape(peers, local_experts, count_rows).astype(f32),
            gate.reshape(peers, local_experts, count_rows),
        ],
        axis=1,
    )

    inputs = tokens.astype(f32)
    below, above = line.step(1, tokens, tokens)
    other = line.other(tokens)
    w_part = jnp.concatenate(
        [
            lax.dynamic_slice_in_dim(wqkv, which * width + first_head * head_dim, own_width, 1)
            for which in range(3)
        ],
        axis=1,
    )
    w_pieces = send_dp(w_part)
    gain_part = jnp.stack([attn_gain, query_gain, key_gain, moe_gain])
    gain_all = jnp.zeros((4, width), bf16)
    for shift in range(groups):
        piece = swap_dp(gain_part, shift) if shift else gain_part
        gain_all = lax.dynamic_update_slice_in_dim(
            gain_all, piece, (my_dp ^ shift) * gain_part.shape[1], 1
        )
    gain_all = gain_all.astype(f32)
    below, above, other, gain_all, table, wo, w_gate, *w_pieces = barrier(
        below, above, other, gain_all, table, wo, w_gate, *w_pieces
    )
    full_gate = lax.all_gather(w_gate, "dp", axis=1, tiled=True)
    w_own = join_dp(w_part, w_pieces, 0)
    gain_attn, gain_moe = gain_all[0:1], gain_all[3:4]
    gain_own = lax.dynamic_slice_in_dim(gain_all, first_head * head_dim, own_width, 1)
    gain_q, gain_k = gain_own[1:2], gain_own[2:3]

    half_rows = wo.shape[0] // 2
    arrived = {-1: below, 1: above}
    own, chip = tokens, line.chip
    kept, travelled = (), ()
    for turn in turns:
        if turn + 1 < line.chips:
            below, above = line.step(turn + 1, below, above)
            arrived[-turn - 1], arrived[turn + 1] = below, above
        next_own, next_chip = line.take(turn, arrived)
        next_other = line.other(next_own)
        at = jnp.stack([2 * chip + core, 2 * chip + 1 - core]).astype(jnp.int32)
        kept = project(at, own, other, w_own, gain_attn, peers, kept)
        travel = list(travelled)
        if turn == 1:
            wo_half = lax.dynamic_slice_in_dim(wo, core * half_rows, half_rows, 0)
            travel = first_dp(wo_half)
        if turn == 2:
            travel.append(swap_dp(wo_half, 3))
        own, other, chip = next_own, next_other, next_chip
        square = kept[2]
        below, above, own, other, square, w_down, *travelled = barrier(
            below, above, own, other, square, w_down, *travel
        )
        kept = (kept[0], kept[1], square)
        if turn + 1 < line.chips:
            arrived[-turn - 1], arrived[turn + 1] = below, above
    cotangent_now, other = barrier(cotangent, other)
    cot_all = lax.all_gather(cotangent_now, "ctx", axis=0, tiled=True).reshape(
        peers, count_rows, width
    )
    down_pieces = first_dp(w_down)
    wo_mine = jnp.concatenate([wo_half, *travelled[:3]], axis=0)
    wo_theirs = line.other(wo_mine)
    table = lax.all_to_all(table, "ctx", split_axis=0, concat_axis=0, tiled=True)
    at = jnp.stack([2 * chip + core, 2 * chip + 1 - core]).astype(jnp.int32)
    normed_all, raw, square = project(at, own, other, w_own, gain_attn, peers, kept)
    square = sum_small(square.transpose(1, 0, 2).reshape(2, group_rows)) * (1.0 / rep)
    inv_qk = lax.rsqrt(square / width + epsilon).T
    slot = table[:, 0].astype(jnp.int32)
    gate_rows = table[:, 1]
    offsets = (jnp.arange(local_experts, dtype=jnp.int32) * room)[None, :, None]
    columns = jnp.where(slot >= 0, slot + offsets, -1).transpose(0, 2, 1)

    inv_qk, w_up, slot, gate_rows, columns, full_gate, wo_mine, wo_theirs, *down_pieces = barrier(
        inv_qk, w_up, slot, gate_rows, columns, full_gate, wo_mine, wo_theirs, *down_pieces
    )
    down_pieces = down_pieces + second_dp(down_pieces, 1)
    up_pieces = first_dp(w_up)
    attended, lse, queries, keys, values = attention_forward(
        raw,
        inv_qk,
        gain_q,
        gain_k,
        seg_col,
        seg_row,
        place,
        first_tile,
        tile,
        prompt_tiles,
        block_len,
        scale,
    )
    attended, *pieces = barrier(attended, *up_pieces, *down_pieces)
    up_pieces, down_pieces = pieces[:2], pieces[2:]
    up_pieces = up_pieces + second_dp(up_pieces, 1)
    attn_low = lax.all_to_all(
        attended.reshape(peers, count_rows, own_width), "ctx", split_axis=0, concat_axis=0, tiled=True
    )[::rep]
    full_down = join_dp(w_down, down_pieces, 1)
    starts = [(my_dp ^ shift) * wo.shape[0] for shift in range(groups)]
    full_wo = join(
        [
            (wo_mine, [start + core * half_rows for start in starts]),
            (wo_theirs, [start + (1 - core) * half_rows for start in starts]),
        ],
        0,
        width,
        half_rows,
    )
    full_up = join_dp(w_up, up_pieces, 1)
    attn_low, full_wo, full_down, full_up = barrier(attn_low, full_wo, full_down, full_up)
    attn_low = attn_low.transpose(1, 0, 2).reshape(count_rows, width)
    state = inputs + jnp.dot(attn_low, full_wo, preferred_element_type=f32)
    inv_state = rms_scale(state)
    hat_state = state * inv_state
    normed_moe = (hat_state * gain_moe).astype(bf16)

    normed_moe, cot_all = barrier(normed_moe, cot_all)
    below, above = normed_moe, normed_moe
    own, chip = normed_moe, line.chip
    arrived = {}
    kept = ()
    for turn in range(line.chips):
        if turn + 1 < line.chips:
            below, above = line.step(turn + 1, below, above)
            arrived[-turn - 1], arrived[turn + 1] = below, above
        if turn > 0:
            own, chip = line.take(turn, arrived)
        other = line.other(own)
        kept = expert_unit(
            jnp.stack([chip, core]).astype(jnp.int32),
            own,
            other,
            cot_all,
            slot,
            gate_rows,
            columns,
            full_gate,
            full_up,
            full_down,
            room,
            kept,
        )
        if turn + 1 < line.chips:
            below, above, *kept = barrier(below, above, *kept)
            arrived[-turn - 1], arrived[turn + 1] = below, above
    expert_in, grad_rows, hidden, grad_gate_pre, grad_up_pre, part_moe = kept
    grad_normed_moe = lax.psum_scatter(
        part_moe.reshape(group_rows, width), "ctx", scatter_dimension=0, tiled=True
    )

    part_mixed = expert_out(hidden, full_down, slot, gate_rows, columns)
    grad_down = jnp.einsum("sncf,sncd->nfd", hidden, grad_rows, preferred_element_type=f32)
    grad_down = grad_down.astype(bf16)
    part_mixed, grad_down, expert_in = barrier(part_mixed, grad_down, expert_in)
    down_pieces = [scatter_one(grad_down, shift, 1) for shift in (1, 2, 3)]
    grad_gate = jnp.einsum("sncd,sncf->ndf", expert_in, grad_gate_pre, preferred_element_type=f32)
    grad_up = jnp.einsum("sncd,sncf->ndf", expert_in, grad_up_pre, preferred_element_type=f32)
    grad_gate, grad_up = grad_gate.astype(bf16), grad_up.astype(bf16)
    grad_normed_moe, part_mixed, grad_gate, grad_up, *down_pieces = barrier(
        grad_normed_moe, part_mixed, grad_gate, grad_up, *down_pieces
    )
    mixed = lax.psum_scatter(
        part_mixed.reshape(group_rows, width), "ctx", scatter_dimension=0, tiled=True
    )

    gate_pieces = [scatter_one(grad_gate, shift, 1) for shift in (1, 2)]
    grad_normed_moe = grad_normed_moe.astype(f32)
    moe_gain_term = jnp.sum(grad_normed_moe * hat_state, axis=0)
    grad_state = cotangent.astype(f32) + rms_back(grad_normed_moe * gain_moe, hat_state, inv_state)
    grad_branch = grad_state.astype(bf16)
    grad_attn = lax.dot_general(grad_branch, full_wo, NT, preferred_element_type=f32).astype(bf16)
    grad_attn = grad_attn.reshape(count_rows, peers // rep, own_width).transpose(1, 0, 2)
    grad_attn = jnp.repeat(grad_attn, rep, axis=0)
    grad_attended = lax.all_to_all(
        grad_attn, "ctx", split_axis=0, concat_axis=0, tiled=True
    ).reshape(group_rows, own_width)
    part_out = lax.dot_general(attn_low, grad_branch, TN, preferred_element_type=f32).astype(bf16)
    half = width // 2
    out_theirs = line.other(lax.dynamic_slice_in_dim(part_out, (1 - core) * half, half, 1))
    part_out = lax.dynamic_slice_in_dim(part_out, core * half, half, 1).astype(f32)
    part_out = (part_out + out_theirs.astype(f32)).astype(bf16)
    down_sum = total_dp(grad_down, down_pieces, 1)
    grad_attended, part_out, down_sum, *gate_pieces = barrier(
        grad_attended, part_out, down_sum, *gate_pieces
    )
    out_pieces = [scatter_one(part_out, shift, 0) for shift in (1, 2, 3)]
    grad_q, grad_k, grad_v = attention_backward(
        queries,
        keys,
        values,
        lse,
        attended,
        grad_attended,
        seg_col,
        seg_row,
        place,
        first_tile,
        tile,
        prompt_tiles,
        block_len,
        scale,
    )
    grad_q, grad_gate, *out_pieces = barrier(grad_q, grad_gate, *out_pieces)
    gate_pieces.append(scatter_one(grad_gate, 3, 1))
    out_sum = total_dp(part_out, out_pieces, 0).astype(bf16)
    rows_dp = out_sum.shape[0]
    share = half // line.chips
    out_sum = out_sum.reshape(rows_dp, line.chips, share).transpose(1, 0, 2)
    hat_q = raw[:, :own_width] * inv_qk[:, 0:1]
    hat_k = raw[:, own_width : 2 * own_width] * inv_qk[:, 1:2]
    query_gain_term = jnp.sum(grad_q * hat_q, axis=0)
    key_gain_term = jnp.sum(grad_k * hat_k, axis=0)
    means = jnp.stack(
        [
            jnp.sum(grad_q * gain_q * hat_q, axis=1),
            jnp.sum(grad_k * gain_k * hat_k, axis=1),
        ]
    )
    means = (sum_small(means) * (1.0 / (rep * width))).T
    grad_raw_q = inv_qk[:, 0:1] * (grad_q * gain_q - hat_q * means[:, 0:1])
    grad_raw_k = inv_qk[:, 1:2] * (grad_k * gain_k - hat_k * means[:, 1:2])
    grad_qkv = jnp.concatenate([grad_raw_q.astype(bf16), grad_raw_k.astype(bf16), grad_v], axis=1)
    part_normed = lax.dot_general(grad_qkv, w_own, NT, preferred_element_type=f32) * (1.0 / rep)
    part_normed = part_normed.astype(bf16)
    part_normed, mixed, grad_up, out_sum = barrier(part_normed, mixed, grad_up, out_sum)
    grad_normed = lax.psum_scatter(part_normed, "ctx", scatter_dimension=0, tiled=True)

    out_sum = lax.all_to_all(
        out_sum,
        "ctx",
        split_axis=0,
        concat_axis=0,
        tiled=True,
        axis_index_groups=[[2 * z + c for z in range(peers // 2)] for c in range(2)],
    )
    part_qkv = lax.dot_general(normed_all, grad_qkv, TN, preferred_element_type=f32).astype(bf16)
    qkv_pieces = [scatter_one(part_qkv, shift, 0) for shift in (1, 2, 3)]
    own_terms = jnp.stack([query_gain_term, key_gain_term]) * (1.0 / rep)
    spread = lax.dynamic_update_slice_in_dim(
        jnp.zeros((2, width), f32), own_terms, first_head * head_dim, 1
    )
    attn_gain_term = (
        jnp.sum(part_normed.astype(f32) * normed_all.astype(f32), axis=0) / gain_attn[0]
    )
    gain_terms = jnp.concatenate([attn_gain_term[None], spread, moe_gain_term[None]], axis=0)
    gain_pieces = [scatter_one(gain_terms, shift, 1) for shift in (1, 2, 3)]
    output = (state + mixed.astype(f32)).astype(bf16)
    out_sum, gain_terms, grad_up, grad_gate, output, *pieces = barrier(
        out_sum, gain_terms, grad_up, grad_gate, output, *qkv_pieces, *gain_pieces, *gate_pieces
    )
    qkv_pieces, gain_pieces, gate_pieces = pieces[:3], pieces[3:6], pieces[6:]
    gate_sum = total_dp(grad_gate, gate_pieces, 1)
    gain_terms = total_dp(gain_terms, gain_pieces, 1)
    qkv_sum = total_dp(part_qkv, qkv_pieces, 0).astype(bf16)
    out_sum = jnp.sum(out_sum.astype(f32), axis=0).astype(bf16)
    own, chip = jnp.concatenate([qkv_sum, out_sum], axis=1), line.chip
    gain_shape = gain_terms.shape
    row = own.shape[1]
    gain_terms = gain_terms.reshape(-1)
    gain_rows = (gain_terms.size // row + 16) // 16 * 16
    gain_size = gain_terms.size
    gain_terms = jnp.pad(gain_terms, (0, gain_rows * row - gain_size)).reshape(gain_rows, row)
    own = jnp.concatenate([own, gain_terms.astype(bf16)], axis=0)
    gain_terms = jnp.zeros((gain_rows, row), f32)
    below, above = own, own
    arrived = {}
    qkv_kept, out_kept = (), ()
    for turn in range(line.chips):
        if turn + 1 < line.chips:
            below, above = line.step(turn + 1, below, above)
        if turn > 0:
            own, chip = line.take(turn, arrived)
        other = line.other(own)
        gain_terms = gain_terms + own[rows_dp:].astype(f32) + other[rows_dp:].astype(f32)
        at = jnp.stack([2 * chip + core, 2 * chip + 1 - core]).astype(jnp.int32) // rep
        qkv_kept = [
            lay(
                at,
                own,
                other,
                (rows_dp, 3 * width),
                own_width,
                0,
                3,
                lambda p, t: t * (width // own_width) + p,
                qkv_kept,
            )
        ]
        at = jnp.stack([core * line.chips + chip, (1 - core) * line.chips + chip]).astype(jnp.int32)
        if share % HEAD_DIM == 0 and 3 * own_width % share == 0:
            out_kept = [
                lay(
                    at,
                    own,
                    other,
                    (rows_dp, width),
                    share,
                    3 * own_width // share,
                    1,
                    lambda p, t: p,
                    out_kept,
                )
            ]
        else:
            out_kept = list(out_kept) or [jnp.zeros((rows_dp, width), f32)]
            for which, part in enumerate((own, other)):
                out_kept[0] = lax.dynamic_update_slice_in_dim(
                    out_kept[0], part[:rows_dp, 3 * own_width :].astype(f32), at[which] * share, 1
                )
        if turn == 0:
            up_pieces = [scatter_one(grad_up, shift, 1) for shift in (1, 2)]
        if turn == 1:
            up_pieces.append(scatter_one(grad_up, 3, 1))
        if turn == 2:
            grad_up = total_dp(grad_up, up_pieces, 1)
            up_pieces = []
        if turn + 1 < line.chips:
            below, above, qkv_kept[0], out_kept[0], grad_up, gate_sum, *up_pieces = barrier(
                below, above, qkv_kept[0], out_kept[0], grad_up, gate_sum, *up_pieces
            )
            arrived[-turn - 1], arrived[turn + 1] = below, above
    qkv_total, out_total = qkv_kept[0], out_kept[0]
    up_sum = grad_up
    gain_terms = gain_terms.reshape(-1)[:gain_size].reshape(gain_shape)
    out_total, qkv_total, up_sum, output, gain_terms, grad_normed = barrier(
        out_total, qkv_total, up_sum, output, gain_terms, grad_normed
    )

    grad_normed = grad_normed.astype(f32)
    inv_in = rms_scale(inputs)
    hat_in = inputs * inv_in
    input_grad = (grad_state + rms_back(grad_normed * gain_attn, hat_in, inv_in)).astype(bf16)
    return (
        output,
        input_grad,
        qkv_total,
        out_total,
        gain_terms[0],
        gain_terms[1],
        gain_terms[2],
        gain_terms[3],
        gate_sum,
        up_sum,
        down_sum,
    )


def solution(mesh):
    rows = P(("dp", "ctx"), None)
    expert = P("ctx", "dp", None)
    by_dp = P("dp", None)
    return jax.shard_map(
        on_device,
        mesh=mesh,
        in_specs=(
            rows,
            rows,
            by_dp,
            by_dp,
            P("dp"),
            P("dp"),
            P("dp"),
            P("dp"),
            expert,
            expert,
            expert,
            rows,
            rows,
            rows,
            by_dp,
            by_dp,
        ),
        out_specs=(
            rows,
            rows,
            by_dp,
            by_dp,
            P("dp"),
            P("dp"),
            P("dp"),
            P("dp"),
            expert,
            expert,
            expert,
        ),
        check_vma=False,
    )
```

```python
import functools

import jax
import jax.numpy as jnp
from jax import lax
from jax.experimental import pallas as pl
from jax.experimental.pallas import tpu as pltpu
from jax.sharding import PartitionSpec as P

HEADS = 16
TOP = 8
BLK_DEV = 2
LOG2E = 1.4426950408889634
HEAD_DIM = 128

epsilon = 1e-06
masked_value = -1e30
f32 = jnp.float32
bf16 = jnp.bfloat16
NT = (((1,), (1,)), ((), ()))
TN = (((0,), (0,)), ((), ()))


def rms_scale(values_in):
    return lax.rsqrt(jnp.mean(values_in * values_in, axis=-1, keepdims=True) + epsilon)


def rms_back(grad_hat, normed, scale_rows):
    return scale_rows * (grad_hat - normed * jnp.mean(grad_hat * normed, axis=-1, keepdims=True))


def tile_mask(seg_col, seg_row, key_first, query_first):
    rows, columns = seg_col.shape[0], seg_row.shape[1]
    key_pos = key_first + lax.broadcasted_iota(jnp.int32, (rows, columns), 0)
    query_pos = query_first + lax.broadcasted_iota(jnp.int32, (rows, columns), 1)
    return (seg_col == seg_row) & (key_pos <= query_pos)


def forward_kernel(
    tile,
    prompt_tiles,
    block_len,
    scale,
    place,
    first_tile,
    raw_q,
    raw_k,
    raw_v,
    inv,
    gain_q,
    gain_k,
    seg_col,
    seg_row,
    out,
    lse,
    queries,
    keys,
    values,
    values_t,
    out_logical,
):
    group, width = raw_q.shape
    tiles = group // tile
    blocks = group // block_len
    columns = [slice(first, first + HEAD_DIM) for first in range(0, width, HEAD_DIM)]

    def bring(block, carry):
        source = pl.ds(pl.multiple_of(place[block] * block_len, block_len), block_len)
        target = pl.ds(pl.multiple_of(block * block_len, block_len), block_len)
        scales = inv[source, :]
        queries[target, :] = (raw_q[source, :] * scales[:, 0:1] * gain_q[...]).astype(bf16)
        keys[target, :] = (raw_k[source, :] * scales[:, 1:2] * gain_k[...]).astype(bf16)
        values[target, :] = raw_v[source, :].astype(bf16)
        return carry

    lax.fori_loop(0, blocks, bring, 0)
    for index in range(tiles):
        values_t[:, index * tile : (index + 1) * tile] = values[
            index * tile : (index + 1) * tile, :
        ].T

    def query_tile(index, carry):
        first = pl.multiple_of(index * tile, tile)
        here = pl.ds(first, tile)
        seg_query = seg_row[pl.ds(index, 1), :]

        def step(is_masked, at, states):
            key_first = pl.multiple_of(at * tile, tile)
            there = pl.ds(key_first, tile)
            if is_masked:
                allowed = tile_mask(seg_col[there, :], seg_query, key_first, first)
            every = [
                lax.dot_general(
                    keys[there, head], queries[here, head], NT, preferred_element_type=f32
                )
                for head in columns
            ]
            after = []
            for scores, head, (largest, total, running) in zip(every, columns, states):
                scores = scores * (scale * LOG2E)
                if is_masked:
                    scores = jnp.where(allowed, scores, masked_value)
                new_largest = jnp.maximum(largest, jnp.max(scores, axis=0, keepdims=True))
                shrink = jnp.exp2(largest - new_largest)
                terms = jnp.exp2(scores - new_largest)
                total = total * shrink + jnp.sum(terms, axis=0, keepdims=True)
                running = running * shrink + jnp.dot(
                    values_t[head, there], terms.astype(bf16), preferred_element_type=f32
                )
                after.append((new_largest, total, running))
            return after

        states = [
            (
                jnp.full((1, tile), masked_value, f32),
                jnp.zeros((1, tile), f32),
                jnp.zeros((HEAD_DIM, tile), f32),
            )
            for _ in columns
        ]
        states = lax.fori_loop(
            0, jnp.minimum(index, prompt_tiles), functools.partial(step, False), states
        )
        states = lax.fori_loop(first_tile[index], index + 1, functools.partial(step, True), states)
        for which, (head, (largest, total, running)) in enumerate(zip(columns, states)):
            lse[which, pl.ds(index, 1), :] = largest + jnp.log2(total)
            out_logical[here, head] = (running / total).T.astype(bf16)
        return carry

    lax.fori_loop(0, tiles, query_tile, 0)

    def send(block, carry):
        target = pl.ds(pl.multiple_of(place[block] * block_len, block_len), block_len)
        source = pl.ds(pl.multiple_of(block * block_len, block_len), block_len)
        out[target, :] = out_logical[source, :]
        return carry

    lax.fori_loop(0, blocks, send, 0)


def backward_kernel(
    tile,
    prompt_tiles,
    block_len,
    scale,
    place,
    first_tile,
    queries,
    keys,
    values,
    lse,
    out,
    grad_out,
    seg_col,
    seg_row,
    grad_q,
    grad_k,
    grad_v,
    keys_t,
    grad_here,
    delta,
    total_q,
    total_k,
    total_v,
):
    group, width = queries.shape
    tiles = group // tile
    blocks = group // block_len
    columns = [slice(first, first + HEAD_DIM) for first in range(0, width, HEAD_DIM)]

    def bring(block, carry):
        source = pl.ds(pl.multiple_of(place[block] * block_len, block_len), block_len)
        target = pl.ds(pl.multiple_of(block * block_len, block_len), block_len)
        grad_here[target, :] = grad_out[source, :]
        total_q[target, :] = out[source, :].astype(f32) * grad_out[source, :].astype(f32)
        return carry

    lax.fori_loop(0, blocks, bring, 0)
    for index in range(tiles):
        rows = slice(index * tile, (index + 1) * tile)
        keys_t[:, rows] = keys[rows, :].T
        for which, head in enumerate(columns):
            delta[which, index : index + 1, :] = jnp.sum(
                total_q[rows, head].T, axis=0, keepdims=True
            )
    total_k[...] = jnp.zeros_like(total_k)
    total_v[...] = jnp.zeros_like(total_v)

    def query_tile(index, carry):
        first = pl.multiple_of(index * tile, tile)
        here = pl.ds(first, tile)
        seg_query = seg_row[pl.ds(index, 1), :]

        def step(is_masked, at, states):
            key_first = pl.multiple_of(at * tile, tile)
            there = pl.ds(key_first, tile)
            if is_masked:
                allowed = tile_mask(seg_col[there, :], seg_query, key_first, first)
            every = [
                (
                    lax.dot_general(
                        keys[there, head], queries[here, head], NT, preferred_element_type=f32
                    ),
                    lax.dot_general(
                        values[there, head], grad_here[here, head], NT, preferred_element_type=f32
                    ),
                )
                for head in columns
            ]
            after = []
            for which, (head, running) in enumerate(zip(columns, states)):
                scores, dprobs = every[which]
                probs = jnp.exp2(scores * (scale * LOG2E) - lse[which, pl.ds(index, 1), :])
                if is_masked:
                    probs = jnp.where(allowed, probs, 0.0)
                dscores = (probs * (dprobs - delta[which, pl.ds(index, 1), :])).astype(bf16)
                total_v[there, head] += jnp.dot(
                    probs.astype(bf16), grad_here[here, head], preferred_element_type=f32
                )
                total_k[there, head] += jnp.dot(
                    dscores, queries[here, head], preferred_element_type=f32
                )
                after.append(
                    running + jnp.dot(keys_t[head, there], dscores, preferred_element_type=f32)
                )
            return after

        states = [jnp.zeros((HEAD_DIM, tile), f32) for _ in columns]
        states = lax.fori_loop(
            0, jnp.minimum(index, prompt_tiles), functools.partial(step, False), states
        )
        states = lax.fori_loop(first_tile[index], index + 1, functools.partial(step, True), states)
        for head, running in zip(columns, states):
            total_q[here, head] = running.T
        return carry

    lax.fori_loop(0, tiles, query_tile, 0)

    def send(block, carry):
        target = pl.ds(pl.multiple_of(place[block] * block_len, block_len), block_len)
        source = pl.ds(pl.multiple_of(block * block_len, block_len), block_len)
        grad_q[target, :] = total_q[source, :] * scale
        grad_k[target, :] = total_k[source, :] * scale
        grad_v[target, :] = total_v[source, :].astype(bf16)
        return carry

    lax.fori_loop(0, blocks, send, 0)


def attention_forward(
    raw, inv, gain_q, gain_k, seg_col, seg_row, place, first_tile, tile, prompt_tiles, block_len, scale
):
    group, width = raw.shape[0], raw.shape[1] // 3
    heads = width // HEAD_DIM
    tiles = group // tile

    def part(which):
        return pl.BlockSpec((group, width), lambda i, *_: (0, which), pipeline_mode=pl.Buffered(1))

    def whole(shape):
        return pl.BlockSpec(
            shape, lambda i, *_: (0,) * len(shape), pipeline_mode=pl.Buffered(1)
        )

    head = whole((group, width))
    return pl.pallas_call(
        functools.partial(forward_kernel, tile, prompt_tiles, block_len, scale),
        grid_spec=pltpu.PrefetchScalarGridSpec(
            num_scalar_prefetch=2,
            grid=(1,),
            in_specs=[
                part(0),
                part(1),
                part(2),
                whole((group, 2)),
                whole((1, width)),
                whole((1, width)),
                whole((group, 1)),
                whole((tiles, tile)),
            ],
            out_specs=[head, whole((heads, tiles, tile)), head, head, head],
            scratch_shapes=[
                pltpu.VMEM((width, group), bf16),
                pltpu.VMEM((group, width), bf16),
            ],
        ),
        out_shape=[
            jax.ShapeDtypeStruct((group, width), bf16),
            jax.ShapeDtypeStruct((heads, tiles, tile), f32),
            jax.ShapeDtypeStruct((group, width), bf16),
            jax.ShapeDtypeStruct((group, width), bf16),
            jax.ShapeDtypeStruct((group, width), bf16),
        ],
        compiler_params=pltpu.CompilerParams(vmem_limit_bytes=60 * 2**20),
        cost_estimate=pl.CostEstimate(
            flops=4 * group * group * width, bytes_accessed=24 * group * width, transcendentals=0
        ),
        name="attention_forward",
    )(place, first_tile, raw, raw, raw, inv, gain_q, gain_k, seg_col, seg_row)


def attention_backward(
    queries, keys, values, lse, out, grad_out, seg_col, seg_row, place, first_tile, tile, prompt_tiles, block_len, scale
):
    group, width = queries.shape
    heads = width // HEAD_DIM
    tiles = group // tile

    def whole(shape):
        return pl.BlockSpec(
            shape, lambda i, *_: (0,) * len(shape), pipeline_mode=pl.Buffered(1)
        )

    head = whole((group, width))
    return pl.pallas_call(
        functools.partial(backward_kernel, tile, prompt_tiles, block_len, scale),
        grid_spec=pltpu.PrefetchScalarGridSpec(
            num_scalar_prefetch=2,
            grid=(1,),
            in_specs=[
                head,
                head,
                head,
                whole((heads, tiles, tile)),
                head,
                head,
                whole((group, 1)),
                whole((tiles, tile)),
            ],
            out_specs=[head, head, head],
            scratch_shapes=[
                pltpu.VMEM((width, group), bf16),
                pltpu.VMEM((group, width), bf16),
                pltpu.VMEM((heads, tiles, tile), f32),
                pltpu.VMEM((group, width), f32),
                pltpu.VMEM((group, width), f32),
                pltpu.VMEM((group, width), f32),
            ],
        ),
        out_shape=[
            jax.ShapeDtypeStruct((group, width), f32),
            jax.ShapeDtypeStruct((group, width), f32),
            jax.ShapeDtypeStruct((group, width), bf16),
        ],
        compiler_params=pltpu.CompilerParams(vmem_limit_bytes=60 * 2**20),
        cost_estimate=pl.CostEstimate(
            flops=5 * group * group * width, bytes_accessed=24 * group * width, transcendentals=0
        ),
        name="attention_backward",
    )(place, first_tile, queries, keys, values, lse, out, grad_out, seg_col, seg_row)


def slot_table(expert_rows, order_rows, gate_rows, count_experts, capacity):
    chosen = expert_rows.T[None, :, :] == jnp.arange(count_experts, dtype=jnp.int32)[:, None, None]
    holds = jnp.any(chosen, axis=1)
    order = jnp.sum(jnp.where(chosen, order_rows.T[None], 0), axis=1)
    gate = jnp.sum(jnp.where(chosen, gate_rows.T[None], 0.0), axis=1)
    earlier = holds[:, None, :] & (order[:, None, :] < order[:, :, None])
    slot = jnp.sum(earlier.astype(jnp.int32), axis=2)
    return (jnp.where(holds & (slot < capacity), slot, -1), gate)


def barrier(*arrays):
    return lax.optimization_barrier(arrays)


class Line:
    def __init__(self):
        peers = lax.axis_size("ctx")
        self.chips = peers // 2
        self.chip = lax.axis_index("ctx") // 2
        self.peers = peers
        self.pair = [(i, i ^ 1) for i in range(peers)]
        steps = range(1, self.chips)
        every = [d for s in steps for d in (s, -s)]
        self.orders = [
            sorted((d for d in every if 0 <= z + d < self.chips), key=lambda d: (abs(d), -d))
            for z in range(self.chips)
        ]

    def step(self, turn, from_below, from_above):
        up = [(i, i + 2) for i in range(2 * (turn - 1), self.peers - 2)]
        down = [(i + 2, i) for i in range(self.peers - 2 * turn)]
        return (
            lax.ppermute(from_below, "ctx", up),
            lax.ppermute(from_above, "ctx", down),
        )

    def other(self, rows):
        return lax.ppermute(rows, "ctx", self.pair)

    def take(self, turn, arrived):
        offsets = [self.orders[z][turn - 1] for z in range(self.chips)]
        offset = jnp.array(offsets, jnp.int32)[self.chip]
        kinds = sorted(set(offsets))
        chosen = arrived[kinds[0]]
        for kind in kinds[1:]:
            chosen = jnp.where(offset == kind, arrived[kind], chosen)
        return chosen, self.chip + offset


def swap_partners(groups, shift):
    return [(i, i ^ shift) for i in range(groups)]


def swap_dp(part, shift):
    return lax.ppermute(part, "dp", swap_partners(lax.axis_size("dp"), shift))


def first_dp(part):
    return [swap_dp(part, 1), swap_dp(part, 2)]


def send_dp(part):
    return [swap_dp(part, shift) for shift in (1, 2, 3)]


def second_dp(pieces, axis):
    half = pieces[0].shape[axis] // 2
    return [
        swap_dp(lax.slice_in_dim(pieces[0], 0, half, axis=axis), 2),
        swap_dp(lax.slice_in_dim(pieces[1], half, 2 * half, axis=axis), 1),
    ]


def join_dp(part, pieces, axis):
    mine = lax.axis_index("dp")
    size = part.shape[axis]
    half = size // 2

    def both(shift):
        return [(mine ^ shift) * size, (mine ^ shift) * size + half]

    parts = [(part, both(0)), (pieces[0], both(1)), (pieces[1], both(2))]
    if len(pieces) == 3:
        parts.append((pieces[2], both(3)))
    else:
        parts += [(pieces[2], both(3)[:1]), (pieces[3], both(3)[1:])]
    return join(parts, axis, size * lax.axis_size("dp"), half)


def pick_dp(term, shift, axis):
    size = term.shape[axis] // lax.axis_size("dp")
    return lax.dynamic_slice_in_dim(term, (lax.axis_index("dp") ^ shift) * size, size, axis)


def scatter_one(term, shift, axis):
    return swap_dp(pick_dp(term, shift, axis), shift)


def total_dp(term, pieces, axis):
    groups = lax.axis_size("dp")
    size = term.shape[axis] // groups
    total = lax.dynamic_slice_in_dim(term, lax.axis_index("dp") * size, size, axis).astype(f32)
    for piece in pieces:
        total = total + piece.astype(f32)
    return total


def sum_small(array):
    peers = lax.axis_size("ctx")

    def swap(rows, shift):
        return lax.ppermute(rows, "ctx", [(i, i ^ shift) for i in range(peers)])

    array = array + swap(array, 1)
    return sum((swap(array, 2 * shift) for shift in range(1, peers // 2)), start=array)


def project_kernel(places, own, other, weight, gain, *rest):
    normed, raw, square = rest[-3:]

    def work(rows_ref):
        rows = rows_ref[...].astype(f32)
        hat = rows * lax.rsqrt(jnp.mean(rows * rows, axis=1, keepdims=True) + epsilon)
        low = (hat * gain[...]).astype(bf16)
        normed[...] = low
        product = jnp.dot(low, weight[...], preferred_element_type=f32)
        raw[...] = product
        third = product.shape[1] // 3
        for which in range(2):
            part = product[:, which * third : (which + 1) * third]
            square[which : which + 1, :] = jnp.sum((part * part).T, axis=0, keepdims=True)

    pl.when(pl.program_id(0) == 0)(lambda: work(own))
    pl.when(pl.program_id(0) == 1)(lambda: work(other))


def project(unit_index, own, other, weight, gain, peers, kept=()):
    rows, width = own.shape
    columns = weight.shape[1]

    def fixed(shape):
        return pl.BlockSpec(shape, lambda s, *_: (0,) * len(shape))

    return pl.pallas_call(
        project_kernel,
        grid_spec=pltpu.PrefetchScalarGridSpec(
            num_scalar_prefetch=1,
            grid=(2,),
            in_specs=[
                fixed((rows, width)),
                fixed((rows, width)),
                fixed((width, columns)),
                fixed((1, width)),
            ]
            + [pl.BlockSpec(memory_space=pl.ANY)] * len(kept),
            out_specs=[
                pl.BlockSpec((rows, width), lambda s, at: (at[s], 0)),
                pl.BlockSpec((rows, columns), lambda s, at: (at[s], 0)),
                pl.BlockSpec((None, 2, rows), lambda s, at: (at[s], 0, 0)),
            ],
        ),
        out_shape=[
            jax.ShapeDtypeStruct((peers * rows, width), bf16),
            jax.ShapeDtypeStruct((peers * rows, columns), f32),
            jax.ShapeDtypeStruct((peers, 2, rows), f32),
        ],
        input_output_aliases={5 + i: i for i in range(len(kept))},
        compiler_params=pltpu.CompilerParams(vmem_limit_bytes=56 * 2**20),
        name="project",
    )(unit_index, own, other, weight, gain, *kept)


def join_kernel(axis, blocks, block, at, *refs):
    out = refs[-1]
    turn = 0
    for ref, count in zip(refs[:-1], blocks):
        for index in range(count):
            here = (slice(None),) * axis + (slice(index * block, (index + 1) * block),)

            @pl.when(pl.program_id(0) == turn)
            def copy(ref=ref, here=here):
                out[...] = ref[here]

            turn += 1


def join(parts, axis, length, block):
    shape = list(parts[0][0].shape)
    shape[axis] = block
    blocks = [len(starts) for _, starts in parts]
    at = jnp.stack([start // block for _, starts in parts for start in starts]).astype(jnp.int32)
    rank = len(shape)

    def target(turn, at):
        return tuple(at[turn] if index == axis else 0 for index in range(rank))

    def fixed(part):
        return pl.BlockSpec(
            part.shape, lambda turn, at: (0,) * rank, pipeline_mode=pl.Buffered(1)
        )

    return pl.pallas_call(
        functools.partial(join_kernel, axis, blocks, block),
        grid_spec=pltpu.PrefetchScalarGridSpec(
            num_scalar_prefetch=1,
            grid=(sum(blocks),),
            in_specs=[fixed(part) for part, _ in parts],
            out_specs=pl.BlockSpec(tuple(shape), target),
        ),
        out_shape=jax.ShapeDtypeStruct(
            tuple(length if index == axis else size for index, size in enumerate(shape)),
            parts[0][0].dtype,
        ),
        compiler_params=pltpu.CompilerParams(vmem_limit_bytes=40 * 2**20),
        name="join",
    )(at, *[part for part, _ in parts])


def lay_kernel(at, own, other, *rest):
    out = rest[-1]

    def work(source):
        out[...] = source[...].astype(f32)

    pl.when(pl.program_id(0) == 0)(lambda: work(own))
    pl.when(pl.program_id(0) == 1)(lambda: work(other))


def lay(at, own, other, out_shape, block_columns, first, pieces, index, kept=()):
    block = (out_shape[0], block_columns)
    return pl.pallas_call(
        lay_kernel,
        grid_spec=pltpu.PrefetchScalarGridSpec(
            num_scalar_prefetch=1,
            grid=(2, pieces),
            in_specs=[pl.BlockSpec(block, lambda s, t, at: (0, first + t))] * 2
            + [pl.BlockSpec(memory_space=pl.ANY)] * len(kept),
            out_specs=pl.BlockSpec(block, lambda s, t, at: (0, index(at[s], t))),
        ),
        out_shape=jax.ShapeDtypeStruct(out_shape, f32),
        input_output_aliases={3: 0} if kept else {},
        name="lay",
    )(at, own, other, *kept)


def expert_kernel(
    unit, own, other, cots, slots, gates, columns, w_gate, w_up, w_down, *rest
):
    expert_in, grad_rows, hidden, grad_gate, grad_up, part, total, ready = rest[-8:]
    expert, piece = pl.program_id(0), pl.program_id(1)
    last_expert = expert == pl.num_programs(0) - 1
    last_piece = piece == pl.num_programs(1) - 1
    room, width = expert_in.shape[1:]
    rows = own.shape[0]
    core = unit[1]

    @pl.when(piece == 0)
    def bring():
        at = lax.broadcasted_iota(jnp.int32, (room, rows), 0)
        for s in range(2):
            found = at == slots[s, pl.ds(expert, 1), :]
            picks = jnp.where(found, 1.0, 0.0).astype(bf16)
            slot_gate = jnp.sum(
                jnp.where(found, gates[s, pl.ds(expert, 1), :], 0.0), axis=1, keepdims=True
            )
            grad_rows[s] = (
                jnp.dot(picks, cots[s], preferred_element_type=f32) * slot_gate
            ).astype(bf16)

            @pl.when(core == s)
            def from_own():
                expert_in[s] = jnp.dot(picks, own[...], preferred_element_type=f32).astype(bf16)

            @pl.when(core != s)
            def from_other():
                expert_in[s] = jnp.dot(picks, other[...], preferred_element_type=f32).astype(bf16)

    rows_in = expert_in[...].reshape(2 * room, width)
    gate_pre = jnp.dot(rows_in, w_gate[...], preferred_element_type=f32)
    up_pre = jnp.dot(rows_in, w_up[...], preferred_element_type=f32)
    grad_hidden = lax.dot_general(
        grad_rows[...].reshape(2 * room, width), w_down[...], NT, preferred_element_type=f32
    )
    sigmoid = 1.0 / (1.0 + jnp.exp(-gate_pre))
    silu = gate_pre * sigmoid
    hidden[...] = (silu * up_pre).astype(bf16).reshape(hidden.shape)
    gate_here = (grad_hidden * up_pre * sigmoid * (1.0 + gate_pre * (1.0 - sigmoid))).astype(bf16)
    up_here = (grad_hidden * silu).astype(bf16)
    grad_gate[...] = gate_here.reshape(grad_gate.shape)
    grad_up[...] = up_here.reshape(grad_up.shape)

    def back():
        return lax.dot_general(gate_here, w_gate[...], NT, preferred_element_type=f32) + lax.dot_general(
            up_here, w_up[...], NT, preferred_element_type=f32
        )

    @pl.when(piece == 0)
    def first():
        total[...] = back()

    @pl.when(piece != 0)
    def later():
        total[...] += back()

    @pl.when(last_piece)
    def keep():
        for s in range(2):
            ready[s, pl.ds(pl.multiple_of(expert * room, 16), room), :] = total[
                s * room : (s + 1) * room, :
            ].astype(bf16)

    @pl.when(last_piece & last_expert)
    def send():
        for s in range(2):
            at = lax.broadcasted_iota(jnp.int32, (rows, ready.shape[1]), 1)
            here = columns[s]
            found = at == here[:, 0:1]
            for e in range(1, here.shape[1]):
                found = found | (at == here[:, e : e + 1])
            part[s] = jnp.dot(
                jnp.where(found, 1.0, 0.0).astype(bf16), ready[s], preferred_element_type=f32
            ).astype(bf16)


def expert_unit(unit, own, other, cot_all, slots, gates, columns, w_gate, w_up, w_down, room, kept=(), piece=256):
    rows, width = own.shape
    experts, _, inner = w_gate.shape
    peers = cot_all.shape[0]
    wide_shape = (peers, experts, room, width)
    thin_shape = (peers, experts, room, inner)
    anywhere = pl.BlockSpec(memory_space=pl.ANY)
    once = pl.Buffered(1)

    def fixed(shape):
        return pl.BlockSpec(shape, lambda e, f, u: (0,) * len(shape), pipeline_mode=once)

    def chip(shape):
        return pl.BlockSpec((2, *shape), lambda e, f, u: (u[0], 0, 0), pipeline_mode=once)

    wide = pl.BlockSpec((2, None, room, width), lambda e, f, u: (u[0], e, 0, 0))
    thin = pl.BlockSpec((2, None, room, piece), lambda e, f, u: (u[0], e, 0, f))
    return pl.pallas_call(
        expert_kernel,
        grid_spec=pltpu.PrefetchScalarGridSpec(
            num_scalar_prefetch=1,
            grid=(experts, inner // piece),
            in_specs=[
                fixed((rows, width)), fixed((rows, width)), chip((rows, width)),
                chip((experts, rows)), chip((experts, rows)), chip((rows, experts)),
                pl.BlockSpec((None, width, piece), lambda e, f, u: (e, 0, f)),
                pl.BlockSpec((None, width, piece), lambda e, f, u: (e, 0, f)),
                pl.BlockSpec((None, piece, width), lambda e, f, u: (e, f, 0)),
            ] + [anywhere] * len(kept),
            out_specs=[wide, wide, thin, thin, thin,
                pl.BlockSpec((2, rows, width), lambda e, f, u: (u[0], 0, 0))],
            scratch_shapes=[
                pltpu.VMEM((2 * room, width), f32),
                pltpu.VMEM((2, experts * room, width), bf16),
            ],
        ),
        out_shape=[
            jax.ShapeDtypeStruct(shape, bf16)
            for shape in [wide_shape] * 2 + [thin_shape] * 3 + [cot_all.shape]
        ],
        input_output_aliases={10 + i: i for i in range(len(kept))},
        compiler_params=pltpu.CompilerParams(vmem_limit_bytes=60 * 2**20),
        name="expert_unit",
    )(unit, own, other, cot_all, slots, gates, columns, w_gate, w_up, w_down, *kept)


def out_kernel(hidden, w_down, slots, gates, columns, part, ready):
    expert = pl.program_id(1)
    room = hidden.shape[1]
    rows = slots.shape[2]
    at = lax.broadcasted_iota(jnp.int32, (room, rows), 0)
    product = jnp.dot(
        hidden[...].reshape(2 * room, hidden.shape[2]), w_down[...], preferred_element_type=f32
    )
    for s in range(2):
        found = at == slots[s, pl.ds(expert, 1), :]
        slot_gate = jnp.sum(jnp.where(found, gates[s, pl.ds(expert, 1), :], 0.0), axis=1, keepdims=True)
        ready[s, pl.ds(pl.multiple_of(expert * room, 16), room), :] = (
            product[s * room : (s + 1) * room] * slot_gate
        ).astype(bf16)

    @pl.when(expert == pl.num_programs(1) - 1)
    def send():
        for s in range(2):
            at = lax.broadcasted_iota(jnp.int32, (rows, ready.shape[1]), 1)
            here = columns[s]
            found = at == here[:, 0:1]
            for e in range(1, here.shape[1]):
                found = found | (at == here[:, e : e + 1])
            part[s] = jnp.dot(
                jnp.where(found, 1.0, 0.0).astype(bf16), ready[s], preferred_element_type=f32
            ).astype(bf16)


def expert_out(hidden, w_down, slots, gates, columns):
    peers, experts, room, inner = hidden.shape
    width = w_down.shape[2]
    rows = slots.shape[2]
    return pl.pallas_call(
        out_kernel,
        grid=(peers // 2, experts),
        in_specs=[
            pl.BlockSpec((2, None, room, inner), lambda c, e: (c, e, 0, 0)),
            pl.BlockSpec((None, inner, width), lambda c, e: (e, 0, 0)),
            pl.BlockSpec((2, experts, rows), lambda c, e: (c, 0, 0)),
            pl.BlockSpec((2, experts, rows), lambda c, e: (c, 0, 0)),
            pl.BlockSpec((2, rows, experts), lambda c, e: (c, 0, 0)),
        ],
        out_specs=pl.BlockSpec((2, rows, width), lambda c, e: (c, 0, 0)),
        out_shape=jax.ShapeDtypeStruct((peers, rows, width), bf16),
        scratch_shapes=[pltpu.VMEM((2, experts * room, width), bf16)],
        compiler_params=pltpu.CompilerParams(vmem_limit_bytes=60 * 2**20),
        name="expert_out",
    )(hidden, w_down, slots, gates, columns)


def on_device(
    tokens,
    cotangent,
    wqkv,
    wo,
    attn_gain,
    query_gain,
    key_gain,
    moe_gain,
    w_gate,
    w_up,
    w_down,
    expert_ids,
    gates,
    slot_order,
    block_assign,
    segment_ids,
):
    count_rows, width = tokens.shape
    head_dim = width // HEADS
    scale = head_dim ** (-0.5)
    peers = lax.axis_size("ctx")
    groups = lax.axis_size("dp")
    me = lax.axis_index("ctx")
    core = me % 2
    my_dp = lax.axis_index("dp")
    group_rows = count_rows * peers
    rep = max(1, peers // HEADS)
    own_heads = max(1, HEADS // peers)
    own_width = own_heads * head_dim
    first_head = (me // rep) * own_heads
    block_len = count_rows // BLK_DEV
    tile = 512
    line = Line()
    turns = range(1, line.chips)

    assign = block_assign[0]
    count_blocks = assign.shape[0]
    place = jnp.argmax(
        assign[None, :] == jnp.arange(count_blocks, dtype=jnp.int32)[:, None], axis=1
    ).astype(jnp.int32)
    cont = segment_ids[0]
    prompt_len = group_rows - cont.shape[0]
    prompt_tiles = prompt_len // tile
    seg_logical = jnp.concatenate([jnp.full((prompt_len,), -1, jnp.int32), cont])
    tiles = group_rows // tile
    tile_seg = seg_logical.reshape(tiles, tile)[:, 0]
    first_tile = jnp.where(
        tile_seg < 0,
        jnp.arange(tiles, dtype=jnp.int32),
        jnp.sum((seg_logical[None, :] < tile_seg[:, None]).astype(jnp.int32), axis=1) // tile,
    ).astype(jnp.int32)
    seg_col = seg_logical[:, None]
    seg_row = seg_logical.reshape(tiles, tile)

    local_experts = w_gate.shape[0]
    count_experts = local_experts * peers
    capacity = 9 * count_rows * TOP // (8 * count_experts)
    room = (capacity + 15) // 16 * 16
    slot, gate = slot_table(expert_ids, slot_order, gates, count_experts, capacity)
    table = jnp.stack(
        [
            slot.reshape(peers, local_experts, count_rows).astype(f32),
            gate.reshape(peers, local_experts, count_rows),
        ],
        axis=1,
    )

    inputs = tokens.astype(f32)
    below, above = line.step(1, tokens, tokens)
    other = line.other(tokens)
    w_part = jnp.concatenate(
        [
            lax.dynamic_slice_in_dim(wqkv, which * width + first_head * head_dim, own_width, 1)
            for which in range(3)
        ],
        axis=1,
    )
    w_pieces = send_dp(w_part)
    gain_part = jnp.stack([attn_gain, query_gain, key_gain, moe_gain])
    gain_all = jnp.zeros((4, width), bf16)
    for shift in range(groups):
        piece = swap_dp(gain_part, shift) if shift else gain_part
        gain_all = lax.dynamic_update_slice_in_dim(
            gain_all, piece, (my_dp ^ shift) * gain_part.shape[1], 1
        )
    gain_all = gain_all.astype(f32)
    below, above, other, gain_all, table, wo, w_gate, *w_pieces = barrier(
        below, above, other, gain_all, table, wo, w_gate, *w_pieces
    )
    full_gate = lax.all_gather(w_gate, "dp", axis=1, tiled=True)
    w_own = join_dp(w_part, w_pieces, 0)
    gain_attn, gain_moe = gain_all[0:1], gain_all[3:4]
    gain_own = lax.dynamic_slice_in_dim(gain_all, first_head * head_dim, own_width, 1)
    gain_q, gain_k = gain_own[1:2], gain_own[2:3]

    half_rows = wo.shape[0] // 2
    arrived = {-1: below, 1: above}
    own, chip = tokens, line.chip
    kept, travelled = (), ()
    for turn in turns:
        if turn + 1 < line.chips:
            below, above = line.step(turn + 1, below, above)
            arrived[-turn - 1], arrived[turn + 1] = below, above
        if turn + 1 == line.chips:
            cotangent_now, arrived[turn] = barrier(cotangent, arrived[turn])
        next_own, next_chip = line.take(turn, arrived)
        next_other = line.other(next_own)
        at = jnp.stack([2 * chip + core, 2 * chip + 1 - core]).astype(jnp.int32)
        kept = project(at, own, other, w_own, gain_attn, peers, kept)
        travel = list(travelled)
        if turn == 2:
            wo_half = lax.dynamic_slice_in_dim(wo, core * half_rows, half_rows, 0)
            travel = first_dp(wo_half)
        own, other, chip = next_own, next_other, next_chip
        square = kept[2]
        below, above, own, other, square, w_down, *travelled = barrier(
            below, above, own, other, square, w_down, *travel
        )
        kept = (kept[0], kept[1], square)
        if turn + 1 < line.chips:
            arrived[-turn - 1], arrived[turn + 1] = below, above
    cot_all = lax.all_gather(cotangent_now, "ctx", axis=0, tiled=True).reshape(
        peers, count_rows, width
    )
    down_pieces = first_dp(w_down)
    wo_pieces = [wo_half, *travelled[:2]]
    table = lax.all_to_all(table, "ctx", split_axis=0, concat_axis=0, tiled=True)
    at = jnp.stack([2 * chip + core, 2 * chip + 1 - core]).astype(jnp.int32)
    normed_all, raw, square = project(at, own, other, w_own, gain_attn, peers, kept)
    square = sum_small(square.transpose(1, 0, 2).reshape(2, group_rows)) * (1.0 / rep)
    inv_qk = lax.rsqrt(square / width + epsilon).T
    slot = table[:, 0].astype(jnp.int32)
    gate_rows = table[:, 1]
    offsets = (jnp.arange(local_experts, dtype=jnp.int32) * room)[None, :, None]
    columns = jnp.where(slot >= 0, slot + offsets, -1).transpose(0, 2, 1)

    inv_qk, w_up, slot, gate_rows, columns, full_gate, wo_half, *down_pieces = barrier(
        inv_qk, w_up, slot, gate_rows, columns, full_gate, wo_half, *down_pieces
    )
    wo_pieces.append(swap_dp(wo_half, 3))
    up_pieces = first_dp(w_up)
    attended, lse, queries, keys, values = attention_forward(
        raw,
        inv_qk,
        gain_q,
        gain_k,
        seg_col,
        seg_row,
        place,
        first_tile,
        tile,
        prompt_tiles,
        block_len,
        scale,
    )
    attended, wo_pieces[3], *up_pieces = barrier(attended, wo_pieces[3], *up_pieces)
    wo_mine = jnp.concatenate(wo_pieces, axis=0)
    wo_theirs = line.other(wo_mine)
    down_pieces = down_pieces + second_dp(down_pieces, 1)
    up_pieces = up_pieces + second_dp(up_pieces, 1)
    attn_low = lax.all_to_all(
        attended.reshape(peers, count_rows, own_width), "ctx", split_axis=0, concat_axis=0, tiled=True
    )[::rep]
    starts = [(my_dp ^ shift) * wo.shape[0] for shift in range(groups)]
    full_wo = join(
        [
            (wo_mine, [start + core * half_rows for start in starts]),
            (wo_theirs, [start + (1 - core) * half_rows for start in starts]),
        ],
        0,
        width,
        half_rows,
    )
    full_down = join_dp(w_down, down_pieces, 1)
    attn_low, full_wo, full_down = barrier(attn_low, full_wo, full_down)
    attn_low = attn_low.transpose(1, 0, 2).reshape(count_rows, width)
    state = inputs + jnp.dot(attn_low, full_wo, preferred_element_type=f32)
    inv_state = rms_scale(state)
    hat_state = state * inv_state
    normed_moe = (hat_state * gain_moe).astype(bf16)

    normed_moe, cot_all, *up_pieces = barrier(normed_moe, cot_all, *up_pieces)
    full_up = join_dp(w_up, up_pieces, 1)
    below, above = normed_moe, normed_moe
    own, chip = normed_moe, line.chip
    arrived = {}
    kept = ()
    for turn in range(line.chips):
        if turn + 1 < line.chips:
            below, above = line.step(turn + 1, below, above)
            arrived[-turn - 1], arrived[turn + 1] = below, above
        if turn > 0:
            own, chip = line.take(turn, arrived)
        other = line.other(own)
        kept = expert_unit(
            jnp.stack([chip, core]).astype(jnp.int32),
            own,
            other,
            cot_all,
            slot,
            gate_rows,
            columns,
            full_gate,
            full_up,
            full_down,
            room,
            kept,
        )
        if turn + 1 < line.chips:
            below, above, *kept = barrier(below, above, *kept)
            arrived[-turn - 1], arrived[turn + 1] = below, above
    expert_in, grad_rows, hidden, grad_gate_pre, grad_up_pre, part_moe = kept
    grad_normed_moe = lax.psum_scatter(
        part_moe.reshape(group_rows, width), "ctx", scatter_dimension=0, tiled=True
    )

    part_mixed = expert_out(hidden, full_down, slot, gate_rows, columns)
    grad_down = jnp.einsum("sncf,sncd->nfd", hidden, grad_rows, preferred_element_type=f32)
    grad_down = grad_down.astype(bf16)
    part_mixed, grad_down, expert_in = barrier(part_mixed, grad_down, expert_in)
    down_pieces = [scatter_one(grad_down, shift, 1) for shift in (1, 2, 3)]
    grad_gate = jnp.einsum("sncd,sncf->ndf", expert_in, grad_gate_pre, preferred_element_type=f32)
    grad_up = jnp.einsum("sncd,sncf->ndf", expert_in, grad_up_pre, preferred_element_type=f32)
    grad_gate, grad_up = grad_gate.astype(bf16), grad_up.astype(bf16)
    grad_normed_moe, part_mixed, grad_gate, grad_up, *down_pieces = barrier(
        grad_normed_moe, part_mixed, grad_gate, grad_up, *down_pieces
    )
    mixed = lax.psum_scatter(
        part_mixed.reshape(group_rows, width), "ctx", scatter_dimension=0, tiled=True
    )

    gate_pieces = [scatter_one(grad_gate, shift, 1) for shift in (1, 2)]
    grad_normed_moe = grad_normed_moe.astype(f32)
    moe_gain_term = jnp.sum(grad_normed_moe * hat_state, axis=0)
    grad_state = cotangent.astype(f32) + rms_back(grad_normed_moe * gain_moe, hat_state, inv_state)
    grad_branch = grad_state.astype(bf16)
    grad_attn = lax.dot_general(grad_branch, full_wo, NT, preferred_element_type=f32).astype(bf16)
    grad_attn = grad_attn.reshape(count_rows, peers // rep, own_width).transpose(1, 0, 2)
    grad_attn = jnp.repeat(grad_attn, rep, axis=0)
    grad_attended = lax.all_to_all(
        grad_attn, "ctx", split_axis=0, concat_axis=0, tiled=True
    ).reshape(group_rows, own_width)
    part_out = lax.dot_general(attn_low, grad_branch, TN, preferred_element_type=f32).astype(bf16)
    half = width // 2
    out_theirs = line.other(lax.dynamic_slice_in_dim(part_out, (1 - core) * half, half, 1))
    part_out = lax.dynamic_slice_in_dim(part_out, core * half, half, 1).astype(f32)
    part_out = (part_out + out_theirs.astype(f32)).astype(bf16)
    out_pieces = [scatter_one(part_out, shift, 0) for shift in (1, 2)]
    down_sum = total_dp(grad_down, down_pieces, 1)
    grad_attended, part_out, down_sum, grad_gate, *pieces = barrier(
        grad_attended, part_out, down_sum, grad_gate, *gate_pieces, *out_pieces
    )
    gate_pieces, out_pieces = pieces[:2], pieces[2:]
    out_pieces.append(scatter_one(part_out, 3, 0))
    gate_pieces.append(scatter_one(grad_gate, 3, 1))
    grad_q, grad_k, grad_v = attention_backward(
        queries,
        keys,
        values,
        lse,
        attended,
        grad_attended,
        seg_col,
        seg_row,
        place,
        first_tile,
        tile,
        prompt_tiles,
        block_len,
        scale,
    )
    grad_q, out_pieces[2], gate_pieces[2] = barrier(grad_q, out_pieces[2], gate_pieces[2])
    out_sum = total_dp(part_out, out_pieces, 0).astype(bf16)
    rows_dp = out_sum.shape[0]
    share = half // line.chips
    out_sum = out_sum.reshape(rows_dp, line.chips, share).transpose(1, 0, 2)
    hat_q = raw[:, :own_width] * inv_qk[:, 0:1]
    hat_k = raw[:, own_width : 2 * own_width] * inv_qk[:, 1:2]
    query_gain_term = jnp.sum(grad_q * hat_q, axis=0)
    key_gain_term = jnp.sum(grad_k * hat_k, axis=0)
    means = jnp.stack(
        [
            jnp.sum(grad_q * gain_q * hat_q, axis=1),
            jnp.sum(grad_k * gain_k * hat_k, axis=1),
        ]
    )
    means = (sum_small(means) * (1.0 / (rep * width))).T
    grad_raw_q = inv_qk[:, 0:1] * (grad_q * gain_q - hat_q * means[:, 0:1])
    grad_raw_k = inv_qk[:, 1:2] * (grad_k * gain_k - hat_k * means[:, 1:2])
    grad_qkv = jnp.concatenate([grad_raw_q.astype(bf16), grad_raw_k.astype(bf16), grad_v], axis=1)
    part_normed = lax.dot_general(grad_qkv, w_own, NT, preferred_element_type=f32) * (1.0 / rep)
    part_normed = part_normed.astype(bf16)
    part_normed, mixed, grad_up, out_sum = barrier(part_normed, mixed, grad_up, out_sum)
    grad_normed = lax.psum_scatter(part_normed, "ctx", scatter_dimension=0, tiled=True)

    out_sum = lax.all_to_all(
        out_sum,
        "ctx",
        split_axis=0,
        concat_axis=0,
        tiled=True,
        axis_index_groups=[[2 * z + c for z in range(peers // 2)] for c in range(2)],
    )
    part_qkv = lax.dot_general(normed_all, grad_qkv, TN, preferred_element_type=f32).astype(bf16)
    qkv_pieces = [scatter_one(part_qkv, shift, 0) for shift in (1, 2, 3)]
    own_terms = jnp.stack([query_gain_term, key_gain_term]) * (1.0 / rep)
    spread = lax.dynamic_update_slice_in_dim(
        jnp.zeros((2, width), f32), own_terms, first_head * head_dim, 1
    )
    attn_gain_term = (
        jnp.sum(part_normed.astype(f32) * normed_all.astype(f32), axis=0) / gain_attn[0]
    )
    gain_terms = jnp.concatenate([attn_gain_term[None], spread, moe_gain_term[None]], axis=0)
    gain_pieces = [scatter_one(gain_terms, shift, 1) for shift in (1, 2, 3)]
    output = (state + mixed.astype(f32)).astype(bf16)
    out_sum, gain_terms, grad_up, output, *pieces = barrier(
        out_sum, gain_terms, grad_up, output, *qkv_pieces, *gain_pieces
    )
    qkv_pieces, gain_pieces = pieces[:3], pieces[3:]
    gate_sum = total_dp(grad_gate, gate_pieces, 1)
    gain_terms = total_dp(gain_terms, gain_pieces, 1)
    qkv_sum = total_dp(part_qkv, qkv_pieces, 0).astype(bf16)
    out_sum = jnp.sum(out_sum.astype(f32), axis=0).astype(bf16)
    own, chip = jnp.concatenate([qkv_sum, out_sum], axis=1), line.chip
    gain_shape = gain_terms.shape
    row = own.shape[1]
    gain_terms = gain_terms.reshape(-1)
    gain_rows = (gain_terms.size // row + 16) // 16 * 16
    gain_size = gain_terms.size
    gain_terms = jnp.pad(gain_terms, (0, gain_rows * row - gain_size)).reshape(gain_rows, row)
    own = jnp.concatenate([own, gain_terms.astype(bf16)], axis=0)
    gain_terms = jnp.zeros((gain_rows, row), f32)
    below, above = own, own
    arrived = {}
    qkv_kept, out_kept = (), ()
    for turn in range(line.chips):
        if turn + 1 < line.chips:
            below, above = line.step(turn + 1, below, above)
        if turn > 0:
            own, chip = line.take(turn, arrived)
        other = line.other(own)
        gain_terms = gain_terms + own[rows_dp:].astype(f32) + other[rows_dp:].astype(f32)
        at = jnp.stack([2 * chip + core, 2 * chip + 1 - core]).astype(jnp.int32) // rep
        qkv_kept = [
            lay(
                at,
                own,
                other,
                (rows_dp, 3 * width),
                own_width,
                0,
                3,
                lambda p, t: t * (width // own_width) + p,
                qkv_kept,
            )
        ]
        at = jnp.stack([core * line.chips + chip, (1 - core) * line.chips + chip]).astype(jnp.int32)
        if share % HEAD_DIM == 0 and 3 * own_width % share == 0:
            out_kept = [
                lay(
                    at,
                    own,
                    other,
                    (rows_dp, width),
                    share,
                    3 * own_width // share,
                    1,
                    lambda p, t: p,
                    out_kept,
                )
            ]
        else:
            out_kept = list(out_kept) or [jnp.zeros((rows_dp, width), f32)]
            for which, part in enumerate((own, other)):
                out_kept[0] = lax.dynamic_update_slice_in_dim(
                    out_kept[0], part[:rows_dp, 3 * own_width :].astype(f32), at[which] * share, 1
                )
        if turn == 0:
            up_pieces = [scatter_one(grad_up, shift, 1) for shift in (1, 2)]
        if turn == 1:
            up_pieces.append(scatter_one(grad_up, 3, 1))
        if turn == 2:
            grad_up = total_dp(grad_up, up_pieces, 1)
            up_pieces = []
        if turn + 1 < line.chips:
            below, above, qkv_kept[0], out_kept[0], grad_up, gate_sum, *up_pieces = barrier(
                below, above, qkv_kept[0], out_kept[0], grad_up, gate_sum, *up_pieces
            )
            arrived[-turn - 1], arrived[turn + 1] = below, above
    qkv_total, out_total = qkv_kept[0], out_kept[0]
    up_sum = grad_up
    gain_terms = gain_terms.reshape(-1)[:gain_size].reshape(gain_shape)
    out_total, qkv_total, up_sum, output, gain_terms, grad_normed = barrier(
        out_total, qkv_total, up_sum, output, gain_terms, grad_normed
    )

    grad_normed = grad_normed.astype(f32)
    inv_in = rms_scale(inputs)
    hat_in = inputs * inv_in
    input_grad = (grad_state + rms_back(grad_normed * gain_attn, hat_in, inv_in)).astype(bf16)
    return (
        output,
        input_grad,
        qkv_total,
        out_total,
        gain_terms[0],
        gain_terms[1],
        gain_terms[2],
        gain_terms[3],
        gate_sum,
        up_sum,
        down_sum,
    )


def solution(mesh):
    rows = P(("dp", "ctx"), None)
    expert = P("ctx", "dp", None)
    by_dp = P("dp", None)
    return jax.shard_map(
        on_device,
        mesh=mesh,
        in_specs=(
            rows,
            rows,
            by_dp,
            by_dp,
            P("dp"),
            P("dp"),
            P("dp"),
            P("dp"),
            expert,
            expert,
            expert,
            rows,
            rows,
            rows,
            by_dp,
            by_dp,
        ),
        out_specs=(
            rows,
            rows,
            by_dp,
            by_dp,
            P("dp"),
            P("dp"),
            P("dp"),
            P("dp"),
            expert,
            expert,
            expert,
        ),
        check_vma=False,
    )
```

```python
import functools

import jax
import jax.numpy as jnp
from jax import lax
from jax.experimental import pallas as pl
from jax.experimental.pallas import tpu as pltpu
from jax.sharding import PartitionSpec as P

HEADS = 16
TOP = 8
BLK_DEV = 2
LOG2E = 1.4426950408889634
HEAD_DIM = 128

epsilon = 1e-06
masked_value = -1e30
f32 = jnp.float32
bf16 = jnp.bfloat16
NT = (((1,), (1,)), ((), ()))
TN = (((0,), (0,)), ((), ()))


def rms_scale(values_in):
    return lax.rsqrt(jnp.mean(values_in * values_in, axis=-1, keepdims=True) + epsilon)


def rms_back(grad_hat, normed, scale_rows):
    return scale_rows * (grad_hat - normed * jnp.mean(grad_hat * normed, axis=-1, keepdims=True))


def tile_mask(seg_col, seg_row, key_first, query_first):
    rows, columns = seg_col.shape[0], seg_row.shape[1]
    key_pos = key_first + lax.broadcasted_iota(jnp.int32, (rows, columns), 0)
    query_pos = query_first + lax.broadcasted_iota(jnp.int32, (rows, columns), 1)
    return (seg_col == seg_row) & (key_pos <= query_pos)


def forward_kernel(
    tile,
    prompt_tiles,
    block_len,
    scale,
    place,
    first_tile,
    raw_q,
    raw_k,
    raw_v,
    inv,
    gain_q,
    gain_k,
    seg_col,
    seg_row,
    out,
    lse,
    queries,
    keys,
    values,
    values_t,
    out_logical,
):
    group, width = raw_q.shape
    tiles = group // tile
    blocks = group // block_len
    columns = [slice(first, first + HEAD_DIM) for first in range(0, width, HEAD_DIM)]

    def bring(block, carry):
        source = pl.ds(pl.multiple_of(place[block] * block_len, block_len), block_len)
        target = pl.ds(pl.multiple_of(block * block_len, block_len), block_len)
        scales = inv[source, :]
        queries[target, :] = (raw_q[source, :] * scales[:, 0:1] * gain_q[...]).astype(bf16)
        keys[target, :] = (raw_k[source, :] * scales[:, 1:2] * gain_k[...]).astype(bf16)
        values[target, :] = raw_v[source, :].astype(bf16)
        return carry

    lax.fori_loop(0, blocks, bring, 0)
    for index in range(tiles):
        values_t[:, index * tile : (index + 1) * tile] = values[
            index * tile : (index + 1) * tile, :
        ].T

    def query_tile(index, carry):
        first = pl.multiple_of(index * tile, tile)
        here = pl.ds(first, tile)
        seg_query = seg_row[pl.ds(index, 1), :]

        def step(is_masked, at, states):
            key_first = pl.multiple_of(at * tile, tile)
            there = pl.ds(key_first, tile)
            if is_masked:
                allowed = tile_mask(seg_col[there, :], seg_query, key_first, first)
            every = [
                lax.dot_general(
                    keys[there, head], queries[here, head], NT, preferred_element_type=f32
                )
                for head in columns
            ]
            after = []
            for scores, head, (largest, total, running) in zip(every, columns, states):
                scores = scores * (scale * LOG2E)
                if is_masked:
                    scores = jnp.where(allowed, scores, masked_value)
                new_largest = jnp.maximum(largest, jnp.max(scores, axis=0, keepdims=True))
                shrink = jnp.exp2(largest - new_largest)
                terms = jnp.exp2(scores - new_largest)
                total = total * shrink + jnp.sum(terms, axis=0, keepdims=True)
                running = running * shrink + jnp.dot(
                    values_t[head, there], terms.astype(bf16), preferred_element_type=f32
                )
                after.append((new_largest, total, running))
            return after

        states = [
            (
                jnp.full((1, tile), masked_value, f32),
                jnp.zeros((1, tile), f32),
                jnp.zeros((HEAD_DIM, tile), f32),
            )
            for _ in columns
        ]
        states = lax.fori_loop(
            0, jnp.minimum(index, prompt_tiles), functools.partial(step, False), states
        )
        states = lax.fori_loop(first_tile[index], index + 1, functools.partial(step, True), states)
        for which, (head, (largest, total, running)) in enumerate(zip(columns, states)):
            lse[which, pl.ds(index, 1), :] = largest + jnp.log2(total)
            out_logical[here, head] = (running / total).T.astype(bf16)
        return carry

    lax.fori_loop(0, tiles, query_tile, 0)

    def send(block, carry):
        target = pl.ds(pl.multiple_of(place[block] * block_len, block_len), block_len)
        source = pl.ds(pl.multiple_of(block * block_len, block_len), block_len)
        out[target, :] = out_logical[source, :]
        return carry

    lax.fori_loop(0, blocks, send, 0)


def backward_kernel(
    tile,
    prompt_tiles,
    block_len,
    scale,
    place,
    first_tile,
    queries,
    keys,
    values,
    lse,
    out,
    grad_out,
    seg_col,
    seg_row,
    grad_q,
    grad_k,
    grad_v,
    keys_t,
    grad_here,
    delta,
    total_q,
    total_k,
    total_v,
):
    group, width = queries.shape
    tiles = group // tile
    blocks = group // block_len
    columns = [slice(first, first + HEAD_DIM) for first in range(0, width, HEAD_DIM)]

    def bring(block, carry):
        source = pl.ds(pl.multiple_of(place[block] * block_len, block_len), block_len)
        target = pl.ds(pl.multiple_of(block * block_len, block_len), block_len)
        grad_here[target, :] = grad_out[source, :]
        total_q[target, :] = out[source, :].astype(f32) * grad_out[source, :].astype(f32)
        return carry

    lax.fori_loop(0, blocks, bring, 0)
    for index in range(tiles):
        rows = slice(index * tile, (index + 1) * tile)
        keys_t[:, rows] = keys[rows, :].T
        for which, head in enumerate(columns):
            delta[which, index : index + 1, :] = jnp.sum(
                total_q[rows, head].T, axis=0, keepdims=True
            )
    total_k[...] = jnp.zeros_like(total_k)
    total_v[...] = jnp.zeros_like(total_v)

    def query_tile(index, carry):
        first = pl.multiple_of(index * tile, tile)
        here = pl.ds(first, tile)
        seg_query = seg_row[pl.ds(index, 1), :]

        def step(is_masked, at, states):
            key_first = pl.multiple_of(at * tile, tile)
            there = pl.ds(key_first, tile)
            if is_masked:
                allowed = tile_mask(seg_col[there, :], seg_query, key_first, first)
            every = [
                (
                    lax.dot_general(
                        keys[there, head], queries[here, head], NT, preferred_element_type=f32
                    ),
                    lax.dot_general(
                        values[there, head], grad_here[here, head], NT, preferred_element_type=f32
                    ),
                )
                for head in columns
            ]
            after = []
            for which, (head, running) in enumerate(zip(columns, states)):
                scores, dprobs = every[which]
                probs = jnp.exp2(scores * (scale * LOG2E) - lse[which, pl.ds(index, 1), :])
                if is_masked:
                    probs = jnp.where(allowed, probs, 0.0)
                dscores = (probs * (dprobs - delta[which, pl.ds(index, 1), :])).astype(bf16)
                total_v[there, head] += jnp.dot(
                    probs.astype(bf16), grad_here[here, head], preferred_element_type=f32
                )
                total_k[there, head] += jnp.dot(
                    dscores, queries[here, head], preferred_element_type=f32
                )
                after.append(
                    running + jnp.dot(keys_t[head, there], dscores, preferred_element_type=f32)
                )
            return after

        states = [jnp.zeros((HEAD_DIM, tile), f32) for _ in columns]
        states = lax.fori_loop(
            0, jnp.minimum(index, prompt_tiles), functools.partial(step, False), states
        )
        states = lax.fori_loop(first_tile[index], index + 1, functools.partial(step, True), states)
        for head, running in zip(columns, states):
            total_q[here, head] = running.T
        return carry

    lax.fori_loop(0, tiles, query_tile, 0)

    def send(block, carry):
        target = pl.ds(pl.multiple_of(place[block] * block_len, block_len), block_len)
        source = pl.ds(pl.multiple_of(block * block_len, block_len), block_len)
        grad_q[target, :] = total_q[source, :] * scale
        grad_k[target, :] = total_k[source, :] * scale
        grad_v[target, :] = total_v[source, :].astype(bf16)
        return carry

    lax.fori_loop(0, blocks, send, 0)


def attention_forward(
    raw, inv, gain_q, gain_k, seg_col, seg_row, place, first_tile, tile, prompt_tiles, block_len, scale
):
    group, width = raw.shape[0], raw.shape[1] // 3
    heads = width // HEAD_DIM
    tiles = group // tile

    def part(which):
        return pl.BlockSpec((group, width), lambda i, *_: (0, which), pipeline_mode=pl.Buffered(1))

    def whole(shape):
        return pl.BlockSpec(
            shape, lambda i, *_: (0,) * len(shape), pipeline_mode=pl.Buffered(1)
        )

    head = whole((group, width))
    return pl.pallas_call(
        functools.partial(forward_kernel, tile, prompt_tiles, block_len, scale),
        grid_spec=pltpu.PrefetchScalarGridSpec(
            num_scalar_prefetch=2,
            grid=(1,),
            in_specs=[
                part(0),
                part(1),
                part(2),
                whole((group, 2)),
                whole((1, width)),
                whole((1, width)),
                whole((group, 1)),
                whole((tiles, tile)),
            ],
            out_specs=[head, whole((heads, tiles, tile)), head, head, head],
            scratch_shapes=[
                pltpu.VMEM((width, group), bf16),
                pltpu.VMEM((group, width), bf16),
            ],
        ),
        out_shape=[
            jax.ShapeDtypeStruct((group, width), bf16),
            jax.ShapeDtypeStruct((heads, tiles, tile), f32),
            jax.ShapeDtypeStruct((group, width), bf16),
            jax.ShapeDtypeStruct((group, width), bf16),
            jax.ShapeDtypeStruct((group, width), bf16),
        ],
        compiler_params=pltpu.CompilerParams(vmem_limit_bytes=60 * 2**20),
        cost_estimate=pl.CostEstimate(
            flops=4 * group * group * width, bytes_accessed=24 * group * width, transcendentals=0
        ),
        name="attention_forward",
    )(place, first_tile, raw, raw, raw, inv, gain_q, gain_k, seg_col, seg_row)


def attention_backward(
    queries, keys, values, lse, out, grad_out, seg_col, seg_row, place, first_tile, tile, prompt_tiles, block_len, scale
):
    group, width = queries.shape
    heads = width // HEAD_DIM
    tiles = group // tile

    def whole(shape):
        return pl.BlockSpec(
            shape, lambda i, *_: (0,) * len(shape), pipeline_mode=pl.Buffered(1)
        )

    head = whole((group, width))
    return pl.pallas_call(
        functools.partial(backward_kernel, tile, prompt_tiles, block_len, scale),
        grid_spec=pltpu.PrefetchScalarGridSpec(
            num_scalar_prefetch=2,
            grid=(1,),
            in_specs=[
                head,
                head,
                head,
                whole((heads, tiles, tile)),
                head,
                head,
                whole((group, 1)),
                whole((tiles, tile)),
            ],
            out_specs=[head, head, head],
            scratch_shapes=[
                pltpu.VMEM((width, group), bf16),
                pltpu.VMEM((group, width), bf16),
                pltpu.VMEM((heads, tiles, tile), f32),
                pltpu.VMEM((group, width), f32),
                pltpu.VMEM((group, width), f32),
                pltpu.VMEM((group, width), f32),
            ],
        ),
        out_shape=[
            jax.ShapeDtypeStruct((group, width), f32),
            jax.ShapeDtypeStruct((group, width), f32),
            jax.ShapeDtypeStruct((group, width), bf16),
        ],
        compiler_params=pltpu.CompilerParams(vmem_limit_bytes=60 * 2**20),
        cost_estimate=pl.CostEstimate(
            flops=5 * group * group * width, bytes_accessed=24 * group * width, transcendentals=0
        ),
        name="attention_backward",
    )(place, first_tile, queries, keys, values, lse, out, grad_out, seg_col, seg_row)


def slot_table(expert_rows, order_rows, gate_rows, count_experts, capacity):
    chosen = expert_rows.T[None, :, :] == jnp.arange(count_experts, dtype=jnp.int32)[:, None, None]
    holds = jnp.any(chosen, axis=1)
    order = jnp.sum(jnp.where(chosen, order_rows.T[None], 0), axis=1)
    gate = jnp.sum(jnp.where(chosen, gate_rows.T[None], 0.0), axis=1)
    earlier = holds[:, None, :] & (order[:, None, :] < order[:, :, None])
    slot = jnp.sum(earlier.astype(jnp.int32), axis=2)
    return (jnp.where(holds & (slot < capacity), slot, -1), gate)


def barrier(*arrays):
    return lax.optimization_barrier(arrays)


class Line:
    def __init__(self):
        peers = lax.axis_size("ctx")
        self.chips = peers // 2
        self.chip = lax.axis_index("ctx") // 2
        self.peers = peers
        self.pair = [(i, i ^ 1) for i in range(peers)]
        steps = range(1, self.chips)
        every = [d for s in steps for d in (s, -s)]
        self.orders = [
            sorted((d for d in every if 0 <= z + d < self.chips), key=lambda d: (abs(d), -d))
            for z in range(self.chips)
        ]

    def step(self, turn, from_below, from_above):
        up = [(i, i + 2) for i in range(2 * (turn - 1), self.peers - 2)]
        down = [(i + 2, i) for i in range(self.peers - 2 * turn)]
        return (
            lax.ppermute(from_below, "ctx", up),
            lax.ppermute(from_above, "ctx", down),
        )

    def other(self, rows):
        return lax.ppermute(rows, "ctx", self.pair)

    def take(self, turn, arrived):
        offsets = [self.orders[z][turn - 1] for z in range(self.chips)]
        offset = jnp.array(offsets, jnp.int32)[self.chip]
        kinds = sorted(set(offsets))
        chosen = arrived[kinds[0]]
        for kind in kinds[1:]:
            chosen = jnp.where(offset == kind, arrived[kind], chosen)
        return chosen, self.chip + offset


def swap_partners(groups, shift):
    return [(i, i ^ shift) for i in range(groups)]


def swap_dp(part, shift):
    return lax.ppermute(part, "dp", swap_partners(lax.axis_size("dp"), shift))


def first_dp(part):
    return [swap_dp(part, 1), swap_dp(part, 2)]


def send_dp(part):
    return [swap_dp(part, shift) for shift in (1, 2, 3)]


def second_dp(pieces, axis):
    half = pieces[0].shape[axis] // 2
    return [
        swap_dp(lax.slice_in_dim(pieces[0], 0, half, axis=axis), 2),
        swap_dp(lax.slice_in_dim(pieces[1], half, 2 * half, axis=axis), 1),
    ]


def join_dp(part, pieces, axis):
    mine = lax.axis_index("dp")
    size = part.shape[axis]
    half = size // 2

    def both(shift):
        return [(mine ^ shift) * size, (mine ^ shift) * size + half]

    parts = [(part, both(0)), (pieces[0], both(1)), (pieces[1], both(2))]
    if len(pieces) == 3:
        parts.append((pieces[2], both(3)))
    else:
        parts += [(pieces[2], both(3)[:1]), (pieces[3], both(3)[1:])]
    return join(parts, axis, size * lax.axis_size("dp"), half)


def pick_dp(term, shift, axis):
    size = term.shape[axis] // lax.axis_size("dp")
    return lax.dynamic_slice_in_dim(term, (lax.axis_index("dp") ^ shift) * size, size, axis)


def scatter_one(term, shift, axis):
    return swap_dp(pick_dp(term, shift, axis), shift)


def total_dp(term, pieces, axis):
    groups = lax.axis_size("dp")
    size = term.shape[axis] // groups
    total = lax.dynamic_slice_in_dim(term, lax.axis_index("dp") * size, size, axis).astype(f32)
    for piece in pieces:
        total = total + piece.astype(f32)
    return total


def sum_small(array):
    peers = lax.axis_size("ctx")

    def swap(rows, shift):
        return lax.ppermute(rows, "ctx", [(i, i ^ shift) for i in range(peers)])

    array = array + swap(array, 1)
    return sum((swap(array, 2 * shift) for shift in range(1, peers // 2)), start=array)


def project_kernel(places, own, other, weight, gain, *rest):
    normed, raw, square = rest[-3:]

    def work(rows_ref):
        rows = rows_ref[...].astype(f32)
        hat = rows * lax.rsqrt(jnp.mean(rows * rows, axis=1, keepdims=True) + epsilon)
        low = (hat * gain[...]).astype(bf16)
        normed[...] = low
        product = jnp.dot(low, weight[...], preferred_element_type=f32)
        raw[...] = product
        third = product.shape[1] // 3
        for which in range(2):
            part = product[:, which * third : (which + 1) * third]
            square[which : which + 1, :] = jnp.sum((part * part).T, axis=0, keepdims=True)

    pl.when(pl.program_id(0) == 0)(lambda: work(own))
    pl.when(pl.program_id(0) == 1)(lambda: work(other))


def project(unit_index, own, other, weight, gain, peers, kept=()):
    rows, width = own.shape
    columns = weight.shape[1]

    def fixed(shape):
        return pl.BlockSpec(shape, lambda s, *_: (0,) * len(shape))

    return pl.pallas_call(
        project_kernel,
        grid_spec=pltpu.PrefetchScalarGridSpec(
            num_scalar_prefetch=1,
            grid=(2,),
            in_specs=[
                fixed((rows, width)),
                fixed((rows, width)),
                fixed((width, columns)),
                fixed((1, width)),
            ]
            + [pl.BlockSpec(memory_space=pl.ANY)] * len(kept),
            out_specs=[
                pl.BlockSpec((rows, width), lambda s, at: (at[s], 0)),
                pl.BlockSpec((rows, columns), lambda s, at: (at[s], 0)),
                pl.BlockSpec((None, 2, rows), lambda s, at: (at[s], 0, 0)),
            ],
        ),
        out_shape=[
            jax.ShapeDtypeStruct((peers * rows, width), bf16),
            jax.ShapeDtypeStruct((peers * rows, columns), f32),
            jax.ShapeDtypeStruct((peers, 2, rows), f32),
        ],
        input_output_aliases={5 + i: i for i in range(len(kept))},
        compiler_params=pltpu.CompilerParams(vmem_limit_bytes=56 * 2**20),
        name="project",
    )(unit_index, own, other, weight, gain, *kept)


def join_kernel(axis, blocks, block, at, *refs):
    out = refs[-1]
    turn = 0
    for ref, count in zip(refs[:-1], blocks):
        for index in range(count):
            here = (slice(None),) * axis + (slice(index * block, (index + 1) * block),)

            @pl.when(pl.program_id(0) == turn)
            def copy(ref=ref, here=here):
                out[...] = ref[here]

            turn += 1


def join(parts, axis, length, block):
    shape = list(parts[0][0].shape)
    shape[axis] = block
    blocks = [len(starts) for _, starts in parts]
    at = jnp.stack([start // block for _, starts in parts for start in starts]).astype(jnp.int32)
    rank = len(shape)

    def target(turn, at):
        return tuple(at[turn] if index == axis else 0 for index in range(rank))

    def fixed(part):
        return pl.BlockSpec(
            part.shape, lambda turn, at: (0,) * rank, pipeline_mode=pl.Buffered(1)
        )

    return pl.pallas_call(
        functools.partial(join_kernel, axis, blocks, block),
        grid_spec=pltpu.PrefetchScalarGridSpec(
            num_scalar_prefetch=1,
            grid=(sum(blocks),),
            in_specs=[fixed(part) for part, _ in parts],
            out_specs=pl.BlockSpec(tuple(shape), target),
        ),
        out_shape=jax.ShapeDtypeStruct(
            tuple(length if index == axis else size for index, size in enumerate(shape)),
            parts[0][0].dtype,
        ),
        compiler_params=pltpu.CompilerParams(vmem_limit_bytes=40 * 2**20),
        name="join",
    )(at, *[part for part, _ in parts])


def lay_kernel(at, own, other, *rest):
    out = rest[-1]

    def work(source):
        out[...] = source[...].astype(f32)

    pl.when(pl.program_id(0) == 0)(lambda: work(own))
    pl.when(pl.program_id(0) == 1)(lambda: work(other))


def lay(at, own, other, out_shape, block_columns, first, pieces, index, kept=()):
    block = (out_shape[0], block_columns)
    return pl.pallas_call(
        lay_kernel,
        grid_spec=pltpu.PrefetchScalarGridSpec(
            num_scalar_prefetch=1,
            grid=(2, pieces),
            in_specs=[pl.BlockSpec(block, lambda s, t, at: (0, first + t))] * 2
            + [pl.BlockSpec(memory_space=pl.ANY)] * len(kept),
            out_specs=pl.BlockSpec(block, lambda s, t, at: (0, index(at[s], t))),
        ),
        out_shape=jax.ShapeDtypeStruct(out_shape, f32),
        input_output_aliases={3: 0} if kept else {},
        name="lay",
    )(at, own, other, *kept)


def expert_kernel(
    unit, own, other, cots, slots, gates, columns, w_gate, w_up, w_down, *rest
):
    expert_in, grad_rows, hidden, grad_gate, grad_up, part, total, ready = rest[-8:]
    expert, piece = pl.program_id(0), pl.program_id(1)
    last_expert = expert == pl.num_programs(0) - 1
    last_piece = piece == pl.num_programs(1) - 1
    room, width = expert_in.shape[1:]
    rows = own.shape[0]
    core = unit[1]

    @pl.when(piece == 0)
    def bring():
        at = lax.broadcasted_iota(jnp.int32, (room, rows), 0)
        for s in range(2):
            found = at == slots[s, pl.ds(expert, 1), :]
            picks = jnp.where(found, 1.0, 0.0).astype(bf16)
            slot_gate = jnp.sum(
                jnp.where(found, gates[s, pl.ds(expert, 1), :], 0.0), axis=1, keepdims=True
            )
            grad_rows[s] = (
                jnp.dot(picks, cots[s], preferred_element_type=f32) * slot_gate
            ).astype(bf16)

            @pl.when(core == s)
            def from_own():
                expert_in[s] = jnp.dot(picks, own[...], preferred_element_type=f32).astype(bf16)

            @pl.when(core != s)
            def from_other():
                expert_in[s] = jnp.dot(picks, other[...], preferred_element_type=f32).astype(bf16)

    rows_in = expert_in[...].reshape(2 * room, width)
    gate_pre = jnp.dot(rows_in, w_gate[...], preferred_element_type=f32)
    up_pre = jnp.dot(rows_in, w_up[...], preferred_element_type=f32)
    grad_hidden = lax.dot_general(
        grad_rows[...].reshape(2 * room, width), w_down[...], NT, preferred_element_type=f32
    )
    sigmoid = 1.0 / (1.0 + jnp.exp(-gate_pre))
    silu = gate_pre * sigmoid
    hidden[...] = (silu * up_pre).astype(bf16).reshape(hidden.shape)
    gate_here = (grad_hidden * up_pre * sigmoid * (1.0 + gate_pre * (1.0 - sigmoid))).astype(bf16)
    up_here = (grad_hidden * silu).astype(bf16)
    grad_gate[...] = gate_here.reshape(grad_gate.shape)
    grad_up[...] = up_here.reshape(grad_up.shape)

    def back():
        return lax.dot_general(gate_here, w_gate[...], NT, preferred_element_type=f32) + lax.dot_general(
            up_here, w_up[...], NT, preferred_element_type=f32
        )

    @pl.when(piece == 0)
    def first():
        total[...] = back()

    @pl.when(piece != 0)
    def later():
        total[...] += back()

    @pl.when(last_piece)
    def keep():
        for s in range(2):
            ready[s, pl.ds(pl.multiple_of(expert * room, 16), room), :] = total[
                s * room : (s + 1) * room, :
            ].astype(bf16)

    @pl.when(last_piece & last_expert)
    def send():
        for s in range(2):
            at = lax.broadcasted_iota(jnp.int32, (rows, ready.shape[1]), 1)
            here = columns[s]
            found = at == here[:, 0:1]
            for e in range(1, here.shape[1]):
                found = found | (at == here[:, e : e + 1])
            part[s] = jnp.dot(
                jnp.where(found, 1.0, 0.0).astype(bf16), ready[s], preferred_element_type=f32
            ).astype(bf16)


def expert_unit(unit, own, other, cot_all, slots, gates, columns, w_gate, w_up, w_down, room, kept=(), piece=256):
    rows, width = own.shape
    experts, _, inner = w_gate.shape
    peers = cot_all.shape[0]
    wide_shape = (peers, experts, room, width)
    thin_shape = (peers, experts, room, inner)
    anywhere = pl.BlockSpec(memory_space=pl.ANY)
    once = pl.Buffered(1)

    def fixed(shape):
        return pl.BlockSpec(shape, lambda e, f, u: (0,) * len(shape), pipeline_mode=once)

    def chip(shape):
        return pl.BlockSpec((2, *shape), lambda e, f, u: (u[0], 0, 0), pipeline_mode=once)

    wide = pl.BlockSpec((2, None, room, width), lambda e, f, u: (u[0], e, 0, 0))
    thin = pl.BlockSpec((2, None, room, piece), lambda e, f, u: (u[0], e, 0, f))
    return pl.pallas_call(
        expert_kernel,
        grid_spec=pltpu.PrefetchScalarGridSpec(
            num_scalar_prefetch=1,
            grid=(experts, inner // piece),
            in_specs=[
                fixed((rows, width)), fixed((rows, width)), chip((rows, width)),
                chip((experts, rows)), chip((experts, rows)), chip((rows, experts)),
                pl.BlockSpec((None, width, piece), lambda e, f, u: (e, 0, f)),
                pl.BlockSpec((None, width, piece), lambda e, f, u: (e, 0, f)),
                pl.BlockSpec((None, piece, width), lambda e, f, u: (e, f, 0)),
            ] + [anywhere] * len(kept),
            out_specs=[wide, wide, thin, thin, thin,
                pl.BlockSpec((2, rows, width), lambda e, f, u: (u[0], 0, 0))],
            scratch_shapes=[
                pltpu.VMEM((2 * room, width), f32),
                pltpu.VMEM((2, experts * room, width), bf16),
            ],
        ),
        out_shape=[
            jax.ShapeDtypeStruct(shape, bf16)
            for shape in [wide_shape] * 2 + [thin_shape] * 3 + [cot_all.shape]
        ],
        input_output_aliases={10 + i: i for i in range(len(kept))},
        compiler_params=pltpu.CompilerParams(vmem_limit_bytes=60 * 2**20),
        name="expert_unit",
    )(unit, own, other, cot_all, slots, gates, columns, w_gate, w_up, w_down, *kept)


def out_kernel(hidden, w_down, slots, gates, columns, part, ready):
    expert = pl.program_id(1)
    room = hidden.shape[1]
    rows = slots.shape[2]
    at = lax.broadcasted_iota(jnp.int32, (room, rows), 0)
    product = jnp.dot(
        hidden[...].reshape(2 * room, hidden.shape[2]), w_down[...], preferred_element_type=f32
    )
    for s in range(2):
        found = at == slots[s, pl.ds(expert, 1), :]
        slot_gate = jnp.sum(jnp.where(found, gates[s, pl.ds(expert, 1), :], 0.0), axis=1, keepdims=True)
        ready[s, pl.ds(pl.multiple_of(expert * room, 16), room), :] = (
            product[s * room : (s + 1) * room] * slot_gate
        ).astype(bf16)

    @pl.when(expert == pl.num_programs(1) - 1)
    def send():
        for s in range(2):
            at = lax.broadcasted_iota(jnp.int32, (rows, ready.shape[1]), 1)
            here = columns[s]
            found = at == here[:, 0:1]
            for e in range(1, here.shape[1]):
                found = found | (at == here[:, e : e + 1])
            part[s] = jnp.dot(
                jnp.where(found, 1.0, 0.0).astype(bf16), ready[s], preferred_element_type=f32
            ).astype(bf16)


def expert_out(hidden, w_down, slots, gates, columns):
    peers, experts, room, inner = hidden.shape
    width = w_down.shape[2]
    rows = slots.shape[2]
    return pl.pallas_call(
        out_kernel,
        grid=(peers // 2, experts),
        in_specs=[
            pl.BlockSpec((2, None, room, inner), lambda c, e: (c, e, 0, 0)),
            pl.BlockSpec((None, inner, width), lambda c, e: (e, 0, 0)),
            pl.BlockSpec((2, experts, rows), lambda c, e: (c, 0, 0)),
            pl.BlockSpec((2, experts, rows), lambda c, e: (c, 0, 0)),
            pl.BlockSpec((2, rows, experts), lambda c, e: (c, 0, 0)),
        ],
        out_specs=pl.BlockSpec((2, rows, width), lambda c, e: (c, 0, 0)),
        out_shape=jax.ShapeDtypeStruct((peers, rows, width), bf16),
        scratch_shapes=[pltpu.VMEM((2, experts * room, width), bf16)],
        compiler_params=pltpu.CompilerParams(vmem_limit_bytes=60 * 2**20),
        name="expert_out",
    )(hidden, w_down, slots, gates, columns)


def on_device(
    tokens,
    cotangent,
    wqkv,
    wo,
    attn_gain,
    query_gain,
    key_gain,
    moe_gain,
    w_gate,
    w_up,
    w_down,
    expert_ids,
    gates,
    slot_order,
    block_assign,
    segment_ids,
):
    count_rows, width = tokens.shape
    head_dim = width // HEADS
    scale = head_dim ** (-0.5)
    peers = lax.axis_size("ctx")
    groups = lax.axis_size("dp")
    me = lax.axis_index("ctx")
    core = me % 2
    my_dp = lax.axis_index("dp")
    group_rows = count_rows * peers
    rep = max(1, peers // HEADS)
    own_heads = max(1, HEADS // peers)
    own_width = own_heads * head_dim
    first_head = (me // rep) * own_heads
    block_len = count_rows // BLK_DEV
    tile = 512
    line = Line()
    turns = range(1, line.chips)

    assign = block_assign[0]
    count_blocks = assign.shape[0]
    place = jnp.argmax(
        assign[None, :] == jnp.arange(count_blocks, dtype=jnp.int32)[:, None], axis=1
    ).astype(jnp.int32)
    cont = segment_ids[0]
    prompt_len = group_rows - cont.shape[0]
    prompt_tiles = prompt_len // tile
    seg_logical = jnp.concatenate([jnp.full((prompt_len,), -1, jnp.int32), cont])
    tiles = group_rows // tile
    tile_seg = seg_logical.reshape(tiles, tile)[:, 0]
    first_tile = jnp.where(
        tile_seg < 0,
        jnp.arange(tiles, dtype=jnp.int32),
        jnp.sum((seg_logical[None, :] < tile_seg[:, None]).astype(jnp.int32), axis=1) // tile,
    ).astype(jnp.int32)
    seg_col = seg_logical[:, None]
    seg_row = seg_logical.reshape(tiles, tile)

    local_experts = w_gate.shape[0]
    count_experts = local_experts * peers
    capacity = 9 * count_rows * TOP // (8 * count_experts)
    room = (capacity + 15) // 16 * 16
    slot, gate = slot_table(expert_ids, slot_order, gates, count_experts, capacity)
    table = jnp.stack(
        [
            slot.reshape(peers, local_experts, count_rows).astype(f32),
            gate.reshape(peers, local_experts, count_rows),
        ],
        axis=1,
    )

    inputs = tokens.astype(f32)
    below, above = line.step(1, tokens, tokens)
    other = line.other(tokens)
    w_part = jnp.concatenate(
        [
            lax.dynamic_slice_in_dim(wqkv, which * width + first_head * head_dim, own_width, 1)
            for which in range(3)
        ],
        axis=1,
    )
    w_pieces = send_dp(w_part)
    gain_part = jnp.stack([attn_gain, query_gain, key_gain, moe_gain])
    gain_all = jnp.zeros((4, width), bf16)
    for shift in range(groups):
        piece = swap_dp(gain_part, shift) if shift else gain_part
        gain_all = lax.dynamic_update_slice_in_dim(
            gain_all, piece, (my_dp ^ shift) * gain_part.shape[1], 1
        )
    gain_all = gain_all.astype(f32)
    below, above, other, gain_all, table, wo, w_gate, *w_pieces = barrier(
        below, above, other, gain_all, table, wo, w_gate, *w_pieces
    )
    full_gate = lax.all_gather(w_gate, "dp", axis=1, tiled=True)
    w_own = join_dp(w_part, w_pieces, 0)
    gain_attn, gain_moe = gain_all[0:1], gain_all[3:4]
    gain_own = lax.dynamic_slice_in_dim(gain_all, first_head * head_dim, own_width, 1)
    gain_q, gain_k = gain_own[1:2], gain_own[2:3]

    half_rows = wo.shape[0] // 2
    arrived = {-1: below, 1: above}
    own, chip = tokens, line.chip
    kept, travelled = (), ()
    for turn in turns:
        if turn + 1 < line.chips:
            below, above = line.step(turn + 1, below, above)
            arrived[-turn - 1], arrived[turn + 1] = below, above
        if turn + 1 == line.chips:
            cotangent_now, arrived[turn] = barrier(cotangent, arrived[turn])
        next_own, next_chip = line.take(turn, arrived)
        next_other = line.other(next_own)
        at = jnp.stack([2 * chip + core, 2 * chip + 1 - core]).astype(jnp.int32)
        kept = project(at, own, other, w_own, gain_attn, peers, kept)
        travel = list(travelled)
        if turn == 2:
            wo_half = lax.dynamic_slice_in_dim(wo, core * half_rows, half_rows, 0)
            travel = first_dp(wo_half)
        own, other, chip = next_own, next_other, next_chip
        square = kept[2]
        below, above, own, other, square, w_down, *travelled = barrier(
            below, above, own, other, square, w_down, *travel
        )
        kept = (kept[0], kept[1], square)
        if turn + 1 < line.chips:
            arrived[-turn - 1], arrived[turn + 1] = below, above
    cot_all = lax.all_gather(cotangent_now, "ctx", axis=0, tiled=True).reshape(
        peers, count_rows, width
    )
    down_pieces = first_dp(w_down)
    wo_pieces = [wo_half, *travelled[:2]]
    table = lax.all_to_all(table, "ctx", split_axis=0, concat_axis=0, tiled=True)
    at = jnp.stack([2 * chip + core, 2 * chip + 1 - core]).astype(jnp.int32)
    normed_all, raw, square = project(at, own, other, w_own, gain_attn, peers, kept)
    square = sum_small(square.transpose(1, 0, 2).reshape(2, group_rows)) * (1.0 / rep)
    inv_qk = lax.rsqrt(square / width + epsilon).T
    slot = table[:, 0].astype(jnp.int32)
    gate_rows = table[:, 1]
    offsets = (jnp.arange(local_experts, dtype=jnp.int32) * room)[None, :, None]
    columns = jnp.where(slot >= 0, slot + offsets, -1).transpose(0, 2, 1)

    inv_qk, w_up, slot, gate_rows, columns, full_gate, wo_half, *down_pieces = barrier(
        inv_qk, w_up, slot, gate_rows, columns, full_gate, wo_half, *down_pieces
    )
    wo_pieces.append(swap_dp(wo_half, 3))
    up_pieces = first_dp(w_up)
    attended, lse, queries, keys, values = attention_forward(
        raw,
        inv_qk,
        gain_q,
        gain_k,
        seg_col,
        seg_row,
        place,
        first_tile,
        tile,
        prompt_tiles,
        block_len,
        scale,
    )
    attended, wo_pieces[3], *up_pieces = barrier(attended, wo_pieces[3], *up_pieces)
    wo_mine = jnp.concatenate(wo_pieces, axis=0)
    wo_theirs = line.other(wo_mine)
    down_pieces = down_pieces + second_dp(down_pieces, 1)
    up_pieces = up_pieces + second_dp(up_pieces, 1)
    attn_low = lax.all_to_all(
        attended.reshape(peers, count_rows, own_width), "ctx", split_axis=0, concat_axis=0, tiled=True
    )[::rep]
    starts = [(my_dp ^ shift) * wo.shape[0] for shift in range(groups)]
    full_wo = join(
        [
            (wo_mine, [start + core * half_rows for start in starts]),
            (wo_theirs, [start + (1 - core) * half_rows for start in starts]),
        ],
        0,
        width,
        half_rows,
    )
    full_down = join_dp(w_down, down_pieces, 1)
    attn_low, full_wo, full_down = barrier(attn_low, full_wo, full_down)
    attn_low = attn_low.transpose(1, 0, 2).reshape(count_rows, width)
    state = inputs + jnp.dot(attn_low, full_wo, preferred_element_type=f32)
    inv_state = rms_scale(state)
    hat_state = state * inv_state
    normed_moe = (hat_state * gain_moe).astype(bf16)

    normed_moe, cot_all, *up_pieces = barrier(normed_moe, cot_all, *up_pieces)
    full_up = join_dp(w_up, up_pieces, 1)
    below, above = normed_moe, normed_moe
    own, chip = normed_moe, line.chip
    arrived = {}
    kept = ()
    for turn in range(line.chips):
        if turn + 1 < line.chips:
            below, above = line.step(turn + 1, below, above)
            arrived[-turn - 1], arrived[turn + 1] = below, above
        if turn > 0:
            own, chip = line.take(turn, arrived)
        other = line.other(own)
        kept = expert_unit(
            jnp.stack([chip, core]).astype(jnp.int32),
            own,
            other,
            cot_all,
            slot,
            gate_rows,
            columns,
            full_gate,
            full_up,
            full_down,
            room,
            kept,
        )
        if turn + 1 < line.chips:
            below, above, *kept = barrier(below, above, *kept)
            arrived[-turn - 1], arrived[turn + 1] = below, above
    expert_in, grad_rows, hidden, grad_gate_pre, grad_up_pre, part_moe = kept
    grad_normed_moe = lax.psum_scatter(
        part_moe.reshape(group_rows, width), "ctx", scatter_dimension=0, tiled=True
    )

    part_mixed = expert_out(hidden, full_down, slot, gate_rows, columns)
    grad_down = jnp.einsum("sncf,sncd->nfd", hidden, grad_rows, preferred_element_type=f32)
    grad_down = grad_down.astype(bf16)
    part_mixed, grad_down, expert_in = barrier(part_mixed, grad_down, expert_in)
    down_pieces = [scatter_one(grad_down, shift, 1) for shift in (1, 2, 3)]
    grad_gate = jnp.einsum("sncd,sncf->ndf", expert_in, grad_gate_pre, preferred_element_type=f32)
    grad_up = jnp.einsum("sncd,sncf->ndf", expert_in, grad_up_pre, preferred_element_type=f32)
    grad_gate, grad_up = grad_gate.astype(bf16), grad_up.astype(bf16)
    grad_normed_moe, part_mixed, grad_gate, grad_up, *down_pieces = barrier(
        grad_normed_moe, part_mixed, grad_gate, grad_up, *down_pieces
    )
    mixed = lax.psum_scatter(
        part_mixed.reshape(group_rows, width), "ctx", scatter_dimension=0, tiled=True
    )

    gate_pieces = [scatter_one(grad_gate, shift, 1) for shift in (1, 2)]
    grad_normed_moe = grad_normed_moe.astype(f32)
    moe_gain_term = jnp.sum(grad_normed_moe * hat_state, axis=0)
    grad_state = cotangent.astype(f32) + rms_back(grad_normed_moe * gain_moe, hat_state, inv_state)
    grad_branch = grad_state.astype(bf16)
    grad_attn = lax.dot_general(grad_branch, full_wo, NT, preferred_element_type=f32).astype(bf16)
    grad_attn = grad_attn.reshape(count_rows, peers // rep, own_width).transpose(1, 0, 2)
    grad_attn = jnp.repeat(grad_attn, rep, axis=0)
    grad_attended = lax.all_to_all(
        grad_attn, "ctx", split_axis=0, concat_axis=0, tiled=True
    ).reshape(group_rows, own_width)
    part_out = lax.dot_general(attn_low, grad_branch, TN, preferred_element_type=f32).astype(bf16)
    half = width // 2
    out_theirs = line.other(lax.dynamic_slice_in_dim(part_out, (1 - core) * half, half, 1))
    part_out = lax.dynamic_slice_in_dim(part_out, core * half, half, 1).astype(f32)
    part_out = (part_out + out_theirs.astype(f32)).astype(bf16)
    out_pieces = [scatter_one(part_out, shift, 0) for shift in (1, 2)]
    down_sum = total_dp(grad_down, down_pieces, 1)
    grad_attended, part_out, down_sum, grad_gate, *pieces = barrier(
        grad_attended, part_out, down_sum, grad_gate, *gate_pieces, *out_pieces
    )
    gate_pieces, out_pieces = pieces[:2], pieces[2:]
    out_pieces.append(scatter_one(part_out, 3, 0))
    gate_pieces.append(scatter_one(grad_gate, 3, 1))
    grad_q, grad_k, grad_v = attention_backward(
        queries,
        keys,
        values,
        lse,
        attended,
        grad_attended,
        seg_col,
        seg_row,
        place,
        first_tile,
        tile,
        prompt_tiles,
        block_len,
        scale,
    )
    grad_q, out_pieces[2], gate_pieces[2] = barrier(grad_q, out_pieces[2], gate_pieces[2])
    out_sum = total_dp(part_out, out_pieces, 0).astype(bf16)
    rows_dp = out_sum.shape[0]
    share = half // line.chips
    out_sum = out_sum.reshape(rows_dp, line.chips, share).transpose(1, 0, 2)
    hat_q = raw[:, :own_width] * inv_qk[:, 0:1]
    hat_k = raw[:, own_width : 2 * own_width] * inv_qk[:, 1:2]
    query_gain_term = jnp.sum(grad_q * hat_q, axis=0)
    key_gain_term = jnp.sum(grad_k * hat_k, axis=0)
    means = jnp.stack(
        [
            jnp.sum(grad_q * gain_q * hat_q, axis=1),
            jnp.sum(grad_k * gain_k * hat_k, axis=1),
        ]
    )
    means = (sum_small(means) * (1.0 / (rep * width))).T
    grad_raw_q = inv_qk[:, 0:1] * (grad_q * gain_q - hat_q * means[:, 0:1])
    grad_raw_k = inv_qk[:, 1:2] * (grad_k * gain_k - hat_k * means[:, 1:2])
    grad_qkv = jnp.concatenate([grad_raw_q.astype(bf16), grad_raw_k.astype(bf16), grad_v], axis=1)
    part_normed = lax.dot_general(grad_qkv, w_own, NT, preferred_element_type=f32) * (1.0 / rep)
    part_normed = part_normed.astype(bf16)
    part_normed, mixed, grad_up, out_sum = barrier(part_normed, mixed, grad_up, out_sum)
    grad_normed = lax.psum_scatter(part_normed, "ctx", scatter_dimension=0, tiled=True)

    out_sum = lax.all_to_all(
        out_sum,
        "ctx",
        split_axis=0,
        concat_axis=0,
        tiled=True,
        axis_index_groups=[[2 * z + c for z in range(peers // 2)] for c in range(2)],
    )
    part_qkv = lax.dot_general(normed_all, grad_qkv, TN, preferred_element_type=f32).astype(bf16)
    qkv_pieces = [scatter_one(part_qkv, shift, 0) for shift in (1, 2, 3)]
    own_terms = jnp.stack([query_gain_term, key_gain_term]) * (1.0 / rep)
    spread = lax.dynamic_update_slice_in_dim(
        jnp.zeros((2, width), f32), own_terms, first_head * head_dim, 1
    )
    attn_gain_term = (
        jnp.sum(part_normed.astype(f32) * normed_all.astype(f32), axis=0) / gain_attn[0]
    )
    gain_terms = jnp.concatenate([attn_gain_term[None], spread, moe_gain_term[None]], axis=0)
    gain_pieces = [scatter_one(gain_terms, shift, 1) for shift in (1, 2, 3)]
    output = (state + mixed.astype(f32)).astype(bf16)
    out_sum, gain_terms, grad_up, output, *pieces = barrier(
        out_sum, gain_terms, grad_up, output, *qkv_pieces, *gain_pieces
    )
    qkv_pieces, gain_pieces = pieces[:3], pieces[3:]
    gate_sum = total_dp(grad_gate, gate_pieces, 1)
    gain_terms = total_dp(gain_terms, gain_pieces, 1)
    qkv_sum = total_dp(part_qkv, qkv_pieces, 0).astype(bf16)
    out_sum = jnp.sum(out_sum.astype(f32), axis=0).astype(bf16)
    own, chip = jnp.concatenate([qkv_sum, out_sum], axis=1), line.chip
    gain_shape = gain_terms.shape
    row = own.shape[1]
    gain_terms = gain_terms.reshape(-1)
    gain_rows = (gain_terms.size // row + 16) // 16 * 16
    gain_size = gain_terms.size
    gain_terms = jnp.pad(gain_terms, (0, gain_rows * row - gain_size)).reshape(gain_rows, row)
    own = jnp.concatenate([own, gain_terms.astype(bf16)], axis=0)
    gain_terms = jnp.zeros((gain_rows, row), f32)
    below, above = own, own
    arrived = {}
    qkv_kept, out_kept = (), ()
    for turn in range(line.chips):
        if turn + 1 < line.chips:
            below, above = line.step(turn + 1, below, above)
        if turn > 0:
            own, chip = line.take(turn, arrived)
        other = line.other(own)
        gain_terms = gain_terms + own[rows_dp:].astype(f32) + other[rows_dp:].astype(f32)
        at = jnp.stack([2 * chip + core, 2 * chip + 1 - core]).astype(jnp.int32) // rep
        qkv_kept = [
            lay(
                at,
                own,
                other,
                (rows_dp, 3 * width),
                own_width,
                0,
                3,
                lambda p, t: t * (width // own_width) + p,
                qkv_kept,
            )
        ]
        at = jnp.stack([core * line.chips + chip, (1 - core) * line.chips + chip]).astype(jnp.int32)
        if share % HEAD_DIM == 0 and 3 * own_width % share == 0:
            out_kept = [
                lay(
                    at,
                    own,
                    other,
                    (rows_dp, width),
                    share,
                    3 * own_width // share,
                    1,
                    lambda p, t: p,
                    out_kept,
                )
            ]
        else:
            out_kept = list(out_kept) or [jnp.zeros((rows_dp, width), f32)]
            for which, part in enumerate((own, other)):
                out_kept[0] = lax.dynamic_update_slice_in_dim(
                    out_kept[0], part[:rows_dp, 3 * own_width :].astype(f32), at[which] * share, 1
                )
        if turn == 0:
            up_pieces = [scatter_one(grad_up, shift, 1) for shift in (1, 2)]
        if turn == 1:
            up_pieces.append(scatter_one(grad_up, 3, 1))
        if turn == 2:
            grad_up = total_dp(grad_up, up_pieces, 1)
            up_pieces = []
        if turn + 2 == line.chips:
            grad_normed = grad_normed.astype(f32)
            inv_in = rms_scale(inputs)
            hat_in = inputs * inv_in
            input_grad = grad_state + rms_back(grad_normed * gain_attn, hat_in, inv_in)
            up_pieces = [*up_pieces, input_grad.astype(bf16)]
        if turn + 1 < line.chips:
            below, above, qkv_kept[0], out_kept[0], grad_up, gate_sum, *up_pieces = barrier(
                below, above, qkv_kept[0], out_kept[0], grad_up, gate_sum, *up_pieces
            )
            arrived[-turn - 1], arrived[turn + 1] = below, above
    qkv_total, out_total = qkv_kept[0], out_kept[0]
    up_sum = grad_up
    input_grad = up_pieces[-1]
    gain_terms = gain_terms.reshape(-1)[:gain_size].reshape(gain_shape)
    return (
        output,
        input_grad,
        qkv_total,
        out_total,
        gain_terms[0],
        gain_terms[1],
        gain_terms[2],
        gain_terms[3],
        gate_sum,
        up_sum,
        down_sum,
    )


def solution(mesh):
    rows = P(("dp", "ctx"), None)
    expert = P("ctx", "dp", None)
    by_dp = P("dp", None)
    return jax.shard_map(
        on_device,
        mesh=mesh,
        in_specs=(
            rows,
            rows,
            by_dp,
            by_dp,
            P("dp"),
            P("dp"),
            P("dp"),
            P("dp"),
            expert,
            expert,
            expert,
            rows,
            rows,
            rows,
            by_dp,
            by_dp,
        ),
        out_specs=(
            rows,
            rows,
            by_dp,
            by_dp,
            P("dp"),
            P("dp"),
            P("dp"),
            P("dp"),
            expert,
            expert,
            expert,
        ),
        check_vma=False,
    )
```

```python
import functools

import jax
import jax.numpy as jnp
from jax import lax
from jax.experimental import pallas as pl
from jax.experimental.pallas import tpu as pltpu
from jax.sharding import PartitionSpec as P

HEADS = 16
TOP = 8
BLK_DEV = 2
LOG2E = 1.4426950408889634
HEAD_DIM = 128

epsilon = 1e-06
masked_value = -1e30
f32 = jnp.float32
bf16 = jnp.bfloat16
NT = (((1,), (1,)), ((), ()))
TN = (((0,), (0,)), ((), ()))


def rms_scale(values_in):
    return lax.rsqrt(jnp.mean(values_in * values_in, axis=-1, keepdims=True) + epsilon)


def rms_back(grad_hat, normed, scale_rows):
    return scale_rows * (grad_hat - normed * jnp.mean(grad_hat * normed, axis=-1, keepdims=True))


def tile_mask(seg_col, seg_row, key_first, query_first):
    rows, columns = seg_col.shape[0], seg_row.shape[1]
    key_pos = key_first + lax.broadcasted_iota(jnp.int32, (rows, columns), 0)
    query_pos = query_first + lax.broadcasted_iota(jnp.int32, (rows, columns), 1)
    return (seg_col == seg_row) & (key_pos <= query_pos)


def forward_kernel(
    tile,
    prompt_tiles,
    block_len,
    scale,
    place,
    first_tile,
    raw_q,
    raw_k,
    raw_v,
    inv,
    gain_q,
    gain_k,
    seg_col,
    seg_row,
    out,
    lse,
    queries,
    keys,
    values,
    values_t,
    out_logical,
):
    group, width = raw_q.shape
    tiles = group // tile
    blocks = group // block_len
    columns = [slice(first, first + HEAD_DIM) for first in range(0, width, HEAD_DIM)]

    def bring(block, carry):
        source = pl.ds(pl.multiple_of(place[block] * block_len, block_len), block_len)
        target = pl.ds(pl.multiple_of(block * block_len, block_len), block_len)
        scales = inv[source, :]
        queries[target, :] = (raw_q[source, :] * scales[:, 0:1] * gain_q[...]).astype(bf16)
        keys[target, :] = (raw_k[source, :] * scales[:, 1:2] * gain_k[...]).astype(bf16)
        values[target, :] = raw_v[source, :].astype(bf16)
        return carry

    lax.fori_loop(0, blocks, bring, 0)
    for index in range(tiles):
        values_t[:, index * tile : (index + 1) * tile] = values[
            index * tile : (index + 1) * tile, :
        ].T

    def query_tile(index, carry):
        first = pl.multiple_of(index * tile, tile)
        here = pl.ds(first, tile)
        seg_query = seg_row[pl.ds(index, 1), :]

        def step(is_masked, at, states):
            key_first = pl.multiple_of(at * tile, tile)
            there = pl.ds(key_first, tile)
            if is_masked:
                allowed = tile_mask(seg_col[there, :], seg_query, key_first, first)
            every = [
                lax.dot_general(
                    keys[there, head], queries[here, head], NT, preferred_element_type=f32
                )
                for head in columns
            ]
            after = []
            for scores, head, (largest, total, running) in zip(every, columns, states):
                scores = scores * (scale * LOG2E)
                if is_masked:
                    scores = jnp.where(allowed, scores, masked_value)
                new_largest = jnp.maximum(largest, jnp.max(scores, axis=0, keepdims=True))
                shrink = jnp.exp2(largest - new_largest)
                terms = jnp.exp2(scores - new_largest)
                total = total * shrink + jnp.sum(terms, axis=0, keepdims=True)
                running = running * shrink + jnp.dot(
                    values_t[head, there], terms.astype(bf16), preferred_element_type=f32
                )
                after.append((new_largest, total, running))
            return after

        states = [
            (
                jnp.full((1, tile), masked_value, f32),
                jnp.zeros((1, tile), f32),
                jnp.zeros((HEAD_DIM, tile), f32),
            )
            for _ in columns
        ]
        states = lax.fori_loop(
            0, jnp.minimum(index, prompt_tiles), functools.partial(step, False), states
        )
        states = lax.fori_loop(first_tile[index], index + 1, functools.partial(step, True), states)
        for which, (head, (largest, total, running)) in enumerate(zip(columns, states)):
            lse[which, pl.ds(index, 1), :] = largest + jnp.log2(total)
            out_logical[here, head] = (running / total).T.astype(bf16)
        return carry

    lax.fori_loop(0, tiles, query_tile, 0)

    def send(block, carry):
        target = pl.ds(pl.multiple_of(place[block] * block_len, block_len), block_len)
        source = pl.ds(pl.multiple_of(block * block_len, block_len), block_len)
        out[target, :] = out_logical[source, :]
        return carry

    lax.fori_loop(0, blocks, send, 0)


def backward_kernel(
    tile,
    prompt_tiles,
    block_len,
    scale,
    place,
    first_tile,
    queries,
    keys,
    values,
    lse,
    out,
    grad_out,
    seg_col,
    seg_row,
    grad_q,
    grad_k,
    grad_v,
    keys_t,
    grad_here,
    delta,
    total_q,
    total_k,
    total_v,
):
    group, width = queries.shape
    tiles = group // tile
    blocks = group // block_len
    columns = [slice(first, first + HEAD_DIM) for first in range(0, width, HEAD_DIM)]

    def bring(block, carry):
        source = pl.ds(pl.multiple_of(place[block] * block_len, block_len), block_len)
        target = pl.ds(pl.multiple_of(block * block_len, block_len), block_len)
        grad_here[target, :] = grad_out[source, :]
        total_q[target, :] = out[source, :].astype(f32) * grad_out[source, :].astype(f32)
        return carry

    lax.fori_loop(0, blocks, bring, 0)
    for index in range(tiles):
        rows = slice(index * tile, (index + 1) * tile)
        keys_t[:, rows] = keys[rows, :].T
        for which, head in enumerate(columns):
            delta[which, index : index + 1, :] = jnp.sum(
                total_q[rows, head].T, axis=0, keepdims=True
            )
    total_k[...] = jnp.zeros_like(total_k)
    total_v[...] = jnp.zeros_like(total_v)

    def query_tile(index, carry):
        first = pl.multiple_of(index * tile, tile)
        here = pl.ds(first, tile)
        seg_query = seg_row[pl.ds(index, 1), :]

        def step(is_masked, at, states):
            key_first = pl.multiple_of(at * tile, tile)
            there = pl.ds(key_first, tile)
            if is_masked:
                allowed = tile_mask(seg_col[there, :], seg_query, key_first, first)
            every = [
                (
                    lax.dot_general(
                        keys[there, head], queries[here, head], NT, preferred_element_type=f32
                    ),
                    lax.dot_general(
                        values[there, head], grad_here[here, head], NT, preferred_element_type=f32
                    ),
                )
                for head in columns
            ]
            after = []
            for which, (head, running) in enumerate(zip(columns, states)):
                scores, dprobs = every[which]
                probs = jnp.exp2(scores * (scale * LOG2E) - lse[which, pl.ds(index, 1), :])
                if is_masked:
                    probs = jnp.where(allowed, probs, 0.0)
                dscores = (probs * (dprobs - delta[which, pl.ds(index, 1), :])).astype(bf16)
                total_v[there, head] += jnp.dot(
                    probs.astype(bf16), grad_here[here, head], preferred_element_type=f32
                )
                total_k[there, head] += jnp.dot(
                    dscores, queries[here, head], preferred_element_type=f32
                )
                after.append(
                    running + jnp.dot(keys_t[head, there], dscores, preferred_element_type=f32)
                )
            return after

        states = [jnp.zeros((HEAD_DIM, tile), f32) for _ in columns]
        states = lax.fori_loop(
            0, jnp.minimum(index, prompt_tiles), functools.partial(step, False), states
        )
        states = lax.fori_loop(first_tile[index], index + 1, functools.partial(step, True), states)
        for head, running in zip(columns, states):
            total_q[here, head] = running.T
        return carry

    lax.fori_loop(0, tiles, query_tile, 0)

    def send(block, carry):
        target = pl.ds(pl.multiple_of(place[block] * block_len, block_len), block_len)
        source = pl.ds(pl.multiple_of(block * block_len, block_len), block_len)
        grad_q[target, :] = total_q[source, :] * scale
        grad_k[target, :] = total_k[source, :] * scale
        grad_v[target, :] = total_v[source, :].astype(bf16)
        return carry

    lax.fori_loop(0, blocks, send, 0)


def attention_forward(
    raw, inv, gain_q, gain_k, seg_col, seg_row, place, first_tile, tile, prompt_tiles, block_len, scale
):
    group, width = raw.shape[0], raw.shape[1] // 3
    heads = width // HEAD_DIM
    tiles = group // tile

    def part(which):
        return pl.BlockSpec((group, width), lambda i, *_: (0, which), pipeline_mode=pl.Buffered(1))

    def whole(shape):
        return pl.BlockSpec(
            shape, lambda i, *_: (0,) * len(shape), pipeline_mode=pl.Buffered(1)
        )

    head = whole((group, width))
    return pl.pallas_call(
        functools.partial(forward_kernel, tile, prompt_tiles, block_len, scale),
        grid_spec=pltpu.PrefetchScalarGridSpec(
            num_scalar_prefetch=2,
            grid=(1,),
            in_specs=[
                part(0),
                part(1),
                part(2),
                whole((group, 2)),
                whole((1, width)),
                whole((1, width)),
                whole((group, 1)),
                whole((tiles, tile)),
            ],
            out_specs=[head, whole((heads, tiles, tile)), head, head, head],
            scratch_shapes=[
                pltpu.VMEM((width, group), bf16),
                pltpu.VMEM((group, width), bf16),
            ],
        ),
        out_shape=[
            jax.ShapeDtypeStruct((group, width), bf16),
            jax.ShapeDtypeStruct((heads, tiles, tile), f32),
            jax.ShapeDtypeStruct((group, width), bf16),
            jax.ShapeDtypeStruct((group, width), bf16),
            jax.ShapeDtypeStruct((group, width), bf16),
        ],
        compiler_params=pltpu.CompilerParams(vmem_limit_bytes=60 * 2**20),
        cost_estimate=pl.CostEstimate(
            flops=4 * group * group * width, bytes_accessed=24 * group * width, transcendentals=0
        ),
        name="attention_forward",
    )(place, first_tile, raw, raw, raw, inv, gain_q, gain_k, seg_col, seg_row)


def attention_backward(
    queries, keys, values, lse, out, grad_out, seg_col, seg_row, place, first_tile, tile, prompt_tiles, block_len, scale
):
    group, width = queries.shape
    heads = width // HEAD_DIM
    tiles = group // tile

    def whole(shape):
        return pl.BlockSpec(
            shape, lambda i, *_: (0,) * len(shape), pipeline_mode=pl.Buffered(1)
        )

    head = whole((group, width))
    return pl.pallas_call(
        functools.partial(backward_kernel, tile, prompt_tiles, block_len, scale),
        grid_spec=pltpu.PrefetchScalarGridSpec(
            num_scalar_prefetch=2,
            grid=(1,),
            in_specs=[
                head,
                head,
                head,
                whole((heads, tiles, tile)),
                head,
                head,
                whole((group, 1)),
                whole((tiles, tile)),
            ],
            out_specs=[head, head, head],
            scratch_shapes=[
                pltpu.VMEM((width, group), bf16),
                pltpu.VMEM((group, width), bf16),
                pltpu.VMEM((heads, tiles, tile), f32),
                pltpu.VMEM((group, width), f32),
                pltpu.VMEM((group, width), f32),
                pltpu.VMEM((group, width), f32),
            ],
        ),
        out_shape=[
            jax.ShapeDtypeStruct((group, width), f32),
            jax.ShapeDtypeStruct((group, width), f32),
            jax.ShapeDtypeStruct((group, width), bf16),
        ],
        compiler_params=pltpu.CompilerParams(vmem_limit_bytes=60 * 2**20),
        cost_estimate=pl.CostEstimate(
            flops=5 * group * group * width, bytes_accessed=24 * group * width, transcendentals=0
        ),
        name="attention_backward",
    )(place, first_tile, queries, keys, values, lse, out, grad_out, seg_col, seg_row)


def slot_table(expert_rows, order_rows, gate_rows, count_experts, capacity):
    chosen = expert_rows.T[None, :, :] == jnp.arange(count_experts, dtype=jnp.int32)[:, None, None]
    holds = jnp.any(chosen, axis=1)
    order = jnp.sum(jnp.where(chosen, order_rows.T[None], 0), axis=1)
    gate = jnp.sum(jnp.where(chosen, gate_rows.T[None], 0.0), axis=1)
    earlier = holds[:, None, :] & (order[:, None, :] < order[:, :, None])
    slot = jnp.sum(earlier.astype(jnp.int32), axis=2)
    return (jnp.where(holds & (slot < capacity), slot, -1), gate)


def barrier(*arrays):
    return lax.optimization_barrier(arrays)


class Line:
    def __init__(self):
        peers = lax.axis_size("ctx")
        self.chips = peers // 2
        self.chip = lax.axis_index("ctx") // 2
        self.peers = peers
        self.pair = [(i, i ^ 1) for i in range(peers)]
        steps = range(1, self.chips)
        every = [d for s in steps for d in (s, -s)]
        self.orders = [
            sorted((d for d in every if 0 <= z + d < self.chips), key=lambda d: (abs(d), -d))
            for z in range(self.chips)
        ]

    def step(self, turn, from_below, from_above):
        up = [(i, i + 2) for i in range(2 * (turn - 1), self.peers - 2)]
        down = [(i + 2, i) for i in range(self.peers - 2 * turn)]
        return (
            lax.ppermute(from_below, "ctx", up),
            lax.ppermute(from_above, "ctx", down),
        )

    def other(self, rows):
        return lax.ppermute(rows, "ctx", self.pair)

    def take(self, turn, arrived):
        offsets = [self.orders[z][turn - 1] for z in range(self.chips)]
        offset = jnp.array(offsets, jnp.int32)[self.chip]
        kinds = sorted(set(offsets))
        chosen = arrived[kinds[0]]
        for kind in kinds[1:]:
            chosen = jnp.where(offset == kind, arrived[kind], chosen)
        return chosen, self.chip + offset


def swap_partners(groups, shift):
    return [(i, i ^ shift) for i in range(groups)]


def swap_dp(part, shift):
    return lax.ppermute(part, "dp", swap_partners(lax.axis_size("dp"), shift))


def first_dp(part):
    return [swap_dp(part, 1), swap_dp(part, 2)]


def send_dp(part):
    return [swap_dp(part, shift) for shift in (1, 2, 3)]


def second_dp(pieces, axis):
    half = pieces[0].shape[axis] // 2
    return [
        swap_dp(lax.slice_in_dim(pieces[0], 0, half, axis=axis), 2),
        swap_dp(lax.slice_in_dim(pieces[1], half, 2 * half, axis=axis), 1),
    ]


def join_dp(part, pieces, axis):
    mine = lax.axis_index("dp")
    size = part.shape[axis]
    half = size // 2

    def both(shift):
        return [(mine ^ shift) * size, (mine ^ shift) * size + half]

    parts = [(part, both(0)), (pieces[0], both(1)), (pieces[1], both(2))]
    if len(pieces) == 3:
        parts.append((pieces[2], both(3)))
    else:
        parts += [(pieces[2], both(3)[:1]), (pieces[3], both(3)[1:])]
    return join(parts, axis, size * lax.axis_size("dp"), half)


def pick_dp(term, shift, axis):
    size = term.shape[axis] // lax.axis_size("dp")
    return lax.dynamic_slice_in_dim(term, (lax.axis_index("dp") ^ shift) * size, size, axis)


def scatter_one(term, shift, axis):
    return swap_dp(pick_dp(term, shift, axis), shift)


def total_dp(term, pieces, axis):
    groups = lax.axis_size("dp")
    size = term.shape[axis] // groups
    total = lax.dynamic_slice_in_dim(term, lax.axis_index("dp") * size, size, axis).astype(f32)
    for piece in pieces:
        total = total + piece.astype(f32)
    return total


def sum_small(array):
    peers = lax.axis_size("ctx")

    def swap(rows, shift):
        return lax.ppermute(rows, "ctx", [(i, i ^ shift) for i in range(peers)])

    array = array + swap(array, 1)
    return sum((swap(array, 2 * shift) for shift in range(1, peers // 2)), start=array)


def project_kernel(places, own, other, weight, gain, *rest):
    normed, raw, square = rest[-3:]

    def work(rows_ref):
        rows = rows_ref[...].astype(f32)
        hat = rows * lax.rsqrt(jnp.mean(rows * rows, axis=1, keepdims=True) + epsilon)
        low = (hat * gain[...]).astype(bf16)
        normed[...] = low
        product = jnp.dot(low, weight[...], preferred_element_type=f32)
        raw[...] = product
        third = product.shape[1] // 3
        for which in range(2):
            part = product[:, which * third : (which + 1) * third]
            square[which : which + 1, :] = jnp.sum((part * part).T, axis=0, keepdims=True)

    pl.when(pl.program_id(0) == 0)(lambda: work(own))
    pl.when(pl.program_id(0) == 1)(lambda: work(other))


def project(unit_index, own, other, weight, gain, peers, kept=()):
    rows, width = own.shape
    columns = weight.shape[1]

    def fixed(shape):
        return pl.BlockSpec(shape, lambda s, *_: (0,) * len(shape))

    return pl.pallas_call(
        project_kernel,
        grid_spec=pltpu.PrefetchScalarGridSpec(
            num_scalar_prefetch=1,
            grid=(2,),
            in_specs=[
                fixed((rows, width)),
                fixed((rows, width)),
                fixed((width, columns)),
                fixed((1, width)),
            ]
            + [pl.BlockSpec(memory_space=pl.ANY)] * len(kept),
            out_specs=[
                pl.BlockSpec((rows, width), lambda s, at: (at[s], 0)),
                pl.BlockSpec((rows, columns), lambda s, at: (at[s], 0)),
                pl.BlockSpec((None, 2, rows), lambda s, at: (at[s], 0, 0)),
            ],
        ),
        out_shape=[
            jax.ShapeDtypeStruct((peers * rows, width), bf16),
            jax.ShapeDtypeStruct((peers * rows, columns), f32),
            jax.ShapeDtypeStruct((peers, 2, rows), f32),
        ],
        input_output_aliases={5 + i: i for i in range(len(kept))},
        compiler_params=pltpu.CompilerParams(vmem_limit_bytes=56 * 2**20),
        name="project",
    )(unit_index, own, other, weight, gain, *kept)


def join_kernel(axis, blocks, block, at, *refs):
    out = refs[-1]
    turn = 0
    for ref, count in zip(refs[:-1], blocks):
        for index in range(count):
            here = (slice(None),) * axis + (slice(index * block, (index + 1) * block),)

            @pl.when(pl.program_id(0) == turn)
            def copy(ref=ref, here=here):
                out[...] = ref[here]

            turn += 1


def join(parts, axis, length, block):
    shape = list(parts[0][0].shape)
    shape[axis] = block
    blocks = [len(starts) for _, starts in parts]
    at = jnp.stack([start // block for _, starts in parts for start in starts]).astype(jnp.int32)
    rank = len(shape)

    def target(turn, at):
        return tuple(at[turn] if index == axis else 0 for index in range(rank))

    def fixed(part):
        return pl.BlockSpec(
            part.shape, lambda turn, at: (0,) * rank, pipeline_mode=pl.Buffered(1)
        )

    return pl.pallas_call(
        functools.partial(join_kernel, axis, blocks, block),
        grid_spec=pltpu.PrefetchScalarGridSpec(
            num_scalar_prefetch=1,
            grid=(sum(blocks),),
            in_specs=[fixed(part) for part, _ in parts],
            out_specs=pl.BlockSpec(tuple(shape), target),
        ),
        out_shape=jax.ShapeDtypeStruct(
            tuple(length if index == axis else size for index, size in enumerate(shape)),
            parts[0][0].dtype,
        ),
        compiler_params=pltpu.CompilerParams(vmem_limit_bytes=40 * 2**20),
        name="join",
    )(at, *[part for part, _ in parts])


def lay_kernel(at, own, other, *rest):
    out = rest[-1]

    def work(source):
        out[...] = source[...].astype(f32)

    pl.when(pl.program_id(0) == 0)(lambda: work(own))
    pl.when(pl.program_id(0) == 1)(lambda: work(other))


def lay(at, own, other, out_shape, block_columns, first, pieces, index, kept=()):
    block = (out_shape[0], block_columns)
    return pl.pallas_call(
        lay_kernel,
        grid_spec=pltpu.PrefetchScalarGridSpec(
            num_scalar_prefetch=1,
            grid=(2, pieces),
            in_specs=[pl.BlockSpec(block, lambda s, t, at: (0, first + t))] * 2
            + [pl.BlockSpec(memory_space=pl.ANY)] * len(kept),
            out_specs=pl.BlockSpec(block, lambda s, t, at: (0, index(at[s], t))),
        ),
        out_shape=jax.ShapeDtypeStruct(out_shape, f32),
        input_output_aliases={3: 0} if kept else {},
        name="lay",
    )(at, own, other, *kept)


def expert_kernel(
    unit, own, other, cots, slots, gates, columns, w_gate, w_up, w_down, *rest
):
    expert_in, grad_rows, hidden, grad_gate, grad_up, part, total, ready = rest[-8:]
    expert, piece = pl.program_id(0), pl.program_id(1)
    last_expert = expert == pl.num_programs(0) - 1
    last_piece = piece == pl.num_programs(1) - 1
    room, width = expert_in.shape[1:]
    rows = own.shape[0]
    core = unit[1]

    @pl.when(piece == 0)
    def bring():
        at = lax.broadcasted_iota(jnp.int32, (room, rows), 0)
        for s in range(2):
            found = at == slots[s, pl.ds(expert, 1), :]
            picks = jnp.where(found, 1.0, 0.0).astype(bf16)
            slot_gate = jnp.sum(
                jnp.where(found, gates[s, pl.ds(expert, 1), :], 0.0), axis=1, keepdims=True
            )
            grad_rows[s] = (
                jnp.dot(picks, cots[s], preferred_element_type=f32) * slot_gate
            ).astype(bf16)

            @pl.when(core == s)
            def from_own():
                expert_in[s] = jnp.dot(picks, own[...], preferred_element_type=f32).astype(bf16)

            @pl.when(core != s)
            def from_other():
                expert_in[s] = jnp.dot(picks, other[...], preferred_element_type=f32).astype(bf16)

    rows_in = expert_in[...].reshape(2 * room, width)
    gate_pre = jnp.dot(rows_in, w_gate[...], preferred_element_type=f32)
    up_pre = jnp.dot(rows_in, w_up[...], preferred_element_type=f32)
    grad_hidden = lax.dot_general(
        grad_rows[...].reshape(2 * room, width), w_down[...], NT, preferred_element_type=f32
    )
    sigmoid = 1.0 / (1.0 + jnp.exp(-gate_pre))
    silu = gate_pre * sigmoid
    hidden[...] = (silu * up_pre).astype(bf16).reshape(hidden.shape)
    gate_here = (grad_hidden * up_pre * sigmoid * (1.0 + gate_pre * (1.0 - sigmoid))).astype(bf16)
    up_here = (grad_hidden * silu).astype(bf16)
    grad_gate[...] = gate_here.reshape(grad_gate.shape)
    grad_up[...] = up_here.reshape(grad_up.shape)

    def back():
        return lax.dot_general(gate_here, w_gate[...], NT, preferred_element_type=f32) + lax.dot_general(
            up_here, w_up[...], NT, preferred_element_type=f32
        )

    @pl.when(piece == 0)
    def first():
        total[...] = back()

    @pl.when(piece != 0)
    def later():
        total[...] += back()

    @pl.when(last_piece)
    def keep():
        for s in range(2):
            ready[s, pl.ds(pl.multiple_of(expert * room, 16), room), :] = total[
                s * room : (s + 1) * room, :
            ].astype(bf16)

    @pl.when(last_piece & last_expert)
    def send():
        for s in range(2):
            at = lax.broadcasted_iota(jnp.int32, (rows, ready.shape[1]), 1)
            here = columns[s]
            found = at == here[:, 0:1]
            for e in range(1, here.shape[1]):
                found = found | (at == here[:, e : e + 1])
            part[s] = jnp.dot(
                jnp.where(found, 1.0, 0.0).astype(bf16), ready[s], preferred_element_type=f32
            ).astype(bf16)


def expert_unit(unit, own, other, cot_all, slots, gates, columns, w_gate, w_up, w_down, room, kept=(), piece=256):
    rows, width = own.shape
    experts, _, inner = w_gate.shape
    peers = cot_all.shape[0]
    wide_shape = (peers, experts, room, width)
    thin_shape = (peers, experts, room, inner)
    anywhere = pl.BlockSpec(memory_space=pl.ANY)
    once = pl.Buffered(1)

    def fixed(shape):
        return pl.BlockSpec(shape, lambda e, f, u: (0,) * len(shape), pipeline_mode=once)

    def chip(shape):
        return pl.BlockSpec((2, *shape), lambda e, f, u: (u[0], 0, 0), pipeline_mode=once)

    wide = pl.BlockSpec((2, None, room, width), lambda e, f, u: (u[0], e, 0, 0))
    thin = pl.BlockSpec((2, None, room, piece), lambda e, f, u: (u[0], e, 0, f))
    return pl.pallas_call(
        expert_kernel,
        grid_spec=pltpu.PrefetchScalarGridSpec(
            num_scalar_prefetch=1,
            grid=(experts, inner // piece),
            in_specs=[
                fixed((rows, width)), fixed((rows, width)), chip((rows, width)),
                chip((experts, rows)), chip((experts, rows)), chip((rows, experts)),
                pl.BlockSpec((None, width, piece), lambda e, f, u: (e, 0, f)),
                pl.BlockSpec((None, width, piece), lambda e, f, u: (e, 0, f)),
                pl.BlockSpec((None, piece, width), lambda e, f, u: (e, f, 0)),
            ] + [anywhere] * len(kept),
            out_specs=[wide, wide, thin, thin, thin,
                pl.BlockSpec((2, rows, width), lambda e, f, u: (u[0], 0, 0))],
            scratch_shapes=[
                pltpu.VMEM((2 * room, width), f32),
                pltpu.VMEM((2, experts * room, width), bf16),
            ],
        ),
        out_shape=[
            jax.ShapeDtypeStruct(shape, bf16)
            for shape in [wide_shape] * 2 + [thin_shape] * 3 + [cot_all.shape]
        ],
        input_output_aliases={10 + i: i for i in range(len(kept))},
        compiler_params=pltpu.CompilerParams(vmem_limit_bytes=60 * 2**20),
        name="expert_unit",
    )(unit, own, other, cot_all, slots, gates, columns, w_gate, w_up, w_down, *kept)


def out_kernel(hidden, w_down, slots, gates, columns, part, ready):
    expert = pl.program_id(1)
    room = hidden.shape[1]
    rows = slots.shape[2]
    at = lax.broadcasted_iota(jnp.int32, (room, rows), 0)
    product = jnp.dot(
        hidden[...].reshape(2 * room, hidden.shape[2]), w_down[...], preferred_element_type=f32
    )
    for s in range(2):
        found = at == slots[s, pl.ds(expert, 1), :]
        slot_gate = jnp.sum(jnp.where(found, gates[s, pl.ds(expert, 1), :], 0.0), axis=1, keepdims=True)
        ready[s, pl.ds(pl.multiple_of(expert * room, 16), room), :] = (
            product[s * room : (s + 1) * room] * slot_gate
        ).astype(bf16)

    @pl.when(expert == pl.num_programs(1) - 1)
    def send():
        for s in range(2):
            at = lax.broadcasted_iota(jnp.int32, (rows, ready.shape[1]), 1)
            here = columns[s]
            found = at == here[:, 0:1]
            for e in range(1, here.shape[1]):
                found = found | (at == here[:, e : e + 1])
            part[s] = jnp.dot(
                jnp.where(found, 1.0, 0.0).astype(bf16), ready[s], preferred_element_type=f32
            ).astype(bf16)


def expert_out(hidden, w_down, slots, gates, columns):
    peers, experts, room, inner = hidden.shape
    width = w_down.shape[2]
    rows = slots.shape[2]
    return pl.pallas_call(
        out_kernel,
        grid=(peers // 2, experts),
        in_specs=[
            pl.BlockSpec((2, None, room, inner), lambda c, e: (c, e, 0, 0)),
            pl.BlockSpec((None, inner, width), lambda c, e: (e, 0, 0)),
            pl.BlockSpec((2, experts, rows), lambda c, e: (c, 0, 0)),
            pl.BlockSpec((2, experts, rows), lambda c, e: (c, 0, 0)),
            pl.BlockSpec((2, rows, experts), lambda c, e: (c, 0, 0)),
        ],
        out_specs=pl.BlockSpec((2, rows, width), lambda c, e: (c, 0, 0)),
        out_shape=jax.ShapeDtypeStruct((peers, rows, width), bf16),
        scratch_shapes=[pltpu.VMEM((2, experts * room, width), bf16)],
        compiler_params=pltpu.CompilerParams(vmem_limit_bytes=60 * 2**20),
        name="expert_out",
    )(hidden, w_down, slots, gates, columns)


def on_device(
    tokens,
    cotangent,
    wqkv,
    wo,
    attn_gain,
    query_gain,
    key_gain,
    moe_gain,
    w_gate,
    w_up,
    w_down,
    expert_ids,
    gates,
    slot_order,
    block_assign,
    segment_ids,
):
    count_rows, width = tokens.shape
    head_dim = width // HEADS
    scale = head_dim ** (-0.5)
    peers = lax.axis_size("ctx")
    groups = lax.axis_size("dp")
    me = lax.axis_index("ctx")
    core = me % 2
    my_dp = lax.axis_index("dp")
    group_rows = count_rows * peers
    rep = max(1, peers // HEADS)
    own_heads = max(1, HEADS // peers)
    own_width = own_heads * head_dim
    first_head = (me // rep) * own_heads
    block_len = count_rows // BLK_DEV
    tile = 512
    line = Line()
    turns = range(1, line.chips)

    assign = block_assign[0]
    count_blocks = assign.shape[0]
    place = jnp.argmax(
        assign[None, :] == jnp.arange(count_blocks, dtype=jnp.int32)[:, None], axis=1
    ).astype(jnp.int32)
    cont = segment_ids[0]
    prompt_len = group_rows - cont.shape[0]
    prompt_tiles = prompt_len // tile
    seg_logical = jnp.concatenate([jnp.full((prompt_len,), -1, jnp.int32), cont])
    tiles = group_rows // tile
    tile_seg = seg_logical.reshape(tiles, tile)[:, 0]
    first_tile = jnp.where(
        tile_seg < 0,
        jnp.arange(tiles, dtype=jnp.int32),
        jnp.sum((seg_logical[None, :] < tile_seg[:, None]).astype(jnp.int32), axis=1) // tile,
    ).astype(jnp.int32)
    seg_col = seg_logical[:, None]
    seg_row = seg_logical.reshape(tiles, tile)

    local_experts = w_gate.shape[0]
    count_experts = local_experts * peers
    capacity = 9 * count_rows * TOP // (8 * count_experts)
    room = (capacity + 15) // 16 * 16
    slot, gate = slot_table(expert_ids, slot_order, gates, count_experts, capacity)
    table = jnp.stack(
        [
            slot.reshape(peers, local_experts, count_rows).astype(f32),
            gate.reshape(peers, local_experts, count_rows),
        ],
        axis=1,
    )

    inputs = tokens.astype(f32)
    below, above = line.step(1, tokens, tokens)
    other = line.other(tokens)
    w_part = jnp.concatenate(
        [
            lax.dynamic_slice_in_dim(wqkv, which * width + first_head * head_dim, own_width, 1)
            for which in range(3)
        ],
        axis=1,
    )
    w_pieces = send_dp(w_part)
    gain_part = jnp.stack([attn_gain, query_gain, key_gain, moe_gain])
    gain_all = jnp.zeros((4, width), bf16)
    for shift in range(groups):
        piece = swap_dp(gain_part, shift) if shift else gain_part
        gain_all = lax.dynamic_update_slice_in_dim(
            gain_all, piece, (my_dp ^ shift) * gain_part.shape[1], 1
        )
    gain_all = gain_all.astype(f32)
    below, above, other, gain_all, table, wo, w_gate, *w_pieces = barrier(
        below, above, other, gain_all, table, wo, w_gate, *w_pieces
    )
    full_gate = lax.all_gather(w_gate, "dp", axis=1, tiled=True)
    w_own = join_dp(w_part, w_pieces, 0)
    gain_attn, gain_moe = gain_all[0:1], gain_all[3:4]
    gain_own = lax.dynamic_slice_in_dim(gain_all, first_head * head_dim, own_width, 1)
    gain_q, gain_k = gain_own[1:2], gain_own[2:3]

    half_rows = wo.shape[0] // 2
    arrived = {-1: below, 1: above}
    own, chip = tokens, line.chip
    kept, travelled = (), ()
    for turn in turns:
        if turn + 1 < line.chips:
            below, above = line.step(turn + 1, below, above)
            arrived[-turn - 1], arrived[turn + 1] = below, above
        if turn + 1 == line.chips:
            cotangent_now, arrived[turn] = barrier(cotangent, arrived[turn])
        next_own, next_chip = line.take(turn, arrived)
        next_other = line.other(next_own)
        at = jnp.stack([2 * chip + core, 2 * chip + 1 - core]).astype(jnp.int32)
        kept = project(at, own, other, w_own, gain_attn, peers, kept)
        travel = list(travelled)
        if turn == 2:
            wo_half = lax.dynamic_slice_in_dim(wo, core * half_rows, half_rows, 0)
            travel = first_dp(wo_half)
        own, other, chip = next_own, next_other, next_chip
        square = kept[2]
        below, above, own, other, square, w_down, *travelled = barrier(
            below, above, own, other, square, w_down, *travel
        )
        kept = (kept[0], kept[1], square)
        if turn + 1 < line.chips:
            arrived[-turn - 1], arrived[turn + 1] = below, above
    cot_all = lax.all_gather(cotangent_now, "ctx", axis=0, tiled=True).reshape(
        peers, count_rows, width
    )
    down_pieces = first_dp(w_down)
    wo_pieces = [wo_half, *travelled[:2]]
    table = lax.all_to_all(table, "ctx", split_axis=0, concat_axis=0, tiled=True)
    at = jnp.stack([2 * chip + core, 2 * chip + 1 - core]).astype(jnp.int32)
    normed_all, raw, square = project(at, own, other, w_own, gain_attn, peers, kept)
    square = sum_small(square.transpose(1, 0, 2).reshape(2, group_rows)) * (1.0 / rep)
    inv_qk = lax.rsqrt(square / width + epsilon).T
    slot = table[:, 0].astype(jnp.int32)
    gate_rows = table[:, 1]
    offsets = (jnp.arange(local_experts, dtype=jnp.int32) * room)[None, :, None]
    columns = jnp.where(slot >= 0, slot + offsets, -1).transpose(0, 2, 1)

    inv_qk, w_up, slot, gate_rows, columns, full_gate, wo_half, *down_pieces = barrier(
        inv_qk, w_up, slot, gate_rows, columns, full_gate, wo_half, *down_pieces
    )
    wo_pieces.append(swap_dp(wo_half, 3))
    up_pieces = first_dp(w_up)
    attended, lse, queries, keys, values = attention_forward(
        raw,
        inv_qk,
        gain_q,
        gain_k,
        seg_col,
        seg_row,
        place,
        first_tile,
        tile,
        prompt_tiles,
        block_len,
        scale,
    )
    attended, wo_pieces[3], *up_pieces = barrier(attended, wo_pieces[3], *up_pieces)
    wo_mine = jnp.concatenate(wo_pieces, axis=0)
    wo_theirs = line.other(wo_mine)
    down_pieces = down_pieces + second_dp(down_pieces, 1)
    up_pieces = up_pieces + second_dp(up_pieces, 1)
    attn_low = lax.all_to_all(
        attended.reshape(peers, count_rows, own_width), "ctx", split_axis=0, concat_axis=0, tiled=True
    )[::rep]
    starts = [(my_dp ^ shift) * wo.shape[0] for shift in range(groups)]
    full_wo = join(
        [
            (wo_mine, [start + core * half_rows for start in starts]),
            (wo_theirs, [start + (1 - core) * half_rows for start in starts]),
        ],
        0,
        width,
        half_rows,
    )
    full_down = join_dp(w_down, down_pieces, 1)
    attn_low, full_wo, full_down = barrier(attn_low, full_wo, full_down)
    attn_low = attn_low.transpose(1, 0, 2).reshape(count_rows, width)
    state = inputs + jnp.dot(attn_low, full_wo, preferred_element_type=f32)
    inv_state = rms_scale(state)
    hat_state = state * inv_state
    normed_moe = (hat_state * gain_moe).astype(bf16)

    normed_moe, cot_all, *up_pieces = barrier(normed_moe, cot_all, *up_pieces)
    full_up = join_dp(w_up, up_pieces, 1)
    below, above = normed_moe, normed_moe
    own, chip = normed_moe, line.chip
    arrived = {}
    kept = ()
    for turn in range(line.chips):
        if turn + 1 < line.chips:
            below, above = line.step(turn + 1, below, above)
            arrived[-turn - 1], arrived[turn + 1] = below, above
        if turn > 0:
            own, chip = line.take(turn, arrived)
        other = line.other(own)
        kept = expert_unit(
            jnp.stack([chip, core]).astype(jnp.int32),
            own,
            other,
            cot_all,
            slot,
            gate_rows,
            columns,
            full_gate,
            full_up,
            full_down,
            room,
            kept,
        )
        if turn + 1 < line.chips:
            below, above, *kept = barrier(below, above, *kept)
            arrived[-turn - 1], arrived[turn + 1] = below, above
    expert_in, grad_rows, hidden, grad_gate_pre, grad_up_pre, part_moe = kept
    grad_normed_moe = lax.psum_scatter(
        part_moe.reshape(group_rows, width), "ctx", scatter_dimension=0, tiled=True
    )

    part_mixed = expert_out(hidden, full_down, slot, gate_rows, columns)
    grad_down = jnp.einsum("sncf,sncd->nfd", hidden, grad_rows, preferred_element_type=f32)
    grad_down = grad_down.astype(bf16)
    part_mixed, grad_down, expert_in = barrier(part_mixed, grad_down, expert_in)
    down_pieces = [scatter_one(grad_down, shift, 1) for shift in (1, 2, 3)]
    grad_gate = jnp.einsum("sncd,sncf->ndf", expert_in, grad_gate_pre, preferred_element_type=f32)
    grad_up = jnp.einsum("sncd,sncf->ndf", expert_in, grad_up_pre, preferred_element_type=f32)
    grad_gate, grad_up = grad_gate.astype(bf16), grad_up.astype(bf16)
    grad_normed_moe, part_mixed, grad_gate, grad_up, *down_pieces = barrier(
        grad_normed_moe, part_mixed, grad_gate, grad_up, *down_pieces
    )
    mixed = lax.psum_scatter(
        part_mixed.reshape(group_rows, width), "ctx", scatter_dimension=0, tiled=True
    )

    gate_pieces = [scatter_one(grad_gate, shift, 1) for shift in (1, 2)]
    grad_normed_moe = grad_normed_moe.astype(f32)
    moe_gain_term = jnp.sum(grad_normed_moe * hat_state, axis=0)
    grad_state = cotangent.astype(f32) + rms_back(grad_normed_moe * gain_moe, hat_state, inv_state)
    grad_branch = grad_state.astype(bf16)
    grad_attn = lax.dot_general(grad_branch, full_wo, NT, preferred_element_type=f32).astype(bf16)
    grad_attn = grad_attn.reshape(count_rows, peers // rep, own_width).transpose(1, 0, 2)
    grad_attn = jnp.repeat(grad_attn, rep, axis=0)
    grad_attended = lax.all_to_all(
        grad_attn, "ctx", split_axis=0, concat_axis=0, tiled=True
    ).reshape(group_rows, own_width)
    part_out = lax.dot_general(attn_low, grad_branch, TN, preferred_element_type=f32).astype(bf16)
    half = width // 2
    out_theirs = line.other(lax.dynamic_slice_in_dim(part_out, (1 - core) * half, half, 1))
    part_out = lax.dynamic_slice_in_dim(part_out, core * half, half, 1).astype(f32)
    part_out = (part_out + out_theirs.astype(f32)).astype(bf16)
    out_pieces = [scatter_one(part_out, shift, 0) for shift in (1, 2)]
    down_sum = total_dp(grad_down, down_pieces, 1)
    grad_attended, part_out, down_sum, grad_gate, *pieces = barrier(
        grad_attended, part_out, down_sum, grad_gate, *gate_pieces, *out_pieces
    )
    gate_pieces, out_pieces = pieces[:2], pieces[2:]
    out_pieces.append(scatter_one(part_out, 3, 0))
    gate_pieces.append(scatter_one(grad_gate, 3, 1))
    grad_q, grad_k, grad_v = attention_backward(
        queries,
        keys,
        values,
        lse,
        attended,
        grad_attended,
        seg_col,
        seg_row,
        place,
        first_tile,
        tile,
        prompt_tiles,
        block_len,
        scale,
    )
    grad_q, out_pieces[2], gate_pieces[2] = barrier(grad_q, out_pieces[2], gate_pieces[2])
    out_sum = total_dp(part_out, out_pieces, 0).astype(bf16)
    rows_dp = out_sum.shape[0]
    share = half // line.chips
    out_sum = out_sum.reshape(rows_dp, line.chips, share).transpose(1, 0, 2)
    hat_q = raw[:, :own_width] * inv_qk[:, 0:1]
    hat_k = raw[:, own_width : 2 * own_width] * inv_qk[:, 1:2]
    query_gain_term = jnp.sum(grad_q * hat_q, axis=0)
    key_gain_term = jnp.sum(grad_k * hat_k, axis=0)
    means = jnp.stack(
        [
            jnp.sum(grad_q * gain_q * hat_q, axis=1),
            jnp.sum(grad_k * gain_k * hat_k, axis=1),
        ]
    )
    means = (sum_small(means) * (1.0 / (rep * width))).T
    grad_raw_q = inv_qk[:, 0:1] * (grad_q * gain_q - hat_q * means[:, 0:1])
    grad_raw_k = inv_qk[:, 1:2] * (grad_k * gain_k - hat_k * means[:, 1:2])
    grad_qkv = jnp.concatenate([grad_raw_q.astype(bf16), grad_raw_k.astype(bf16), grad_v], axis=1)
    part_normed = lax.dot_general(grad_qkv, w_own, NT, preferred_element_type=f32) * (1.0 / rep)
    part_normed = part_normed.astype(bf16)
    part_normed, mixed, grad_up, out_sum = barrier(part_normed, mixed, grad_up, out_sum)
    grad_normed = lax.psum_scatter(part_normed, "ctx", scatter_dimension=0, tiled=True)

    out_sum = lax.all_to_all(
        out_sum,
        "ctx",
        split_axis=0,
        concat_axis=0,
        tiled=True,
        axis_index_groups=[[2 * z + c for z in range(peers // 2)] for c in range(2)],
    )
    part_qkv = lax.dot_general(normed_all, grad_qkv, TN, preferred_element_type=f32).astype(bf16)
    qkv_pieces = [scatter_one(part_qkv, shift, 0) for shift in (1, 2, 3)]
    own_terms = jnp.stack([query_gain_term, key_gain_term]) * (1.0 / rep)
    spread = lax.dynamic_update_slice_in_dim(
        jnp.zeros((2, width), f32), own_terms, first_head * head_dim, 1
    )
    attn_gain_term = (
        jnp.sum(part_normed.astype(f32) * normed_all.astype(f32), axis=0) / gain_attn[0]
    )
    gain_terms = jnp.concatenate([attn_gain_term[None], spread, moe_gain_term[None]], axis=0)
    gain_terms, out_sum = barrier(gain_terms, out_sum)
    gain_pieces = [scatter_one(gain_terms, shift, 1) for shift in (1, 2, 3)]
    output = (state + mixed.astype(f32)).astype(bf16)
    out_sum, gain_terms, grad_up, output, *pieces = barrier(
        out_sum, gain_terms, grad_up, output, *qkv_pieces, *gain_pieces
    )
    qkv_pieces, gain_pieces = pieces[:3], pieces[3:]
    gate_sum = total_dp(grad_gate, gate_pieces, 1)
    gain_terms = total_dp(gain_terms, gain_pieces, 1)
    qkv_sum = total_dp(part_qkv, qkv_pieces, 0).astype(bf16)
    out_sum = jnp.sum(out_sum.astype(f32), axis=0).astype(bf16)
    own, chip = jnp.concatenate([qkv_sum, out_sum], axis=1), line.chip
    gain_shape = gain_terms.shape
    row = own.shape[1]
    gain_terms = gain_terms.reshape(-1)
    gain_rows = (gain_terms.size // row + 16) // 16 * 16
    gain_size = gain_terms.size
    gain_terms = jnp.pad(gain_terms, (0, gain_rows * row - gain_size)).reshape(gain_rows, row)
    own = jnp.concatenate([own, gain_terms.astype(bf16)], axis=0)
    gain_terms = jnp.zeros((gain_rows, row), f32)
    below, above = own, own
    arrived = {}
    qkv_kept, out_kept = (), ()
    for turn in range(line.chips):
        if turn + 1 < line.chips:
            below, above = line.step(turn + 1, below, above)
        if turn > 0:
            own, chip = line.take(turn, arrived)
        other = line.other(own)
        gain_terms = gain_terms + own[rows_dp:].astype(f32) + other[rows_dp:].astype(f32)
        at = jnp.stack([2 * chip + core, 2 * chip + 1 - core]).astype(jnp.int32) // rep
        qkv_kept = [
            lay(
                at,
                own,
                other,
                (rows_dp, 3 * width),
                own_width,
                0,
                3,
                lambda p, t: t * (width // own_width) + p,
                qkv_kept,
            )
        ]
        at = jnp.stack([core * line.chips + chip, (1 - core) * line.chips + chip]).astype(jnp.int32)
        if share % HEAD_DIM == 0 and 3 * own_width % share == 0:
            out_kept = [
                lay(
                    at,
                    own,
                    other,
                    (rows_dp, width),
                    share,
                    3 * own_width // share,
                    1,
                    lambda p, t: p,
                    out_kept,
                )
            ]
        else:
            out_kept = list(out_kept) or [jnp.zeros((rows_dp, width), f32)]
            for which, part in enumerate((own, other)):
                out_kept[0] = lax.dynamic_update_slice_in_dim(
                    out_kept[0], part[:rows_dp, 3 * own_width :].astype(f32), at[which] * share, 1
                )
        if turn == 0:
            up_pieces = [scatter_one(grad_up, shift, 1) for shift in (1, 2)]
        if turn == 1:
            up_pieces.append(scatter_one(grad_up, 3, 1))
        if turn == 2:
            grad_up = total_dp(grad_up, up_pieces, 1)
            up_pieces = []
        if turn + 2 == line.chips:
            grad_normed = grad_normed.astype(f32)
            inv_in = rms_scale(inputs)
            hat_in = inputs * inv_in
            input_grad = grad_state + rms_back(grad_normed * gain_attn, hat_in, inv_in)
            up_pieces = [*up_pieces, input_grad.astype(bf16)]
        if turn + 1 < line.chips:
            below, above, qkv_kept[0], out_kept[0], grad_up, gate_sum, *up_pieces = barrier(
                below, above, qkv_kept[0], out_kept[0], grad_up, gate_sum, *up_pieces
            )
            arrived[-turn - 1], arrived[turn + 1] = below, above
    qkv_total, out_total = qkv_kept[0], out_kept[0]
    up_sum = grad_up
    input_grad = up_pieces[-1]
    gain_terms = gain_terms.reshape(-1)[:gain_size].reshape(gain_shape)
    return (
        output,
        input_grad,
        qkv_total,
        out_total,
        gain_terms[0],
        gain_terms[1],
        gain_terms[2],
        gain_terms[3],
        gate_sum,
        up_sum,
        down_sum,
    )


def solution(mesh):
    rows = P(("dp", "ctx"), None)
    expert = P("ctx", "dp", None)
    by_dp = P("dp", None)
    return jax.shard_map(
        on_device,
        mesh=mesh,
        in_specs=(
            rows,
            rows,
            by_dp,
            by_dp,
            P("dp"),
            P("dp"),
            P("dp"),
            P("dp"),
            expert,
            expert,
            expert,
            rows,
            rows,
            rows,
            by_dp,
            by_dp,
        ),
        out_specs=(
            rows,
            rows,
            by_dp,
            by_dp,
            P("dp"),
            P("dp"),
            P("dp"),
            P("dp"),
            expert,
            expert,
            expert,
        ),
        check_vma=False,
    )
```
